32 devices in a mesh: dp: 16 (over z, x, core), tensor: 2 (over y).
Axes of the slice: x: 2, y: 2, z: 4, core: 2. Of those that a mesh axis runs over, the one named last changes fastest.
Arguments:
- tokens: bfloat16 [32, 1024, 768], P('dp', 'tensor'), may hold values from -6 to 6
- lengths: int32 [32], P('dp'), may hold values from 128 to 1024, as said below
- layer_index: int32 [1], replicated, may hold values from 0 to 3
- norm_one_gain: bfloat16 [4, 768], replicated, may hold values from 0.5 to 1.5
- norm_one_bias: bfloat16 [4, 768], replicated, may hold values from -1.1953125 to 1.1953125
- attend_weight: bfloat16 [4, 768, 3, 768], P(None, None, None, 'tensor'), may hold values from -0.21875 to 0.21875
- query_bias: bfloat16 [4, 768], P(None, 'tensor'), may hold values from -1.1953125 to 1.1953125
- value_bias: bfloat16 [4, 768], P(None, 'tensor'), may hold values from -1.1953125 to 1.1953125
- output_weight: bfloat16 [4, 768, 768], P(None, 'tensor'), may hold values from -0.875 to 0.875
- output_bias: bfloat16 [4, 768], replicated, may hold values from -1.1953125 to 1.1953125
- norm_two_gain: bfloat16 [4, 768], replicated, may hold values from 0.5 to 1.5
- norm_two_bias: bfloat16 [4, 768], replicated, may hold values from -1.1953125 to 1.1953125
- expand_weight: bfloat16 [4, 768, 3072], P(None, None, 'tensor'), may hold values from -0.21875 to 0.21875
- expand_bias: bfloat16 [4, 3072], P(None, 'tensor'), may hold values from -1.1953125 to 1.1953125
- shrink_weight: bfloat16 [4, 3072, 768], P(None, 'tensor'), may hold values from -0.109375 to 0.109375
- shrink_bias: bfloat16 [4, 768], replicated, may hold values from -1.1953125 to 1.1953125
- cotangent: bfloat16 [32, 1024, 768], P('dp', 'tensor'), may hold values from -6 to 6
Outputs:
- block_output: float32 [32, 1024, 768], P('dp', 'tensor')
- input_grad: float32 [32, 1024, 768], P('dp', 'tensor')
- norm_one_gain_grad: float32 [768], replicated
- norm_one_bias_grad: float32 [768], replicated
- attend_weight_grad: float32 [768, 3, 768], P(None, None, 'tensor')
- query_bias_grad: float32 [768], P('tensor')
- value_bias_grad: float32 [768], P('tensor')
- output_weight_grad: float32 [768, 768], P('tensor')
- output_bias_grad: float32 [768], replicated
- norm_two_gain_grad: float32 [768], replicated
- norm_two_bias_grad: float32 [768], replicated
- expand_weight_grad: float32 [768, 3072], P(None, 'tensor')
- expand_bias_grad: float32 [3072], P('tensor')
- shrink_weight_grad: float32 [3072, 768], P('tensor')
- shrink_bias_grad: float32 [768], replicated
- rms_values: float32 [3], replicated
The draws below stay inside these ranges and needn't reach their ends.
Inputs may be any that keep to these rules, and one draw needn't show every extreme that they name: `lengths`: of the 2 sequences of each aligned block, one is longer than 512; some sequence has exactly 1024 tokens.
All inputs are finite; a program needn't handle non-finite values.
Results may differ from the reference program's by a relative error of at most 0.011.
Values may be sent and summed in bfloat16 or wider, within the bound.
A program may use at most 256 MiB of HBM per device.

```python
from functools import partial
import jax
import jax.numpy as jnp
from jax import lax

D = 768
H = 12
HD = 64
FF = 3072
LAYERS = 4
SEQ_LEN = 1024
MIN_LEN = 128
SEQ_DEV = 2
SEQS = 32


def draw_lengths(key, part):
    key = jax.random.fold_in(key, 11)
    first, second, third, fourth = jax.random.split(key, 4)
    spread = jax.random.randint(first, (SEQS,), MIN_LEN, SEQ_LEN + 1)
    longer = jax.random.randint(second, (SEQS,), SEQ_LEN // 2 + 1, SEQ_LEN + 1)
    chosen = jax.random.randint(third, (SEQS // SEQ_DEV, 1), 0, SEQ_DEV)
    is_long = (jnp.arange(SEQ_DEV)[None, :] == chosen).reshape(-1)
    lengths = jnp.where(is_long, longer, spread)
    fullest = jax.random.randint(fourth, (), 0, SEQS)
    lengths = jnp.where(jnp.arange(SEQS) == fullest, SEQ_LEN, lengths)
    return lengths.astype(jnp.int32)


def levels(stream_key, dims, cuts, least, high):
    def one(position, blocks):
        draws = jax.random.uniform(jax.random.fold_in(jax.random.fold_in(stream_key, 6), position), (blocks,), jnp.float32, least / len(cuts), high / len(cuts))
        return jnp.repeat(jnp.exp(draws), dims[position] // blocks).reshape((-1,) + (1,) * (len(dims) - position - 1))

    loudness = one(*cuts[0])
    for cut in cuts[1:]:
        loudness = loudness * one(*cut)
    return loudness


def gaussian(own_key, dims, scale, most, shards=(), held_as=jnp.bfloat16):
    level = levels(own_key, dims, shards, -0.22, 0.18) if shards else 1.0
    drawn = jax.random.normal(own_key, dims, jnp.float32) * scale * level
    return jnp.minimum(jnp.maximum(drawn, -most), most).astype(held_as)


def setup_inputs(seed: int = 0) -> dict:
    streams_of = jax.random.split(jax.random.key(seed), 18)
    tokens = gaussian(streams_of[0], (SEQS, SEQ_LEN, D), 1.0, 6.0, ((0, 16), (1, 2)))
    lengths = draw_lengths(jax.random.fold_in(streams_of[17], 71), 0)
    layer_index = jax.random.randint(streams_of[2], (1,), 0, LAYERS).astype(jnp.int32)
    norm_one_gain = jnp.clip(1.0 + 0.1 * jax.random.normal(streams_of[3], (LAYERS, D), jnp.float32), 0.5, 1.5).astype(jnp.bfloat16)
    norm_one_bias = gaussian(streams_of[4], (LAYERS, D), 0.2, 1.1953125)
    attend_weight = gaussian(streams_of[5], (LAYERS, D, 3, D), D ** -0.5, 0.21875, ((3, 2),))
    query_bias = gaussian(streams_of[6], (LAYERS, D), 0.2, 1.1953125, ((1, 2),))
    value_bias = gaussian(streams_of[7], (LAYERS, D), 0.2, 1.1953125, ((1, 2),))
    output_weight = gaussian(streams_of[8], (LAYERS, D, D), (D // 16) ** -0.5, 0.875, ((1, 2),))
    output_bias = gaussian(streams_of[9], (LAYERS, D), 0.2, 1.1953125)
    norm_two_gain = jnp.clip(1.0 + 0.1 * jax.random.normal(streams_of[10], (LAYERS, D), jnp.float32), 0.5, 1.5).astype(jnp.bfloat16)
    norm_two_bias = gaussian(streams_of[11], (LAYERS, D), 0.2, 1.1953125)
    expand_weight = gaussian(streams_of[12], (LAYERS, D, FF), D ** -0.5, 0.21875, ((2, 2),))
    expand_bias = gaussian(streams_of[13], (LAYERS, FF), 0.2, 1.1953125, ((1, 2),))
    shrink_weight = gaussian(streams_of[14], (LAYERS, FF, D), FF ** -0.5, 0.109375, ((1, 2),))
    shrink_bias = gaussian(streams_of[15], (LAYERS, D), 0.2, 1.1953125)
    cotangent = gaussian(streams_of[16], (SEQS, SEQ_LEN, D), 1.0, 6.0, ((0, 16), (1, 2)))
    return dict(tokens=tokens, lengths=lengths, layer_index=layer_index, norm_one_gain=norm_one_gain, norm_one_bias=norm_one_bias, attend_weight=attend_weight, query_bias=query_bias, value_bias=value_bias, output_weight=output_weight, output_bias=output_bias, norm_two_gain=norm_two_gain, norm_two_bias=norm_two_bias, expand_weight=expand_weight, expand_bias=expand_bias, shrink_weight=shrink_weight, shrink_bias=shrink_bias, cotangent=cotangent)


@jax.custom_vjp
def low(v):
    return lax.optimization_barrier(v.astype(jnp.bfloat16)).astype(jnp.float32)

@jax.custom_vjp
def low_back(v):
    return v

def low_keep(v):
    return (low(v), None)

def low_pass(kept, grad):
    return (grad,)

def back_keep(v):
    return (v, None)

def back_low(kept, grad):
    return (low(grad),)
low.defvjp(low_keep, low_pass)
low_back.defvjp(back_keep, back_low)
highest = lax.Precision.HIGHEST
epsilon = 1e-05
masked_fill = -1e+30

def layer_norm(values, gain, shift):
    center = lax.optimization_barrier(jnp.mean(values, axis=-1, keepdims=True))
    centered = values - center
    spread = lax.optimization_barrier(jnp.mean(centered * centered, axis=-1, keepdims=True))
    return centered * lax.rsqrt(spread + epsilon) * gain + shift

def attend_one(item):
    query, key, value, length = item
    scale = HD ** (-0.5)
    raw = jnp.einsum('qhd,khd->hqk', query, key, precision=highest)
    positions = jnp.arange(SEQ_LEN, dtype=jnp.int32)
    allowed = (positions[None, :] <= positions[:, None]) & (positions[None, :] < length)
    scores = low_back(jnp.where(allowed[None], raw * scale, masked_fill))
    weights = jax.nn.softmax(scores, axis=-1)
    return jnp.einsum('hqk,khd->qhd', low(weights), value, precision=highest)

def forward(lengths, tokens, gain_one, shift_one, attend, query_shift, value_shift, out_mat, out_shift, gain_two, shift_two, expand_mat, expand_shift, shrink_mat, shrink_shift):
    positions = jnp.arange(SEQ_LEN, dtype=jnp.int32)
    valid = (positions[None, :] < lengths[:, None]).astype(jnp.float32).reshape(-1, 1)
    rows_in = tokens.reshape(-1, D)
    normed_one = low(valid * layer_norm(rows_in, gain_one, shift_one))
    query = low(low_back(jnp.dot(normed_one, attend[:, 0, :], precision=highest) + query_shift))
    key = low(low_back(jnp.dot(normed_one, attend[:, 1, :], precision=highest)))
    value = low(low_back(jnp.dot(normed_one, attend[:, 2, :], precision=highest) + value_shift))
    shape = (SEQS, SEQ_LEN, H, HD)
    attended = lax.map(jax.checkpoint(attend_one), (query.reshape(shape), key.reshape(shape), value.reshape(shape), lengths))
    mixed = low(low_back(attended.reshape(-1, D)))
    attn_rows = low_back(jnp.dot(mixed, out_mat, precision=highest)) + out_shift
    resid_one = rows_in + valid * attn_rows
    normed_two = low(valid * layer_norm(resid_one, gain_two, shift_two))
    pre_act = low_back(jnp.dot(normed_two, expand_mat, precision=highest) + expand_shift)
    activated = low(jax.nn.gelu(pre_act, approximate=True))
    mlp_rows = low_back(jnp.dot(activated, shrink_mat, precision=highest)) + shrink_shift
    result = resid_one + valid * mlp_rows
    return (result.reshape(SEQS, SEQ_LEN, D), (attn_rows, mlp_rows, result, valid))

def reference(tokens, lengths, layer_index, norm_one_gain, norm_one_bias, attend_weight, query_bias, value_bias, output_weight, output_bias, norm_two_gain, norm_two_bias, expand_weight, expand_bias, shrink_weight, shrink_bias, cotangent):
    index = layer_index[0]
    stacks = (norm_one_gain, norm_one_bias, attend_weight, query_bias, value_bias, output_weight, output_bias, norm_two_gain, norm_two_bias, expand_weight, expand_bias, shrink_weight, shrink_bias)
    params = [lax.dynamic_index_in_dim(stack, index, 0, keepdims=False).astype(jnp.float32) for stack in stacks]
    result, pullback, extras = jax.vjp(partial(forward, lengths), tokens.astype(jnp.float32), *params, has_aux=True)
    grads = pullback(cotangent.astype(jnp.float32))
    attn_rows, mlp_rows, rows_out, valid = extras
    denom = jnp.sum(valid) * D
    rms_values = jnp.stack([jnp.sqrt(jnp.sum(valid * rows_out * rows_out) / denom), jnp.sqrt(jnp.sum(valid * attn_rows * attn_rows) / denom), jnp.sqrt(jnp.sum(valid * mlp_rows * mlp_rows) / denom)])
    return (result, grads[0], grads[1], grads[2], grads[3], grads[4], grads[5], grads[6], grads[7], grads[8], grads[9], grads[10], grads[11], grads[12], grads[13], rms_values)
```

```python
import functools

import jax
import jax.numpy as jnp
from jax import lax
from jax.experimental import pallas as pl
from jax.experimental.pallas import tpu as pltpu
from jax.sharding import PartitionSpec as P

HD = 64
PAIR = 2 * HD
epsilon = 1e-05
masked_fill = -1e30
VMEM_LIMIT = 56 * 1024 * 1024
f32 = jnp.float32
bf16 = jnp.bfloat16


def dot_nn(left, right):
    return lax.dot_general(left, right, (((1,), (0,)), ((), ())), preferred_element_type=f32)


def dot_nt(left, right):
    return lax.dot_general(left, right, (((1,), (1,)), ((), ())), preferred_element_type=f32)


def dot_tn(left, right):
    return lax.dot_general(left, right, (((0,), (0,)), ((), ())), preferred_element_type=f32)


def select_layer(stack, layer_index):
    return lax.dynamic_index_in_dim(stack, layer_index[0], 0, keepdims=False)


def whole(shape):
    return pl.BlockSpec(shape, lambda *index: (0,) * len(shape))


def params(steps=1):
    return pltpu.CompilerParams(
        dimension_semantics=("arbitrary",) * steps, vmem_limit_bytes=VMEM_LIMIT
    )


def project_kernel(length_ref, x_ref, gain_ref, shift_ref, weight_ref, bias_ref, h_ref, qkv_ref):
    rows = x_ref.shape[0]
    x = x_ref[...].astype(f32)
    center = jnp.mean(x, axis=-1, keepdims=True)
    x = x - center
    spread = jnp.mean(x * x, axis=-1, keepdims=True)
    h = x * lax.rsqrt(spread + epsilon) * gain_ref[...] + shift_ref[...]
    position = pl.program_id(0) * rows + lax.broadcasted_iota(jnp.int32, (rows, 1), 0)
    h = jnp.where(position < length_ref[0], h, 0.0).astype(bf16)
    h_ref[...] = h
    qkv_ref[...] = (dot_nn(h, weight_ref[...]) + bias_ref[...]).astype(bf16)


def project(length, x, gain, shift, weight, bias):
    seq_len, width = x.shape
    columns = weight.shape[1]
    rows = min(256, seq_len)
    return pl.pallas_call(
        project_kernel,
        grid=(seq_len // rows,),
        in_specs=[
            pl.BlockSpec(memory_space=pltpu.SMEM),
            pl.BlockSpec((rows, width), lambda i: (i, 0)),
            whole((1, width)),
            whole((1, width)),
            whole((width, columns)),
            whole((1, columns)),
        ],
        out_specs=[
            pl.BlockSpec((rows, width), lambda i: (i, 0)),
            pl.BlockSpec((rows, columns), lambda i: (i, 0)),
        ],
        out_shape=[
            jax.ShapeDtypeStruct((seq_len, width), bf16),
            jax.ShapeDtypeStruct((seq_len, columns), bf16),
        ],
        compiler_params=params(),
        name="project",
    )(length, x, gain, shift, weight, bias)


def lane_index(rows):
    return lax.broadcasted_iota(jnp.int32, (rows, PAIR), 1)


def causal_block(block):
    row = lax.broadcasted_iota(jnp.int32, (block, block), 0)
    column = lax.broadcasted_iota(jnp.int32, (block, block), 1)
    return row, column


def attend_kernel(length_ref, q_ref, k_ref, v_ref, o_ref, lse_ref, *, block):
    seq_len = q_ref.shape[0]
    lane = lane_index(seq_len)
    position = lax.broadcasted_iota(jnp.int32, (seq_len, PAIR), 0)
    key_bias = jnp.where(position < length_ref[0], 0.0, masked_fill)
    row, column = causal_block(block)
    keep = column <= row
    q = q_ref[...].astype(f32) * (HD**-0.5)
    k = k_ref[...].astype(f32)
    values = v_ref[...]
    low = lane < HD
    outs = []
    stats = []
    for head in range(2):
        mine = low if head == 0 else jnp.logical_not(low)
        spare = HD if head == 0 else 0
        q_aug = jnp.where(mine, q, jnp.where(lane == spare, 1.0, 0.0)).astype(bf16)
        k_aug = jnp.where(mine, k, jnp.where(lane == spare, key_bias, 0.0)).astype(bf16)
        v_own = jnp.where(mine, values, jnp.zeros_like(values))
        pieces = []
        notes = []
        for index in range(seq_len // block):
            start, end = index * block, (index + 1) * block
            scores = dot_nt(q_aug[start:end], k_aug[:end])
            last = jnp.where(keep, scores[:, start:end], masked_fill)
            if index:
                scores = jnp.concatenate([scores[:, :start], last], axis=1)
            else:
                scores = last
            top = jnp.max(scores, axis=-1, keepdims=True)
            weights = jnp.exp(scores - top)
            total = jnp.sum(weights, axis=-1, keepdims=True)
            mixed = dot_nn(weights.astype(bf16), v_own[:end])
            pieces.append(mixed * (1.0 / total))
            notes.append(jnp.broadcast_to(top + jnp.log(total), (block, PAIR)))
        outs.append(jnp.concatenate(pieces, axis=0))
        stats.append(jnp.concatenate(notes, axis=0))
    o_ref[...] = (outs[0] + outs[1]).astype(bf16)
    lse_ref[...] = jnp.where(low, stats[1], stats[0])


def attend(length, qkv):
    seq_len = qkv.shape[0]
    width = qkv.shape[1] // 3
    pairs = width // PAIR
    block = min(256, seq_len)

    def columns(part):
        return pl.BlockSpec((seq_len, PAIR), lambda i: (0, part * pairs + i))

    return pl.pallas_call(
        functools.partial(attend_kernel, block=block),
        grid=(pairs,),
        in_specs=[pl.BlockSpec(memory_space=pltpu.SMEM), columns(0), columns(1), columns(2)],
        out_specs=[columns(0), columns(0)],
        out_shape=[
            jax.ShapeDtypeStruct((seq_len, width), bf16),
            jax.ShapeDtypeStruct((seq_len, width), f32),
        ],
        compiler_params=params(),
        name="attend",
    )(length, qkv, qkv, qkv)


def three_parts(values):
    first = values.astype(bf16).astype(f32)
    rest = values - first
    second = rest.astype(bf16).astype(f32)
    return first, second, rest - second


def attend_back_kernel(
    length_ref, q_ref, k_ref, v_ref, o_ref, lse_ref, go_ref, gq_ref, gk_ref, gv_ref, acc_ref, *, block
):
    seq_len = q_ref.shape[0]
    scale = HD**-0.5
    lane = lane_index(seq_len)
    position = lax.broadcasted_iota(jnp.int32, (seq_len, PAIR), 0)
    inside = position < length_ref[0]
    key_bias = jnp.where(inside, 0.0, masked_fill)
    row, column = causal_block(block)
    keep = row <= column
    q = q_ref[...]
    k = k_ref[...]
    v = v_ref[...]
    go = go_ref[...]
    q_wide = q.astype(f32) * scale
    k_wide = k.astype(f32)
    v_wide = v.astype(f32)
    go_wide = go.astype(f32)
    both = go_wide * o_ref[...].astype(f32)
    lse_parts = three_parts(-lse_ref[...])
    low = lane < HD
    zero = jnp.zeros_like(q)
    acc_ref[...] = jnp.zeros_like(acc_ref)
    count = seq_len // block
    grads_k = [None] * count
    grads_v = [None] * count
    for head in range(2):
        mine = low if head == 0 else jnp.logical_not(low)
        spare = HD if head == 0 else 0
        delta = jnp.sum(jnp.where(mine, both, 0.0), axis=-1, keepdims=True)
        delta_parts = three_parts(-jnp.broadcast_to(delta, (seq_len, PAIR)))

        def extras(parts):
            return jnp.where(
                lane == spare + 1,
                parts[0],
                jnp.where(lane == spare + 2, parts[1], jnp.where(lane == spare + 3, parts[2], 0.0)),
            )

        ones = jnp.where((lane > spare) & (lane < spare + 4), 1.0, 0.0)
        q_aug = jnp.where(mine, q_wide, jnp.where(lane == spare, 1.0, extras(lse_parts))).astype(bf16)
        k_aug = jnp.where(mine, k_wide, jnp.where(lane == spare, key_bias, ones)).astype(bf16)
        v_aug = jnp.where(mine, v_wide, ones).astype(bf16)
        go_aug = jnp.where(mine, go_wide, extras(delta_parts)).astype(bf16)
        q_own = jnp.where(mine, q, zero)
        k_own = jnp.where(mine, k, zero)
        go_own = jnp.where(mine, go, zero)
        for index in range(count):
            start, end = index * block, (index + 1) * block
            scores = dot_nt(k_aug[start:end], q_aug[start:])
            first = jnp.where(keep, scores[:, :block], masked_fill)
            if index + 1 < count:
                scores = jnp.concatenate([first, scores[:, block:]], axis=1)
            else:
                scores = first
            shares = jnp.exp(scores)
            moved = dot_nt(v_aug[start:end], go_aug[start:])
            grad_scores = (shares * moved).astype(bf16)
            grad_v = dot_nn(shares.astype(bf16), go_own[start:])
            grad_k = dot_nn(grad_scores, q_own[start:])
            grads_v[index] = grad_v if head == 0 else grads_v[index] + grad_v
            grads_k[index] = grad_k if head == 0 else grads_k[index] + grad_k
            acc_ref[start:, :] += dot_tn(grad_scores, k_own[start:end])
    gq_ref[...] = (acc_ref[...] * scale).astype(bf16)
    gk_ref[...] = (jnp.concatenate(grads_k, axis=0) * scale).astype(bf16)
    gv_ref[...] = jnp.where(inside, jnp.concatenate(grads_v, axis=0), 0.0).astype(bf16)


def attend_back(length, qkv, o, lse, go):
    seq_len = qkv.shape[0]
    width = qkv.shape[1] // 3
    pairs = width // PAIR
    block = min(256, seq_len)

    def columns(part):
        return pl.BlockSpec((seq_len, PAIR), lambda i: (0, part * pairs + i))

    one = jax.ShapeDtypeStruct((seq_len, width), bf16)
    return pl.pallas_call(
        functools.partial(attend_back_kernel, block=block),
        grid=(pairs,),
        in_specs=[pl.BlockSpec(memory_space=pltpu.SMEM)]
        + [columns(0), columns(1), columns(2)]
        + [columns(0)] * 3,
        out_specs=[columns(0)] * 3,
        out_shape=[one, one, one],
        scratch_shapes=[pltpu.VMEM((seq_len, PAIR), f32)],
        compiler_params=params(),
        name="attend_back",
    )(length, qkv, qkv, qkv, o, lse, go)


def feed_kernel(
    h_ref, gf_ref, e_ref, b_ref, s_ref, *rest, chunk, carried
):
    if carried:
        f_in, gh_in, f_ref, gh_ref, de_ref, ds_ref, db_ref, act_ref, gu_ref = rest
    else:
        f_ref, gh_ref, de_ref, ds_ref, db_ref, act_ref, gu_ref = rest
    seq_len = h_ref.shape[0]
    tile = e_ref.shape[1]
    root = 0.7978845608
    cube = 0.044715

    @pl.when(pl.program_id(0) == 0)
    def _():
        if carried:
            f_ref[...] = f_in[...]
            gh_ref[...] = gh_in[...]
        else:
            f_ref[...] = jnp.zeros_like(f_ref)
            gh_ref[...] = jnp.zeros_like(gh_ref)

    e = e_ref[...]
    s = s_ref[...]
    bias = b_ref[...]
    total = jnp.zeros((1, tile), f32)
    for index in range(seq_len // chunk):
        rows = pl.ds(index * chunk, chunk)
        u = dot_nn(h_ref[rows, :], e) + bias
        ga = dot_nt(gf_ref[rows, :], s)
        square = u * u
        bent = jnp.tanh(u * (root + (root * cube) * square))
        half = 0.5 + 0.5 * bent
        act = (u * half).astype(bf16)
        slope = half + (0.5 * u) * (1.0 - bent * bent) * (root + (3.0 * root * cube) * square)
        gu_wide = (slope * ga).astype(bf16)
        act_ref[rows, :] = act
        gu_ref[rows, :] = gu_wide
        total += jnp.sum(gu_wide.astype(f32), axis=0, keepdims=True)
        f_ref[rows, :] += dot_nn(act, s)
        gh_ref[rows, :] += dot_nt(gu_wide, e)
    db_ref[...] = total
    ds_ref[...] = dot_tn(act_ref[...], gf_ref[...]).astype(bf16)
    de_ref[...] = dot_tn(h_ref[...], gu_ref[...]).astype(bf16)


def feed(h, gf, expand, bias, shrink, carry=None):
    seq_len, width = h.shape
    hidden = expand.shape[1]
    tile = min(512, hidden)
    chunk = min(256, seq_len)
    rows = whole((seq_len, width))
    row_shape = jax.ShapeDtypeStruct((seq_len, width), f32)
    carried = carry is not None
    return pl.pallas_call(
        functools.partial(feed_kernel, chunk=chunk, carried=carried),
        grid=(hidden // tile,),
        in_specs=[
            rows,
            rows,
            pl.BlockSpec((width, tile), lambda i: (0, i)),
            pl.BlockSpec((1, tile), lambda i: (0, i)),
            pl.BlockSpec((tile, width), lambda i: (i, 0)),
        ]
        + ([rows, rows] if carried else []),
        out_specs=[
            rows,
            rows,
            pl.BlockSpec((width, tile), lambda i: (0, i)),
            pl.BlockSpec((tile, width), lambda i: (i, 0)),
            pl.BlockSpec((1, tile), lambda i: (0, i)),
        ],
        out_shape=[
            row_shape,
            row_shape,
            jax.ShapeDtypeStruct((width, hidden), bf16),
            jax.ShapeDtypeStruct((hidden, width), bf16),
            jax.ShapeDtypeStruct((1, hidden), f32),
        ],
        scratch_shapes=[pltpu.VMEM((seq_len, tile), bf16), pltpu.VMEM((seq_len, tile), bf16)],
        compiler_params=params(),
        name="feed",
    )(h, gf, expand, bias, shrink, *(carry if carried else ()))


def norm_parts(values):
    center = jnp.mean(values, axis=-1, keepdims=True)
    centered = values - center
    spread = jnp.mean(centered * centered, axis=-1, keepdims=True)
    inverse = lax.rsqrt(spread + epsilon)
    return centered * inverse, inverse


def norm_back(unit, inverse, gain, grad):
    scaled = grad * gain
    return inverse * (
        scaled
        - jnp.mean(scaled, axis=-1, keepdims=True)
        - unit * jnp.mean(scaled * unit, axis=-1, keepdims=True)
    )


def body(
    tokens,
    lengths,
    layer_index,
    norm_one_gain,
    norm_one_bias,
    attend_weight,
    query_bias,
    value_bias,
    output_weight,
    output_bias,
    norm_two_gain,
    norm_two_bias,
    expand_weight,
    expand_bias,
    shrink_weight,
    shrink_bias,
    cotangent,
):
    seq_dev, half, width = tokens.shape
    seq_len = 2 * half
    dp = lax.axis_size("dp")
    here = lax.axis_index("tensor")
    there = 1 - here
    place = lax.axis_index("dp")
    swap = [(0, 1), (1, 0)]

    def exchange(values):
        return lax.ppermute(values, "tensor", swap)

    def pick(values, index):
        return lax.dynamic_index_in_dim(values, index, 0, keepdims=False)

    def joined(mine, other):
        out = jnp.zeros((seq_len,) + mine.shape[1:], mine.dtype)
        out = lax.dynamic_update_slice_in_dim(out, mine, here * half, 0)
        return lax.dynamic_update_slice_in_dim(out, other, there * half, 0)

    def rows_of(values, index):
        return lax.dynamic_slice_in_dim(values, index * half, half, 0)

    def layer(stack):
        return select_layer(stack, layer_index)

    x_far = joined(pick(tokens, there), exchange(pick(tokens, here)))
    x_own = joined(pick(tokens, here), exchange(pick(tokens, there)))
    len_far = lax.dynamic_slice_in_dim(lengths, there, 1, 0)
    len_own = lax.dynamic_slice_in_dim(lengths, here, 1, 0)
    cot_own = joined(pick(cotangent, here), exchange(pick(cotangent, there)))

    gain_one = layer(norm_one_gain).astype(f32)[None]
    shift_one = layer(norm_one_bias).astype(f32)[None]
    gain_two = layer(norm_two_gain).astype(f32)[None]
    shift_two = layer(norm_two_bias).astype(f32)[None]
    attend_flat = layer(attend_weight).reshape(width, -1)
    local = attend_flat.shape[1] // 3
    qkv_bias = jnp.concatenate(
        [layer(query_bias).astype(f32), jnp.zeros((local,), f32), layer(value_bias).astype(f32)]
    )[None]
    out_mat = layer(output_weight)
    out_shift = layer(output_bias).astype(f32)[None]
    expand_mat = layer(expand_weight)
    expand_shift = layer(expand_bias).astype(f32)[None]
    shrink_mat = layer(shrink_weight)
    shrink_shift = layer(shrink_bias).astype(f32)[None]

    def fetch(matrix):
        share = matrix.shape[0] // dp
        piece = lax.dynamic_slice_in_dim(matrix, place * share, share, 0)
        return lax.all_gather(exchange(piece), "dp", axis=0, tiled=True)

    out_far = fetch(out_mat)
    shrink_far = fetch(shrink_mat)
    expand_far = fetch(expand_mat)
    expand_shift_far = exchange(layer(expand_bias))[None].astype(f32)

    h_far, qkv_far = project(len_far, x_far, gain_one, shift_one, attend_flat, qkv_bias)
    o_far, lse_far = attend(len_far, qkv_far)
    o_got = exchange(o_far)
    h_own, qkv_own = project(len_own, x_own, gain_one, shift_one, attend_flat, qkv_bias)
    o_own, lse_own = attend(len_own, qkv_own)

    valid = (lax.broadcasted_iota(jnp.int32, (seq_len, 1), 0) < len_own[0]).astype(f32)
    attn = dot_nn(o_own, out_mat) + dot_nn(o_got, out_far) + out_shift
    resid = x_own.astype(f32) + valid * attn
    unit_two, inverse_two = norm_parts(resid)
    h_two = (valid * (unit_two * gain_two + shift_two)).astype(bf16)
    cot = cot_own.astype(f32)
    gf_wide = valid * cot
    gf = gf_wide.astype(bf16)

    f_part, gh_part, de_own, ds_own, db_own = feed(h_two, gf, expand_mat, expand_shift, shrink_mat)
    f_sum, gh_two, de_far, ds_far, db_far = feed(
        h_two, gf, expand_far, expand_shift_far, shrink_far, (f_part, gh_part)
    )
    mlp = f_sum + shrink_shift
    result = resid + valid * mlp
    result_got = exchange(rows_of(result, there).astype(bf16))

    grad_norm = valid * gh_two
    grad_resid = cot + norm_back(unit_two, inverse_two, gain_two, grad_norm)
    gain_two_grad = jnp.sum(grad_norm * unit_two, axis=0)
    shift_two_grad = jnp.sum(grad_norm, axis=0)
    grad_attn = valid * grad_resid
    ga = grad_attn.astype(bf16)
    go_send = dot_nt(ga, out_far).astype(bf16)
    go_far = exchange(go_send)
    go_own = dot_nt(ga, out_mat).astype(bf16)
    do_own = dot_tn(o_own, ga).astype(bf16)
    do_far = dot_tn(o_got, ga).astype(bf16)

    gq_own, gk_own, gv_own = attend_back(len_own, qkv_own, o_own, lse_own, go_own)

    def back_rows(gq, gk, gv, x, length):
        stacked = jnp.concatenate([gq, gk, gv], axis=1)
        inside = (lax.broadcasted_iota(jnp.int32, (seq_len, 1), 0) < length[0]).astype(f32)
        partial = inside * dot_nt(stacked, attend_flat)
        unit, inverse = norm_parts(x.astype(f32))
        return (
            stacked,
            norm_back(unit, inverse, gain_one, partial),
            jnp.sum(partial * unit, axis=0),
            jnp.sum(partial, axis=0),
        )

    stack_own, back_own, gain_own, shift_own = back_rows(gq_own, gk_own, gv_own, x_own, len_own)
    back_own = grad_resid + back_own
    in_far_got = exchange(rows_of(back_own, there).astype(bf16))

    gq_far, gk_far, gv_far = attend_back(len_far, qkv_far, o_far, lse_far, go_far)
    stack_far, back_far, gain_far, shift_far = back_rows(gq_far, gk_far, gv_far, x_far, len_far)
    in_own_got = exchange(rows_of(back_far, there).astype(bf16))
    da = (dot_tn(h_own, stack_own) + dot_tn(h_far, stack_far)).astype(bf16)

    input_own = rows_of(back_own, here) + in_own_got.astype(f32)
    input_far = rows_of(back_far, here) + in_far_got.astype(f32)

    def by_sequence(own, far):
        out = jnp.zeros((2,) + own.shape, own.dtype)
        out = lax.dynamic_update_index_in_dim(out, own, here, 0)
        return lax.dynamic_update_index_in_dim(out, far, there, 0)

    block_output = by_sequence(rows_of(result, here), result_got.astype(f32))
    input_grad = by_sequence(input_own, input_far)

    def by_half(own, far):
        return by_sequence(own, far).reshape((2 * own.shape[0],) + own.shape[1:])

    def total(own, far):
        share = lax.psum_scatter(
            by_half(own, far), ("tensor", "dp"), scatter_dimension=0, tiled=True
        )
        return lax.all_gather(share, "dp", axis=0, tiled=True).astype(f32)

    shrink_grad = total(ds_own, ds_far)
    expand_grad = total(de_own, de_far)
    out_grad = total(do_own, do_far)
    attend_grad = lax.psum(da, "dp").astype(f32).reshape(width, 3, local)
    expand_shift_grad = by_sequence(db_own[0], db_far[0])
    qv_bias = jnp.stack(
        [
            jnp.sum(gq_own.astype(f32), axis=0) + jnp.sum(gq_far.astype(f32), axis=0),
            jnp.sum(gv_own.astype(f32), axis=0) + jnp.sum(gv_far.astype(f32), axis=0),
        ]
    )
    bias_grads = by_sequence(qv_bias, jnp.zeros_like(qv_bias))
    counters = jnp.stack(
        [
            jnp.sum(valid * result * result),
            jnp.sum(valid * attn * attn),
            jnp.sum(valid * mlp * mlp),
            jnp.sum(valid),
        ]
    )
    small = lax.psum(
        (
            gain_own + gain_far,
            shift_own + shift_far,
            jnp.sum(grad_attn, axis=0),
            gain_two_grad,
            shift_two_grad,
            jnp.sum(gf_wide, axis=0),
            counters,
            expand_shift_grad,
            bias_grads,
        ),
        ("dp", "tensor"),
    )
    rms_values = jnp.sqrt(small[6][:3] / (small[6][3] * width))
    biases = pick(small[8], here)
    return (
        block_output,
        input_grad,
        small[0],
        small[1],
        attend_grad,
        biases[0],
        biases[1],
        out_grad,
        small[2],
        small[3],
        small[4],
        expand_grad,
        pick(small[7], here),
        shrink_grad,
        small[5],
        rms_values,
    )


def solution(mesh):
    in_specs = (
        P("dp", "tensor", None),
        P("dp"),
        P(),
        P(),
        P(),
        P(None, None, None, "tensor"),
        P(None, "tensor"),
        P(None, "tensor"),
        P(None, "tensor", None),
        P(),
        P(),
        P(),
        P(None, None, "tensor"),
        P(None, "tensor"),
        P(None, "tensor", None),
        P(),
        P("dp", "tensor", None),
    )
    out_specs = (
        P("dp", "tensor", None),
        P("dp", "tensor", None),
        P(),
        P(),
        P(None, None, "tensor"),
        P("tensor"),
        P("tensor"),
        P("tensor", None),
        P(),
        P(),
        P(),
        P(None, "tensor"),
        P("tensor"),
        P("tensor", None),
        P(),
        P(),
    )
    return jax.shard_map(body, mesh=mesh, in_specs=in_specs, out_specs=out_specs, check_vma=False)
```

```python
import functools

import jax
import jax.numpy as jnp
from jax import lax
from jax.experimental import pallas as pl
from jax.experimental.pallas import tpu as pltpu
from jax.sharding import PartitionSpec as P

HD = 64
PAIR = 2 * HD
epsilon = 1e-05
masked_fill = -1e30
VMEM_LIMIT = 56 * 1024 * 1024
f32 = jnp.float32
bf16 = jnp.bfloat16


def dot_nn(left, right):
    return lax.dot_general(left, right, (((1,), (0,)), ((), ())), preferred_element_type=f32)


def dot_nt(left, right):
    return lax.dot_general(left, right, (((1,), (1,)), ((), ())), preferred_element_type=f32)


def dot_tn(left, right):
    return lax.dot_general(left, right, (((0,), (0,)), ((), ())), preferred_element_type=f32)


def select_layer(stack, layer_index):
    return lax.dynamic_index_in_dim(stack, layer_index[0], 0, keepdims=False)


def whole(shape):
    return pl.BlockSpec(shape, lambda *index: (0,) * len(shape))


def params(steps=1):
    return pltpu.CompilerParams(
        dimension_semantics=("arbitrary",) * steps, vmem_limit_bytes=VMEM_LIMIT
    )


def project_kernel(length_ref, x_ref, gain_ref, shift_ref, weight_ref, bias_ref, h_ref, qkv_ref):
    rows = x_ref.shape[0]
    x = x_ref[...].astype(f32)
    center = jnp.mean(x, axis=-1, keepdims=True)
    x = x - center
    spread = jnp.mean(x * x, axis=-1, keepdims=True)
    h = x * lax.rsqrt(spread + epsilon) * gain_ref[...] + shift_ref[...]
    position = pl.program_id(0) * rows + lax.broadcasted_iota(jnp.int32, (rows, 1), 0)
    h = jnp.where(position < length_ref[0], h, 0.0).astype(bf16)
    h_ref[...] = h
    qkv_ref[...] = (dot_nn(h, weight_ref[...]) + bias_ref[...]).astype(bf16)


def project(length, x, gain, shift, weight, bias):
    seq_len, width = x.shape
    columns = weight.shape[1]
    rows = min(256, seq_len)
    return pl.pallas_call(
        project_kernel,
        grid=(seq_len // rows,),
        in_specs=[
            pl.BlockSpec(memory_space=pltpu.SMEM),
            pl.BlockSpec((rows, width), lambda i: (i, 0)),
            whole((1, width)),
            whole((1, width)),
            whole((width, columns)),
            whole((1, columns)),
        ],
        out_specs=[
            pl.BlockSpec((rows, width), lambda i: (i, 0)),
            pl.BlockSpec((rows, columns), lambda i: (i, 0)),
        ],
        out_shape=[
            jax.ShapeDtypeStruct((seq_len, width), bf16),
            jax.ShapeDtypeStruct((seq_len, columns), bf16),
        ],
        compiler_params=params(),
        name="project",
    )(length, x, gain, shift, weight, bias)


def lane_index(rows):
    return lax.broadcasted_iota(jnp.int32, (rows, PAIR), 1)


def causal_block(block):
    row = lax.broadcasted_iota(jnp.int32, (block, block), 0)
    column = lax.broadcasted_iota(jnp.int32, (block, block), 1)
    return row, column


def attend_kernel(length_ref, q_ref, k_ref, v_ref, o_ref, lse_ref, *, block):
    seq_len = q_ref.shape[0]
    lane = lane_index(seq_len)
    position = lax.broadcasted_iota(jnp.int32, (seq_len, PAIR), 0)
    key_bias = jnp.where(position < length_ref[0], 0.0, masked_fill)
    row, column = causal_block(block)
    keep = column <= row
    q = q_ref[...].astype(f32) * (HD**-0.5)
    k = k_ref[...].astype(f32)
    values = v_ref[...]
    low = lane < HD
    outs = []
    stats = []
    for head in range(2):
        mine = low if head == 0 else jnp.logical_not(low)
        spare = HD if head == 0 else 0
        q_aug = jnp.where(mine, q, jnp.where(lane == spare, 1.0, 0.0)).astype(bf16)
        k_aug = jnp.where(mine, k, jnp.where(lane == spare, key_bias, 0.0)).astype(bf16)
        v_own = jnp.where(mine, values, jnp.zeros_like(values))
        pieces = []
        notes = []
        for index in range(seq_len // block):
            start, end = index * block, (index + 1) * block
            scores = dot_nt(q_aug[start:end], k_aug[:end])
            last = jnp.where(keep, scores[:, start:end], masked_fill)
            if index:
                scores = jnp.concatenate([scores[:, :start], last], axis=1)
            else:
                scores = last
            top = jnp.max(scores, axis=-1, keepdims=True)
            weights = jnp.exp(scores - top)
            total = jnp.sum(weights, axis=-1, keepdims=True)
            mixed = dot_nn(weights.astype(bf16), v_own[:end])
            pieces.append(mixed * (1.0 / total))
            notes.append(jnp.broadcast_to(top + jnp.log(total), (block, PAIR)))
        outs.append(jnp.concatenate(pieces, axis=0))
        stats.append(jnp.concatenate(notes, axis=0))
    o_ref[...] = (outs[0] + outs[1]).astype(bf16)
    lse_ref[...] = jnp.where(low, stats[1], stats[0])


def attend(length, qkv):
    seq_len = qkv.shape[0]
    width = qkv.shape[1] // 3
    pairs = width // PAIR
    block = min(256, seq_len)

    def columns(part):
        return pl.BlockSpec((seq_len, PAIR), lambda i: (0, part * pairs + i))

    return pl.pallas_call(
        functools.partial(attend_kernel, block=block),
        grid=(pairs,),
        in_specs=[pl.BlockSpec(memory_space=pltpu.SMEM), columns(0), columns(1), columns(2)],
        out_specs=[columns(0), columns(0)],
        out_shape=[
            jax.ShapeDtypeStruct((seq_len, width), bf16),
            jax.ShapeDtypeStruct((seq_len, width), f32),
        ],
        compiler_params=params(),
        name="attend",
    )(length, qkv, qkv, qkv)


def three_parts(values):
    first = values.astype(bf16).astype(f32)
    rest = values - first
    second = rest.astype(bf16).astype(f32)
    return first, second, rest - second


def attend_back_kernel(
    length_ref, q_ref, k_ref, v_ref, o_ref, lse_ref, go_ref, gq_ref, gk_ref, gv_ref, acc_ref, *, block
):
    seq_len = q_ref.shape[0]
    scale = HD**-0.5
    lane = lane_index(seq_len)
    position = lax.broadcasted_iota(jnp.int32, (seq_len, PAIR), 0)
    inside = position < length_ref[0]
    key_bias = jnp.where(inside, 0.0, masked_fill)
    row, column = causal_block(block)
    keep = row <= column
    q = q_ref[...]
    k = k_ref[...]
    v = v_ref[...]
    go = go_ref[...]
    q_wide = q.astype(f32) * scale
    k_wide = k.astype(f32)
    v_wide = v.astype(f32)
    go_wide = go.astype(f32)
    both = go_wide * o_ref[...].astype(f32)
    lse_parts = three_parts(-lse_ref[...])
    low = lane < HD
    zero = jnp.zeros_like(q)
    acc_ref[...] = jnp.zeros_like(acc_ref)
    count = seq_len // block
    grads_k = [None] * count
    grads_v = [None] * count
    for head in range(2):
        mine = low if head == 0 else jnp.logical_not(low)
        spare = HD if head == 0 else 0
        delta = jnp.sum(jnp.where(mine, both, 0.0), axis=-1, keepdims=True)
        delta_parts = three_parts(-jnp.broadcast_to(delta, (seq_len, PAIR)))

        def extras(parts):
            return jnp.where(
                lane == spare + 1,
                parts[0],
                jnp.where(lane == spare + 2, parts[1], jnp.where(lane == spare + 3, parts[2], 0.0)),
            )

        ones = jnp.where((lane > spare) & (lane < spare + 4), 1.0, 0.0)
        q_aug = jnp.where(mine, q_wide, jnp.where(lane == spare, 1.0, extras(lse_parts))).astype(bf16)
        k_aug = jnp.where(mine, k_wide, jnp.where(lane == spare, key_bias, ones)).astype(bf16)
        v_aug = jnp.where(mine, v_wide, ones).astype(bf16)
        go_aug = jnp.where(mine, go_wide, extras(delta_parts)).astype(bf16)
        q_own = jnp.where(mine, q, zero)
        k_own = jnp.where(mine, k, zero)
        go_own = jnp.where(mine, go, zero)
        for index in range(count):
            start, end = index * block, (index + 1) * block
            scores = dot_nt(k_aug[start:end], q_aug[start:])
            first = jnp.where(keep, scores[:, :block], masked_fill)
            if index + 1 < count:
                scores = jnp.concatenate([first, scores[:, block:]], axis=1)
            else:
                scores = first
            shares = jnp.exp(scores)
            moved = dot_nt(v_aug[start:end], go_aug[start:])
            grad_scores = (shares * moved).astype(bf16)
            grad_v = dot_nn(shares.astype(bf16), go_own[start:])
            grad_k = dot_nn(grad_scores, q_own[start:])
            grads_v[index] = grad_v if head == 0 else grads_v[index] + grad_v
            grads_k[index] = grad_k if head == 0 else grads_k[index] + grad_k
            acc_ref[start:, :] += dot_tn(grad_scores, k_own[start:end])
    gq_ref[...] = (acc_ref[...] * scale).astype(bf16)
    gk_ref[...] = (jnp.concatenate(grads_k, axis=0) * scale).astype(bf16)
    gv_ref[...] = jnp.where(inside, jnp.concatenate(grads_v, axis=0), 0.0).astype(bf16)


def attend_back(length, qkv, o, lse, go):
    seq_len = qkv.shape[0]
    width = qkv.shape[1] // 3
    pairs = width // PAIR
    block = min(256, seq_len)

    def columns(part):
        return pl.BlockSpec((seq_len, PAIR), lambda i: (0, part * pairs + i))

    one = jax.ShapeDtypeStruct((seq_len, width), bf16)
    return pl.pallas_call(
        functools.partial(attend_back_kernel, block=block),
        grid=(pairs,),
        in_specs=[pl.BlockSpec(memory_space=pltpu.SMEM)]
        + [columns(0), columns(1), columns(2)]
        + [columns(0)] * 3,
        out_specs=[columns(0)] * 3,
        out_shape=[one, one, one],
        scratch_shapes=[pltpu.VMEM((seq_len, PAIR), f32)],
        compiler_params=params(),
        name="attend_back",
    )(length, qkv, qkv, qkv, o, lse, go)


def feed_kernel(
    h_ref, gf_ref, e_ref, b_ref, s_ref, *rest, chunk, carried
):
    if carried:
        f_in, gh_in, f_ref, gh_ref, de_ref, ds_ref, db_ref, act_ref, gu_ref = rest
    else:
        f_ref, gh_ref, de_ref, ds_ref, db_ref, act_ref, gu_ref = rest
    seq_len = h_ref.shape[0]
    tile = e_ref.shape[1]
    root = 0.7978845608
    cube = 0.044715

    @pl.when(pl.program_id(0) == 0)
    def _():
        if carried:
            f_ref[...] = f_in[...]
            gh_ref[...] = gh_in[...]
        else:
            f_ref[...] = jnp.zeros_like(f_ref)
            gh_ref[...] = jnp.zeros_like(gh_ref)

    e = e_ref[...]
    s = s_ref[...]
    bias = b_ref[...]
    total = jnp.zeros((1, tile), f32)
    for index in range(seq_len // chunk):
        rows = pl.ds(index * chunk, chunk)
        u = dot_nn(h_ref[rows, :], e) + bias
        ga = dot_nt(gf_ref[rows, :], s)
        square = u * u
        bent = jnp.tanh(u * (root + (root * cube) * square))
        half = 0.5 + 0.5 * bent
        act = (u * half).astype(bf16)
        slope = half + (0.5 * u) * (1.0 - bent * bent) * (root + (3.0 * root * cube) * square)
        gu_wide = (slope * ga).astype(bf16)
        act_ref[rows, :] = act
        gu_ref[rows, :] = gu_wide
        total += jnp.sum(gu_wide.astype(f32), axis=0, keepdims=True)
        f_ref[rows, :] += dot_nn(act, s)
        gh_ref[rows, :] += dot_nt(gu_wide, e)
    db_ref[...] = total
    ds_ref[...] = dot_tn(act_ref[...], gf_ref[...]).astype(bf16)
    de_ref[...] = dot_tn(gu_ref[...], h_ref[...]).astype(bf16)


def feed(h, gf, expand, bias, shrink, carry=None):
    seq_len, width = h.shape
    hidden = expand.shape[1]
    tile = min(512, hidden)
    chunk = min(256, seq_len)
    rows = whole((seq_len, width))
    row_shape = jax.ShapeDtypeStruct((seq_len, width), f32)
    carried = carry is not None
    return pl.pallas_call(
        functools.partial(feed_kernel, chunk=chunk, carried=carried),
        grid=(hidden // tile,),
        in_specs=[
            rows,
            rows,
            pl.BlockSpec((width, tile), lambda i: (0, i)),
            pl.BlockSpec((1, tile), lambda i: (0, i)),
            pl.BlockSpec((tile, width), lambda i: (i, 0)),
        ]
        + ([rows, rows] if carried else []),
        out_specs=[
            rows,
            rows,
            pl.BlockSpec((tile, width), lambda i: (i, 0)),
            pl.BlockSpec((tile, width), lambda i: (i, 0)),
            pl.BlockSpec((1, tile), lambda i: (0, i)),
        ],
        out_shape=[
            row_shape,
            row_shape,
            jax.ShapeDtypeStruct((hidden, width), bf16),
            jax.ShapeDtypeStruct((hidden, width), bf16),
            jax.ShapeDtypeStruct((1, hidden), f32),
        ],
        scratch_shapes=[pltpu.VMEM((seq_len, tile), bf16), pltpu.VMEM((seq_len, tile), bf16)],
        compiler_params=params(),
        name="feed",
    )(h, gf, expand, bias, shrink, *(carry if carried else ()))


class Ring:
    def __init__(self, dp):
        self.chips = dp // 2
        self.far_hops = self.chips // 2
        self.near_hops = self.chips - 1 - self.far_hops
        place = lax.axis_index("dp")
        self.tensor = lax.axis_index("tensor")
        self.core = place % 2
        chip = place // 2
        depth = chip // 2
        self.spot = depth + (chip % 2) * (self.chips - 1 - 2 * depth)
        self.turn = 1 - 2 * self.core

    def device(self, spot, core):
        spot = (spot + self.chips) % self.chips
        side = spot // (self.chips // 2)
        chip = 2 * (spot + side * (self.chips - 1 - 2 * spot)) + side
        return (chip * 2 + core, self.tensor)

    def ahead(self):
        return self.device(self.spot + self.turn, self.core)

    def behind(self):
        return self.device(self.spot - self.turn, self.core)

    def sibling(self):
        return self.device(self.spot, 1 - self.core)

    def partner(self):
        return (lax.axis_index("dp"), 1 - self.tensor)

    def chunk(self, offset):
        return (self.spot + self.turn * offset + 2 * self.chips) % self.chips


def send(source, target, sems, index, device):
    copy = pltpu.make_async_remote_copy(
        src_ref=source,
        dst_ref=target,
        send_sem=sems.at[0, index],
        recv_sem=sems.at[1, index],
        device_id=device,
        device_id_type=pl.DeviceIdType.MESH,
    )
    return copy


def loop(start, stop, step):
    def run(index, carry):
        step(index)
        return carry

    lax.fori_loop(start, stop, run, 0)


class Group:
    def __init__(self, ring, local, scratch):
        self.ring = ring
        self.local = local
        self.pair, self.slots, self.outbox, self.pair_sems, self.ring_sems = scratch
        self.rows = local.shape[0] // (2 * ring.chips)

    @staticmethod
    def scratch(rows, width, dp):
        chips = dp // 2
        size = rows // (2 * chips)
        return [
            pltpu.VMEM((chips, size, width), bf16),
            pltpu.VMEM((chips, size, width), bf16),
            pltpu.VMEM((chips, size, width), bf16),
            pltpu.SemaphoreType.DMA((2, chips)),
            pltpu.SemaphoreType.DMA((2, chips)),
        ]

    def place(self, core, chunk):
        start = (core * self.ring.chips + chunk) * self.rows
        return pl.ds(pl.multiple_of(start, 16), self.rows)

    def to_sibling(self, chunk):
        source = self.local.at[self.place(1 - self.ring.core, chunk)]
        return send(source, self.pair.at[chunk], self.pair_sems, chunk, self.ring.sibling())

    def hand_over(self):
        ring = self.ring

        def both(step):
            self.to_sibling(ring.chunk(step - ring.far_hops)).start()
            self.to_sibling(ring.chunk(ring.near_hops - step)).start()

        loop(0, ring.near_hops, both)
        self.to_sibling(ring.chunk(-1)).start()
        self.to_sibling(ring.chunk(0)).start()

    def term(self, chunk):
        self.to_sibling(chunk).wait_recv()
        mine = self.local[self.place(self.ring.core, chunk), :].astype(f32)
        return mine + self.pair[chunk].astype(f32)

    def far_copy(self, step):
        return send(
            self.outbox.at[step], self.slots.at[step], self.ring_sems, step, self.ring.ahead()
        )

    def near_copy(self, step):
        slot = self.ring.far_hops + step
        return send(
            self.outbox.at[slot], self.slots.at[slot], self.ring_sems, slot, self.ring.behind()
        )

    def far_step(self, step, first=False):
        value = self.term(self.ring.chunk(self.ring.far_hops - step))
        if not first:
            self.far_copy(step - 1).wait_recv()
            value += self.slots[step - 1].astype(f32)
        self.outbox[step] = value.astype(bf16)
        self.far_copy(step).start()

    def near_step(self, step, first=False):
        slot = self.ring.far_hops + step
        value = self.term(self.ring.chunk(step - self.ring.near_hops))
        if not first:
            self.near_copy(step - 1).wait_recv()
            value += self.slots[slot - 1].astype(f32)
        self.outbox[slot] = value.astype(bf16)
        self.near_copy(step).start()

    def finish(self):
        ring = self.ring
        value = self.term(ring.chunk(0))
        self.far_copy(ring.far_hops - 1).wait_recv()
        self.near_copy(ring.near_hops - 1).wait_recv()
        value += self.slots[ring.far_hops - 1].astype(f32)
        return value + self.slots[ring.chips - 2].astype(f32)

    def sent(self):
        ring = self.ring
        loop(0, ring.chips, lambda chunk: self.to_sibling(chunk).wait_send())
        loop(0, ring.far_hops, lambda step: self.far_copy(step).wait_send())
        loop(0, ring.near_hops, lambda step: self.near_copy(step).wait_send())


class Spread:
    def __init__(self, ring, out, scratch):
        self.ring = ring
        self.out = out
        self.pair_sems, self.ring_sems = scratch
        self.rows = out.shape[0] // (2 * ring.chips)

    @staticmethod
    def scratch(dp):
        chips = dp // 2
        return [pltpu.SemaphoreType.DMA((2, chips)), pltpu.SemaphoreType.DMA((2, chips))]

    def place(self, core, chunk):
        start = (core * self.ring.chips + chunk) * self.rows
        return pl.ds(pl.multiple_of(start, 16), self.rows)

    def pass_on(self, chunk, slot, device):
        where = self.out.at[self.place(self.ring.core, chunk)]
        return send(where, where, self.ring_sems, slot, device)

    def to_sibling(self, chunk):
        where = self.out.at[self.place(self.ring.core, chunk)]
        return send(where, where, self.pair_sems, chunk, self.ring.sibling())

    def from_sibling(self, chunk):
        where = self.out.at[self.place(1 - self.ring.core, chunk)]
        return send(where, where, self.pair_sems, chunk, self.ring.sibling())

    def far_copy(self, step):
        return self.pass_on(self.ring.chunk(-step), step, self.ring.ahead())

    def near_copy(self, step):
        return self.pass_on(self.ring.chunk(step), self.ring.far_hops + step, self.ring.behind())

    def far_landed(self, step):
        return self.pass_on(self.ring.chunk(-step - 1), step, self.ring.ahead())

    def near_landed(self, step):
        return self.pass_on(
            self.ring.chunk(step + 1), self.ring.far_hops + step, self.ring.behind()
        )

    def begin(self):
        self.far_copy(0).start()
        self.near_copy(0).start()
        self.to_sibling(self.ring.chunk(0)).start()

    def far_step(self, step, last=False):
        self.far_landed(step - 1).wait_recv()
        if not last:
            self.far_copy(step).start()
        self.to_sibling(self.ring.chunk(-step)).start()

    def near_step(self, step, last=False):
        self.near_landed(step - 1).wait_recv()
        if not last:
            self.near_copy(step).start()
        self.to_sibling(self.ring.chunk(step)).start()

    def sent(self):
        ring = self.ring
        loop(0, ring.chips, lambda chunk: self.from_sibling(chunk).wait_recv())
        loop(0, ring.chips, lambda chunk: self.to_sibling(chunk).wait_send())
        loop(0, ring.far_hops, lambda step: self.far_copy(step).wait_send())
        loop(0, ring.near_hops, lambda step: self.near_copy(step).wait_send())


def greet(ring):
    barrier = pltpu.get_barrier_semaphore()
    for device in (ring.ahead(), ring.behind(), ring.sibling(), ring.partner()):
        pl.semaphore_signal(barrier, inc=1, device_id=device, device_id_type=pl.DeviceIdType.MESH)
    pl.semaphore_wait(barrier, 4)


def fill(local, pieces, sems, first):
    row = 0
    copies = []
    for index, piece in enumerate(pieces):
        count = piece.shape[0]
        copy = pltpu.make_async_copy(piece, local.at[pl.ds(row, count)], sems.at[first + index])
        copy.start()
        copies.append(copy)
        row += count
    return copies


def reduce_kernel(
    e_far, s_far, w_far, m_far, e_own, s_own, w_own, m_own, q_grad, q_more, *rest, dp
):
    feed_out, attend_out = rest[:2]
    rest = list(rest[2:])

    def take(count):
        taken = rest[:count]
        del rest[:count]
        return taken

    fill_sems, far_local, own_local, q_local, shard, got, cross_sems = take(7)
    ring = Ring(dp)
    far = Group(ring, far_local, take(5))
    own = Group(ring, own_local, take(5))
    query = Group(ring, q_local, take(5))
    feed_spread = Spread(ring, feed_out, take(2))
    attend_spread = Spread(ring, attend_out, take(2))

    copies = fill(far_local, (e_far, s_far, w_far, m_far), fill_sems, 0)
    copies += fill(own_local, (e_own, s_own, w_own, m_own), fill_sems, 4)
    copies += fill(q_local, (q_grad, q_more), fill_sems, 8)
    greet(ring)
    for copy in copies:
        copy.wait()

    groups = (far, own, query)
    for group in groups:
        group.hand_over()
    for group in groups:
        group.far_step(0, first=True)
        group.near_step(0, first=True)

    def middle(step):
        for group in groups:
            group.far_step(step)
            group.near_step(step)

    loop(1, ring.near_hops, middle)
    for group in groups:
        group.far_step(ring.far_hops - 1)

    cross = send(shard, got, cross_sems, 0, ring.partner())
    shard[...] = far.finish().astype(bf16)
    cross.start()
    attend_out[attend_spread.place(ring.core, ring.spot), :] = query.finish().astype(bf16)
    attend_spread.begin()
    value = own.finish()
    cross.wait_recv()
    feed_out[feed_spread.place(ring.core, ring.spot), :] = (value + got[...].astype(f32)).astype(bf16)
    feed_spread.begin()

    def onward(step):
        for spread in (attend_spread, feed_spread):
            spread.far_step(step)
            spread.near_step(step)

    loop(1, ring.near_hops, onward)
    for spread in (attend_spread, feed_spread):
        spread.far_step(ring.near_hops)
        spread.near_step(ring.near_hops, last=True)
        spread.far_step(ring.far_hops, last=True)
    for group in groups:
        group.sent()
    cross.wait_send()
    for spread in (attend_spread, feed_spread):
        spread.sent()


def padded(rows, dp):
    unit = 16 * dp
    return -(-rows // unit) * unit


def reduce_all(far, own, query, dp):
    width = far[0].shape[1]
    feed_rows = sum(piece.shape[0] for piece in own)
    query_rows = sum(piece.shape[0] for piece in query)
    size = feed_rows // dp
    anywhere = pl.BlockSpec(memory_space=pl.ANY)
    inside = pl.BlockSpec(memory_space=pltpu.VMEM)
    return pl.pallas_call(
        functools.partial(reduce_kernel, dp=dp),
        in_specs=[anywhere] * 10,
        out_specs=[inside, inside],
        out_shape=[
            jax.ShapeDtypeStruct((feed_rows, width), bf16),
            jax.ShapeDtypeStruct((query_rows, width), bf16),
        ],
        scratch_shapes=[
            pltpu.SemaphoreType.DMA((10,)),
            pltpu.VMEM((feed_rows, width), bf16),
            pltpu.VMEM((feed_rows, width), bf16),
            pltpu.VMEM((query_rows, width), bf16),
            pltpu.VMEM((size, width), bf16),
            pltpu.VMEM((size, width), bf16),
            pltpu.SemaphoreType.DMA((2, 1)),
        ]
        + Group.scratch(feed_rows, width, dp)
        + Group.scratch(feed_rows, width, dp)
        + Group.scratch(query_rows, width, dp)
        + Spread.scratch(dp)
        + Spread.scratch(dp),
        compiler_params=pltpu.CompilerParams(
            collective_id=0, has_side_effects=True, vmem_limit_bytes=VMEM_LIMIT
        ),
        name="reduce_all",
    )(*far, *own, *query)


def norm_parts(values):
    center = jnp.mean(values, axis=-1, keepdims=True)
    centered = values - center
    spread = jnp.mean(centered * centered, axis=-1, keepdims=True)
    inverse = lax.rsqrt(spread + epsilon)
    return centered * inverse, inverse


def norm_back(unit, inverse, gain, grad):
    scaled = grad * gain
    return inverse * (
        scaled
        - jnp.mean(scaled, axis=-1, keepdims=True)
        - unit * jnp.mean(scaled * unit, axis=-1, keepdims=True)
    )


def body(
    tokens,
    lengths,
    layer_index,
    norm_one_gain,
    norm_one_bias,
    attend_weight,
    query_bias,
    value_bias,
    output_weight,
    output_bias,
    norm_two_gain,
    norm_two_bias,
    expand_weight,
    expand_bias,
    shrink_weight,
    shrink_bias,
    cotangent,
):
    seq_dev, half, width = tokens.shape
    seq_len = 2 * half
    dp = lax.axis_size("dp")
    here = lax.axis_index("tensor")
    there = 1 - here
    place = lax.axis_index("dp")
    swap = [(0, 1), (1, 0)]

    def exchange(values):
        return lax.ppermute(values, "tensor", swap)

    def pick(values, index):
        return lax.dynamic_index_in_dim(values, index, 0, keepdims=False)

    def joined(mine, other):
        out = jnp.zeros((seq_len,) + mine.shape[1:], mine.dtype)
        out = lax.dynamic_update_slice_in_dim(out, mine, here * half, 0)
        return lax.dynamic_update_slice_in_dim(out, other, there * half, 0)

    def rows_of(values, index):
        return lax.dynamic_slice_in_dim(values, index * half, half, 0)

    def layer(stack):
        return select_layer(stack, layer_index)

    def after(values, earlier):
        return lax.optimization_barrier((values, earlier))[0]

    token_far = exchange(pick(tokens, here))
    x_far = joined(pick(tokens, there), token_far)
    token_own = exchange(after(pick(tokens, there), token_far))
    x_own = joined(pick(tokens, here), token_own)
    len_far = lax.dynamic_slice_in_dim(lengths, there, 1, 0)
    len_own = lax.dynamic_slice_in_dim(lengths, here, 1, 0)
    cot_own = joined(pick(cotangent, here), exchange(after(pick(cotangent, there), token_own)))

    gain_one = layer(norm_one_gain).astype(f32)[None]
    shift_one = layer(norm_one_bias).astype(f32)[None]
    gain_two = layer(norm_two_gain).astype(f32)[None]
    shift_two = layer(norm_two_bias).astype(f32)[None]
    attend_flat = layer(attend_weight).reshape(width, -1)
    local = attend_flat.shape[1] // 3
    qkv_bias = jnp.concatenate(
        [layer(query_bias).astype(f32), jnp.zeros((local,), f32), layer(value_bias).astype(f32)]
    )[None]
    out_mat = layer(output_weight)
    out_shift = layer(output_bias).astype(f32)[None]
    expand_mat = layer(expand_weight)
    expand_shift = layer(expand_bias).astype(f32)[None]
    shrink_mat = layer(shrink_weight)
    shrink_shift = layer(shrink_bias).astype(f32)[None]

    def share(matrix):
        rows = matrix.shape[0] // dp
        return lax.dynamic_slice_in_dim(matrix, place * rows, rows, 0)

    def gather(piece):
        return lax.all_gather(piece, "dp", axis=0, tiled=False)

    proj_rows = out_mat.shape[0] // dp
    first_piece = jnp.concatenate([share(out_mat), share(shrink_mat)], axis=0)
    first_got = exchange(after(first_piece, token_far))
    first_all = gather(first_got)
    out_far = first_all[:, :proj_rows].reshape(out_mat.shape)
    shrink_far = first_all[:, proj_rows:].reshape(shrink_mat.shape)
    expand_got = exchange(after(share(expand_mat), token_far))
    expand_far = gather(expand_got).reshape(expand_mat.shape)
    expand_shift_far = exchange(after(layer(expand_bias), token_far))[None].astype(f32)

    h_far, qkv_far = project(len_far, x_far, gain_one, shift_one, attend_flat, qkv_bias)
    o_far, lse_far = attend(len_far, qkv_far)
    o_got = exchange(o_far)
    h_own, qkv_own = project(len_own, x_own, gain_one, shift_one, attend_flat, qkv_bias)
    o_own, lse_own = attend(len_own, qkv_own)

    valid = (lax.broadcasted_iota(jnp.int32, (seq_len, 1), 0) < len_own[0]).astype(f32)
    attn = dot_nn(o_own, out_mat) + dot_nn(o_got, out_far) + out_shift
    resid = x_own.astype(f32) + valid * attn
    unit_two, inverse_two = norm_parts(resid)
    h_two = (valid * (unit_two * gain_two + shift_two)).astype(bf16)
    cot = cot_own.astype(f32)
    gf_wide = valid * cot
    gf = gf_wide.astype(bf16)

    f_part, gh_part, de_own, ds_own, db_own = feed(h_two, gf, expand_mat, expand_shift, shrink_mat)
    f_sum, gh_two, de_far, ds_far, db_far = feed(
        h_two, gf, expand_far, expand_shift_far, shrink_far, (f_part, gh_part)
    )
    mlp = f_sum + shrink_shift
    result = resid + valid * mlp
    result_got = exchange(rows_of(result, there).astype(bf16))

    grad_norm = valid * gh_two
    grad_resid = cot + norm_back(unit_two, inverse_two, gain_two, grad_norm)
    gain_two_grad = jnp.sum(grad_norm * unit_two, axis=0)
    shift_two_grad = jnp.sum(grad_norm, axis=0)
    grad_attn = valid * grad_resid
    ga = grad_attn.astype(bf16)
    go_send = dot_nt(ga, out_far).astype(bf16)
    go_far = exchange(go_send)
    go_own = dot_nt(ga, out_mat).astype(bf16)
    do_own = dot_tn(o_own, ga).astype(bf16)
    do_far = dot_tn(o_got, ga).astype(bf16)

    gq_own, gk_own, gv_own = attend_back(len_own, qkv_own, o_own, lse_own, go_own)

    def back_rows(gq, gk, gv, x, length):
        stacked = jnp.concatenate([gq, gk, gv], axis=1)
        inside = (lax.broadcasted_iota(jnp.int32, (seq_len, 1), 0) < length[0]).astype(f32)
        partial = inside * dot_nt(stacked, attend_flat)
        unit, inverse = norm_parts(x.astype(f32))
        return (
            stacked,
            norm_back(unit, inverse, gain_one, partial),
            jnp.sum(partial * unit, axis=0),
            jnp.sum(partial, axis=0),
        )

    stack_own, back_own, gain_own, shift_own = back_rows(gq_own, gk_own, gv_own, x_own, len_own)
    back_own = grad_resid + back_own
    in_far_got = exchange(rows_of(back_own, there).astype(bf16))

    gq_far, gk_far, gv_far = attend_back(len_far, qkv_far, o_far, lse_far, go_far)
    stack_far, back_far, gain_far, shift_far = back_rows(gq_far, gk_far, gv_far, x_far, len_far)
    in_own_got = exchange(rows_of(back_far, there).astype(bf16))
    da = (dot_tn(stack_own, h_own) + dot_tn(stack_far, h_far)).astype(bf16)

    input_own = rows_of(back_own, here) + in_own_got.astype(f32)
    input_far = rows_of(back_far, here) + in_far_got.astype(f32)

    def by_sequence(own, far):
        out = jnp.zeros((2,) + own.shape, own.dtype)
        out = lax.dynamic_update_index_in_dim(out, own, here, 0)
        return lax.dynamic_update_index_in_dim(out, far, there, 0)

    block_output = by_sequence(rows_of(result, here), result_got.astype(f32))
    input_grad = by_sequence(input_own, input_far)

    counters = jnp.stack(
        [
            jnp.sum(valid * result * result),
            jnp.sum(valid * attn * attn),
            jnp.sum(valid * mlp * mlp),
            jnp.sum(valid),
        ]
    )
    everywhere = [
        jnp.sum(grad_attn, axis=0),
        gain_two_grad,
        shift_two_grad,
        jnp.sum(gf_wide, axis=0),
        jnp.pad(counters, (0, width - counters.shape[0])),
    ]
    norm_one = jnp.stack([gain_own + gain_far, shift_own + shift_far])
    norm_one = norm_one + exchange(norm_one)
    value_grad = jnp.stack(
        [
            jnp.sum(gq_own.astype(f32), axis=0) + jnp.sum(gq_far.astype(f32), axis=0),
            jnp.sum(gv_own.astype(f32), axis=0) + jnp.sum(gv_far.astype(f32), axis=0),
        ]
    )

    def small_rows(rows, used):
        rows = jnp.concatenate(rows, axis=0).astype(bf16)
        return jnp.pad(rows, ((0, padded(used, dp) - used - rows.shape[0]), (0, 0)))

    everywhere = jnp.stack(everywhere)
    used = expand_mat.shape[1] + shrink_mat.shape[0] + out_mat.shape[0]
    more_own = small_rows([everywhere, db_own.reshape(-1, width)], used)
    more_far = small_rows([everywhere, db_far.reshape(-1, width)], used)
    more_query = small_rows([norm_one, value_grad.reshape(-1, width)], da.shape[0])
    feed_sum, query_sum = reduce_all(
        (de_far, ds_far, do_far, more_far),
        (de_own, ds_own, do_own, more_own),
        (da, more_query),
        dp,
    )
    hidden = expand_mat.shape[1]
    expand_grad = feed_sum[:hidden].astype(f32).T
    shrink_grad = feed_sum[hidden : 2 * hidden].astype(f32)
    out_grad = feed_sum[2 * hidden : used].astype(f32)
    small = feed_sum[used : used + 16].astype(f32)
    attend_grad = query_sum[: da.shape[0]].astype(f32).T.reshape(width, 3, local)
    last = query_sum[da.shape[0] : da.shape[0] + 16].astype(f32)
    rms_values = jnp.sqrt(small[4, :3] / (small[4, 3] * width))
    count = hidden // width
    biases = last[2:3].reshape(2, local)
    return (
        block_output,
        input_grad,
        last[0],
        last[1],
        attend_grad,
        biases[0],
        biases[1],
        out_grad,
        small[0],
        small[1],
        small[2],
        expand_grad,
        small[5 : 5 + count].reshape(hidden),
        shrink_grad,
        small[3],
        rms_values,
    )


def solution(mesh):
    in_specs = (
        P("dp", "tensor", None),
        P("dp"),
        P(),
        P(),
        P(),
        P(None, None, None, "tensor"),
        P(None, "tensor"),
        P(None, "tensor"),
        P(None, "tensor", None),
        P(),
        P(),
        P(),
        P(None, None, "tensor"),
        P(None, "tensor"),
        P(None, "tensor", None),
        P(),
        P("dp", "tensor", None),
    )
    out_specs = (
        P("dp", "tensor", None),
        P("dp", "tensor", None),
        P(),
        P(),
        P(None, None, "tensor"),
        P("tensor"),
        P("tensor"),
        P("tensor", None),
        P(),
        P(),
        P(),
        P(None, "tensor"),
        P("tensor"),
        P("tensor", None),
        P(),
        P(),
    )
    return jax.shard_map(body, mesh=mesh, in_specs=in_specs, out_specs=out_specs, check_vma=False)
```

```python
import functools

import jax
import jax.numpy as jnp
from jax import lax
from jax.experimental import pallas as pl
from jax.experimental.pallas import tpu as pltpu
from jax.sharding import PartitionSpec as P

HD = 64
PAIR = 2 * HD
epsilon = 1e-05
masked_fill = -1e30
VMEM_LIMIT = 56 * 1024 * 1024
f32 = jnp.float32
bf16 = jnp.bfloat16


def dot_nn(left, right):
    return lax.dot_general(left, right, (((1,), (0,)), ((), ())), preferred_element_type=f32)


def dot_nt(left, right):
    return lax.dot_general(left, right, (((1,), (1,)), ((), ())), preferred_element_type=f32)


def dot_tn(left, right):
    return lax.dot_general(left, right, (((0,), (0,)), ((), ())), preferred_element_type=f32)


def select_layer(stack, layer_index):
    return lax.dynamic_index_in_dim(stack, layer_index[0], 0, keepdims=False)


def whole(shape):
    return pl.BlockSpec(shape, lambda *index: (0,) * len(shape))


def params():
    return pltpu.CompilerParams(dimension_semantics=("arbitrary",), vmem_limit_bytes=VMEM_LIMIT)


def remote_params(number):
    return pltpu.CompilerParams(
        collective_id=number, has_side_effects=True, vmem_limit_bytes=VMEM_LIMIT
    )


def cost(microseconds):
    return pl.CostEstimate(
        flops=int(microseconds * 1e9), bytes_accessed=int(microseconds * 3e6), transcendentals=0
    )


def normalized(x):
    center = jnp.mean(x, axis=-1, keepdims=True)
    x = x - center
    inverse = lax.rsqrt(jnp.mean(x * x, axis=-1, keepdims=True) + epsilon)
    return x * inverse, inverse


def norm_back(unit, inverse, gain, grad):
    scaled = grad * gain
    return inverse * (
        scaled
        - jnp.mean(scaled, axis=-1, keepdims=True)
        - unit * jnp.mean(scaled * unit, axis=-1, keepdims=True)
    )


class Halves:
    def __init__(self, half, block):
        self.count = half // block
        self.block = block

    def mine(self, i, at):
        return jnp.minimum(i, self.count - 1), 0

    def got(self, i, at):
        return jnp.maximum(i - self.count, 0), 0

    def whole(self, i, at):
        first = i < self.count
        side = jnp.where(first, at[0], 1 - at[0])
        return side * self.count + jnp.where(first, i, i - self.count), 0

    def position(self, at):
        i = pl.program_id(0)
        return self.whole(i, at)[0] * self.block + lax.broadcasted_iota(
            jnp.int32, (self.block, 1), 0
        )

    def pick(self, mine, got):
        return jnp.where(pl.program_id(0) < self.count, mine[...], got[...]).astype(f32)

    def specs(self, width, kind):
        return pl.BlockSpec((self.block, width), getattr(self, kind))


def fixed(shape):
    return pl.BlockSpec(shape, lambda i, at: (0,) * len(shape))


def project_kernel(at, mine, got, gain_ref, shift_ref, weight_ref, bias_ref, h_ref, qkv_ref, *, halves):
    unit, _ = normalized(halves.pick(mine, got))
    h = unit * gain_ref[...] + shift_ref[...]
    h = jnp.where(halves.position(at) < at[1], h, 0.0).astype(bf16)
    h_ref[...] = h
    qkv_ref[...] = (dot_nn(h, weight_ref[...]) + bias_ref[...]).astype(bf16)


def project(at, mine, got, gain, shift, weight, bias):
    half, width = mine.shape
    columns = weight.shape[1]
    halves = Halves(half, min(256, half))
    return pl.pallas_call(
        functools.partial(project_kernel, halves=halves),
        grid_spec=pltpu.PrefetchScalarGridSpec(
            num_scalar_prefetch=1,
            grid=(2 * halves.count,),
            in_specs=[
                halves.specs(width, "mine"),
                halves.specs(width, "got"),
                fixed((1, width)),
                fixed((1, width)),
                fixed((width, columns)),
                fixed((1, columns)),
            ],
            out_specs=[halves.specs(width, "whole"), halves.specs(columns, "whole")],
        ),
        out_shape=[
            jax.ShapeDtypeStruct((2 * half, width), bf16),
            jax.ShapeDtypeStruct((2 * half, columns), bf16),
        ],
        compiler_params=params(),
        cost_estimate=cost(7),
        name="project",
    )(at, mine, got, gain, shift, weight, bias)


def lane_index(rows):
    return lax.broadcasted_iota(jnp.int32, (rows, PAIR), 1)


def causal_block(block):
    row = lax.broadcasted_iota(jnp.int32, (block, block), 0)
    column = lax.broadcasted_iota(jnp.int32, (block, block), 1)
    return row, column


def attend_kernel(length_ref, q_ref, k_ref, v_ref, o_ref, lse_ref, *, block):
    seq_len = q_ref.shape[0]
    lane = lane_index(seq_len)
    position = lax.broadcasted_iota(jnp.int32, (seq_len, PAIR), 0)
    key_bias = jnp.where(position < length_ref[0], 0.0, masked_fill)
    row, column = causal_block(block)
    keep = column <= row
    q = q_ref[...].astype(f32) * (HD**-0.5)
    k = k_ref[...].astype(f32)
    values = v_ref[...]
    low = lane < HD
    outs = []
    stats = []
    for head in range(2):
        mine = low if head == 0 else jnp.logical_not(low)
        spare = HD if head == 0 else 0
        q_aug = jnp.where(mine, q, jnp.where(lane == spare, 1.0, 0.0)).astype(bf16)
        k_aug = jnp.where(mine, k, jnp.where(lane == spare, key_bias, 0.0)).astype(bf16)
        v_own = jnp.where(mine, values, jnp.zeros_like(values))
        pieces = []
        notes = []
        for index in range(seq_len // block):
            start, end = index * block, (index + 1) * block
            scores = dot_nt(q_aug[start:end], k_aug[:end])
            last = jnp.where(keep, scores[:, start:end], masked_fill)
            if index:
                scores = jnp.concatenate([scores[:, :start], last], axis=1)
            else:
                scores = last
            top = jnp.max(scores, axis=-1, keepdims=True)
            weights = jnp.exp(scores - top)
            total = jnp.sum(weights, axis=-1, keepdims=True)
            mixed = dot_nn(weights.astype(bf16), v_own[:end])
            pieces.append(mixed * (1.0 / total))
            notes.append(jnp.broadcast_to(top + jnp.log(total), (block, PAIR)))
        outs.append(jnp.concatenate(pieces, axis=0))
        stats.append(jnp.concatenate(notes, axis=0))
    o_ref[...] = (outs[0] + outs[1]).astype(bf16)
    lse_ref[...] = jnp.where(low, stats[1], stats[0])


def attend(length, qkv):
    seq_len = qkv.shape[0]
    width = qkv.shape[1] // 3
    pairs = width // PAIR
    block = min(256, seq_len)

    def columns(part):
        return pl.BlockSpec((seq_len, PAIR), lambda i: (0, part * pairs + i))

    return pl.pallas_call(
        functools.partial(attend_kernel, block=block),
        grid=(pairs,),
        in_specs=[pl.BlockSpec(memory_space=pltpu.SMEM), columns(0), columns(1), columns(2)],
        out_specs=[columns(0), columns(0)],
        out_shape=[
            jax.ShapeDtypeStruct((seq_len, width), bf16),
            jax.ShapeDtypeStruct((seq_len, width), f32),
        ],
        compiler_params=params(),
        cost_estimate=cost(13),
        name="attend",
    )(length, qkv, qkv, qkv)


def three_parts(values):
    first = values.astype(bf16).astype(f32)
    rest = values - first
    second = rest.astype(bf16).astype(f32)
    return first, second, rest - second


def resid_kernel(
    at, mine, got, cot_mine, cot_got, o_ref, o_got, w_ref, w_far, shift_out, gain, shift,
    h_ref, gf_ref, resid_ref, sums_ref, *, halves
):
    valid = (halves.position(at) < at[1]).astype(f32)
    attn = dot_nn(o_ref[...], w_ref[...]) + dot_nn(o_got[...], w_far[...]) + shift_out[...]
    resid = halves.pick(mine, got) + valid * attn
    resid_ref[...] = resid
    unit, _ = normalized(resid)
    h_ref[...] = (valid * (unit * gain[...] + shift[...])).astype(bf16)
    gf = valid * halves.pick(cot_mine, cot_got)
    gf_ref[...] = gf.astype(bf16)

    @pl.when(pl.program_id(0) == 0)
    def _():
        sums_ref[...] = jnp.zeros_like(sums_ref)

    sums_ref[0:1] += jnp.sum(valid * attn * attn, axis=0, keepdims=True)
    sums_ref[1:2] += jnp.sum(gf, axis=0, keepdims=True)


def resid_norm(at, mine, got, cot_mine, cot_got, o, o_got, w, w_far, shift_out, gain, shift):
    half, width = mine.shape
    local = o.shape[1]
    halves = Halves(half, min(256, half))
    return pl.pallas_call(
        functools.partial(resid_kernel, halves=halves),
        grid_spec=pltpu.PrefetchScalarGridSpec(
            num_scalar_prefetch=1,
            grid=(2 * halves.count,),
            in_specs=[
                halves.specs(width, "mine"),
                halves.specs(width, "got"),
                halves.specs(width, "mine"),
                halves.specs(width, "got"),
                halves.specs(local, "whole"),
                halves.specs(local, "whole"),
                fixed((local, width)),
                fixed((local, width)),
                fixed((1, width)),
                fixed((1, width)),
                fixed((1, width)),
            ],
            out_specs=[halves.specs(width, "whole")] * 3 + [fixed((8, width))],
        ),
        out_shape=[
            jax.ShapeDtypeStruct((2 * half, width), bf16),
            jax.ShapeDtypeStruct((2 * half, width), bf16),
            jax.ShapeDtypeStruct((2 * half, width), f32),
            jax.ShapeDtypeStruct((8, width), f32),
        ],
        compiler_params=params(),
        cost_estimate=cost(6),
        name="resid_norm",
    )(at, mine, got, cot_mine, cot_got, o, o_got, w, w_far, shift_out, gain, shift)


def turn_kernel(
    at, cot_mine, cot_got, resid_ref, f_ref, gh_ref, o_ref, o_got, w_ref, w_far, shift_mlp, gain,
    sums_in, db_own, db_far, result_ref, grad_ref, go_ref, go_send, own_ref, far_ref,
    own_acc, far_acc, sums, *, halves
):
    valid = (halves.position(at) < at[1]).astype(f32)
    resid = resid_ref[...]
    mlp = f_ref[...] + shift_mlp[...]
    result = resid + valid * mlp
    result_ref[...] = result
    unit, inverse = normalized(resid)
    grad_norm = valid * gh_ref[...]
    grad = halves.pick(cot_mine, cot_got) + norm_back(unit, inverse, gain[...], grad_norm)
    grad_ref[...] = grad
    grad_attn = valid * grad
    ga = grad_attn.astype(bf16)
    go_send[...] = dot_nt(ga, w_far[...]).astype(bf16)
    go_ref[...] = dot_nt(ga, w_ref[...]).astype(bf16)

    @pl.when(pl.program_id(0) == 0)
    def _():
        own_acc[...] = jnp.zeros_like(own_acc)
        far_acc[...] = jnp.zeros_like(far_acc)
        sums[...] = jnp.zeros_like(sums)

    own_acc[...] += dot_tn(o_ref[...], ga)
    far_acc[...] += dot_tn(o_got[...], ga)

    def add(row, values):
        sums[row : row + 1] += jnp.sum(values, axis=0, keepdims=True)

    add(0, grad_attn)
    add(1, grad_norm * unit)
    add(2, grad_norm)
    add(4, valid * result * result)
    add(6, valid * mlp * mlp)

    @pl.when(pl.program_id(0) == 2 * halves.count - 1)
    def _():
        width = sums.shape[1]
        lane = lax.broadcasted_iota(jnp.int32, (1, width), 1)
        seq_len = 2 * halves.count * halves.block
        tokens = jnp.zeros((1, width), f32)
        for start in range(0, seq_len, width):
            tokens += (lane + start < at[1]).astype(f32)
        sums[3:4] = sums_in[1:2]
        sums[5:6] = sums_in[0:1]
        sums[7:8] = tokens
        rows = own_acc.shape[0]
        for out, acc, db in ((own_ref, own_acc, db_own), (far_ref, far_acc, db_far)):
            out[:rows] = acc[...].astype(bf16)
            out[rows : rows + 16] = jnp.concatenate([sums[0:8], db[...]], axis=0).astype(bf16)
            out[rows + 16 :] = jnp.zeros((out.shape[0] - rows - 16, width), bf16)


def turn(
    at, cot_mine, cot_got, resid, f_sum, gh, o, o_got, w, w_far, shift, gain, sums, db_own, db_far, rows
):
    half, width = cot_mine.shape
    local = o.shape[1]
    halves = Halves(half, min(256, half))
    return pl.pallas_call(
        functools.partial(turn_kernel, halves=halves),
        grid_spec=pltpu.PrefetchScalarGridSpec(
            num_scalar_prefetch=1,
            grid=(2 * halves.count,),
            in_specs=[
                halves.specs(width, "mine"),
                halves.specs(width, "got"),
                halves.specs(width, "whole"),
                halves.specs(width, "whole"),
                halves.specs(width, "whole"),
                halves.specs(local, "whole"),
                halves.specs(local, "whole"),
                fixed((local, width)),
                fixed((local, width)),
                fixed((1, width)),
                fixed((1, width)),
                fixed((8, width)),
                fixed((8, width)),
                fixed((8, width)),
            ],
            out_specs=[halves.specs(width, "whole")] * 2
            + [halves.specs(local, "whole")] * 2
            + [fixed((rows, width))] * 2,
            scratch_shapes=[
                pltpu.VMEM((local, width), f32),
                pltpu.VMEM((local, width), f32),
                pltpu.VMEM((8, width), f32),
            ],
        ),
        out_shape=[
            jax.ShapeDtypeStruct((2 * half, width), f32),
            jax.ShapeDtypeStruct((2 * half, width), f32),
            jax.ShapeDtypeStruct((2 * half, local), bf16),
            jax.ShapeDtypeStruct((2 * half, local), bf16),
            jax.ShapeDtypeStruct((rows, width), bf16),
            jax.ShapeDtypeStruct((rows, width), bf16),
        ],
        compiler_params=params(),
        cost_estimate=cost(9),
        name="turn",
    )(at, cot_mine, cot_got, resid, f_sum, gh, o, o_got, w, w_far, shift, gain, sums, db_own, db_far)


class Ring:
    def __init__(self, dp):
        self.chips = dp // 2
        self.far_hops = self.chips // 2
        self.near_hops = self.chips - 1 - self.far_hops
        place = lax.axis_index("dp")
        self.tensor = lax.axis_index("tensor")
        self.base = place // dp * dp
        place = place % dp
        self.core = place % 2
        chip = place // 2
        depth = chip // 2
        self.spot = depth + (chip % 2) * (self.chips - 1 - 2 * depth)
        self.turn = 1 - 2 * self.core

    def device(self, spot, core):
        spot = (spot + self.chips) % self.chips
        side = spot // (self.chips // 2)
        chip = 2 * (spot + side * (self.chips - 1 - 2 * spot)) + side
        return (self.base + chip * 2 + core, self.tensor)

    def ahead(self):
        return self.device(self.spot + self.turn, self.core)

    def behind(self):
        return self.device(self.spot - self.turn, self.core)

    def sibling(self):
        return self.device(self.spot, 1 - self.core)

    def partner(self):
        return (lax.axis_index("dp"), 1 - self.tensor)

    def chunk(self, offset):
        return (self.spot + self.turn * offset + 2 * self.chips) % self.chips


def send(source, target, sems, index, device):
    copy = pltpu.make_async_remote_copy(
        src_ref=source,
        dst_ref=target,
        send_sem=sems.at[0, index],
        recv_sem=sems.at[1, index],
        device_id=device,
        device_id_type=pl.DeviceIdType.MESH,
    )
    return copy


def loop(start, stop, step):
    def run(index, carry):
        step(index)
        return carry

    lax.fori_loop(start, stop, run, 0)


class Group:
    def __init__(self, ring, source, acc, scratch):
        self.ring = ring
        self.source = source
        self.acc = acc
        self.pair, self.slots, self.pair_sems, self.ring_sems, self.load_sem = scratch
        self.rows = source.shape[0] // (2 * ring.chips)

    @staticmethod
    def scratch(rows, width, dp):
        chips = dp // 2
        size = rows // (2 * chips)
        return [
            pltpu.VMEM((chips, size, width), bf16),
            pltpu.VMEM((chips - 1, size, width), bf16),
            pltpu.SemaphoreType.DMA((2, chips)),
            pltpu.SemaphoreType.DMA((2, chips - 1)),
            pltpu.SemaphoreType.DMA((1,)),
        ]

    def place(self, core, chunk):
        start = (core * self.ring.chips + chunk) * self.rows
        return pl.ds(pl.multiple_of(start, 16), self.rows)

    def mine(self, chunk):
        if self.acc is None:
            return self.source.at[self.place(self.ring.core, chunk)]
        return self.acc.at[pl.ds(pl.multiple_of(chunk * self.rows, 16), self.rows)]

    def load(self):
        count = self.rows * self.ring.chips
        start = pl.multiple_of(self.ring.core * count, 16)
        return pltpu.make_async_copy(
            self.source.at[pl.ds(start, count)], self.acc, self.load_sem.at[0]
        )

    def to_sibling(self, chunk):
        source = self.source.at[self.place(1 - self.ring.core, chunk)]
        return send(source, self.pair.at[chunk], self.pair_sems, chunk, self.ring.sibling())

    def hand_over(self):
        ring = self.ring

        def both(step):
            self.to_sibling(ring.chunk(step - ring.far_hops)).start()
            self.to_sibling(ring.chunk(ring.near_hops - step)).start()

        loop(0, ring.near_hops, both)
        self.to_sibling(ring.chunk(-1)).start()
        self.to_sibling(ring.chunk(0)).start()

    def term(self, chunk):
        self.to_sibling(chunk).wait_recv()
        return self.mine(chunk)[...].astype(f32) + self.pair[chunk].astype(f32)

    def far_copy(self, step):
        chunk = self.ring.chunk(self.ring.far_hops - step)
        return send(
            self.mine(chunk), self.slots.at[step], self.ring_sems, step, self.ring.ahead()
        )

    def near_copy(self, step):
        slot = self.ring.far_hops + step
        chunk = self.ring.chunk(step - self.ring.near_hops)
        return send(
            self.mine(chunk), self.slots.at[slot], self.ring_sems, slot, self.ring.behind()
        )

    def far_step(self, step, first=False):
        chunk = self.ring.chunk(self.ring.far_hops - step)
        value = self.term(chunk)
        if not first:
            self.far_copy(step - 1).wait_recv()
            value += self.slots[step - 1].astype(f32)
        self.mine(chunk)[...] = value.astype(bf16)
        self.far_copy(step).start()

    def near_step(self, step, first=False):
        slot = self.ring.far_hops + step
        chunk = self.ring.chunk(step - self.ring.near_hops)
        value = self.term(chunk)
        if not first:
            self.near_copy(step - 1).wait_recv()
            value += self.slots[slot - 1].astype(f32)
        self.mine(chunk)[...] = value.astype(bf16)
        self.near_copy(step).start()

    def both_steps(self, step, first=False):
        self.far_step(step, first)
        self.near_step(step, first)

    def finish(self):
        ring = self.ring
        value = self.term(ring.chunk(0))
        self.far_copy(ring.far_hops - 1).wait_recv()
        self.near_copy(ring.near_hops - 1).wait_recv()
        value += self.slots[ring.far_hops - 1].astype(f32)
        return value + self.slots[ring.chips - 2].astype(f32)

    def sent(self):
        ring = self.ring
        loop(0, ring.chips, lambda chunk: self.to_sibling(chunk).wait_send())
        loop(0, ring.far_hops, lambda step: self.far_copy(step).wait_send())
        loop(0, ring.near_hops, lambda step: self.near_copy(step).wait_send())


class Spread:
    def __init__(self, ring, out, scratch):
        self.ring = ring
        self.out = out
        self.pair_sems, self.ring_sems = scratch
        self.rows = out.shape[0] // (2 * ring.chips)

    @staticmethod
    def scratch(dp):
        chips = dp // 2
        return [pltpu.SemaphoreType.DMA((2, chips)), pltpu.SemaphoreType.DMA((2, chips))]

    def place(self, core, chunk):
        start = (core * self.ring.chips + chunk) * self.rows
        return pl.ds(pl.multiple_of(start, 16), self.rows)

    def pass_on(self, chunk, slot, device):
        where = self.out.at[self.place(self.ring.core, chunk)]
        return send(where, where, self.ring_sems, slot, device)

    def to_sibling(self, chunk):
        where = self.out.at[self.place(self.ring.core, chunk)]
        return send(where, where, self.pair_sems, chunk, self.ring.sibling())

    def from_sibling(self, chunk):
        where = self.out.at[self.place(1 - self.ring.core, chunk)]
        return send(where, where, self.pair_sems, chunk, self.ring.sibling())

    def far_copy(self, step):
        return self.pass_on(self.ring.chunk(-step), step, self.ring.ahead())

    def near_copy(self, step):
        return self.pass_on(self.ring.chunk(step), self.ring.far_hops + step, self.ring.behind())

    def far_landed(self, step):
        return self.pass_on(self.ring.chunk(-step - 1), step, self.ring.ahead())

    def near_landed(self, step):
        return self.pass_on(
            self.ring.chunk(step + 1), self.ring.far_hops + step, self.ring.behind()
        )

    def begin(self):
        self.far_copy(0).start()
        self.near_copy(0).start()
        self.to_sibling(self.ring.chunk(0)).start()

    def far_step(self, step, last=False):
        self.far_landed(step - 1).wait_recv()
        if not last:
            self.far_copy(step).start()
        self.to_sibling(self.ring.chunk(-step)).start()

    def near_step(self, step, last=False):
        self.near_landed(step - 1).wait_recv()
        if not last:
            self.near_copy(step).start()
        self.to_sibling(self.ring.chunk(step)).start()

    def both_steps(self, step):
        self.far_step(step)
        self.near_step(step)

    def close(self):
        self.far_step(self.ring.near_hops)
        self.near_step(self.ring.near_hops, last=True)

    def sent(self):
        ring = self.ring
        loop(0, ring.chips, lambda chunk: self.from_sibling(chunk).wait_recv())
        loop(0, ring.chips, lambda chunk: self.to_sibling(chunk).wait_send())
        loop(0, ring.far_hops, lambda step: self.far_copy(step).wait_send())
        loop(0, ring.near_hops, lambda step: self.near_copy(step).wait_send())


def greet(*devices):
    barrier = pltpu.get_barrier_semaphore()
    for device in devices:
        pl.semaphore_signal(barrier, inc=1, device_id=device, device_id_type=pl.DeviceIdType.MESH)
    pl.semaphore_wait(barrier, len(devices))


def padded(rows, dp):
    unit = 16 * dp
    return -(-rows // unit) * unit


def feed_kernel(h_ref, gf_ref, e_ref, b_ref, s_ref, *rest, chunk, dp):
    rest = list(rest)

    def take(count):
        taken = rest[:count]
        del rest[:count]
        return taken

    if dp:
        f_in, gh_in, source = take(3)
    f_ref, gh_ref, grad_ref, db_ref = take(4)
    if dp:
        (shard,) = take(1)
    act_ref, gu_ref = take(2)
    seq_len = h_ref.shape[0]
    tile = e_ref.shape[1]
    root = 0.7978845608
    cube = 0.044715
    step = pl.program_id(0)
    steps = pl.num_programs(0)
    parts = seq_len // chunk
    if dp:
        ring = Ring(dp)
        group = Group(ring, source, rest[0], rest[1:6])

    @pl.when(step == 0)
    def _():
        if dp:
            f_ref[...] = f_in[...]
            gh_ref[...] = gh_in[...]
            group.load().start()
            greet(ring.ahead(), ring.behind(), ring.sibling())
            group.hand_over()
            group.load().wait()
        else:
            f_ref[...] = jnp.zeros_like(f_ref)
            gh_ref[...] = jnp.zeros_like(gh_ref)

    e = e_ref[...]
    s = s_ref[...]
    bias = b_ref[...]
    total = jnp.zeros((1, tile), f32)
    for index in range(parts):
        rows = pl.ds(index * chunk, chunk)
        u = dot_nn(h_ref[rows, :], e) + bias
        ga = dot_nt(gf_ref[rows, :], s)
        square = u * u
        bent = jnp.tanh(u * (root + (root * cube) * square))
        half = 0.5 + 0.5 * bent
        act = (u * half).astype(bf16)
        slope = half + (0.5 * u) * (1.0 - bent * bent) * (root + (3.0 * root * cube) * square)
        gu_wide = (slope * ga).astype(bf16)
        act_ref[rows, :] = act
        gu_ref[rows, :] = gu_wide
        total += jnp.sum(gu_wide.astype(f32), axis=0, keepdims=True)
        f_ref[rows, :] += dot_nn(act, s)
        gh_ref[rows, :] += dot_nt(gu_wide, e)
    db_ref[...] = total
    grad_ref[0] = dot_tn(gu_ref[...], h_ref[...]).astype(bf16)
    if dp:
        ring_steps(group, step, steps)
    grad_ref[1] = dot_tn(act_ref[...], gf_ref[...]).astype(bf16)

    if dp:

        @pl.when(step == steps - 1)
        def _():
            shard[...] = group.finish()
            group.sent()


def ring_steps(group, step, steps):
    ring = group.ring

    @pl.when(step == 0)
    def _():
        group.both_steps(0, first=True)

    @pl.when(step == steps - 1)
    def _():
        loop(1, ring.near_hops, group.both_steps)
        group.far_step(ring.far_hops - 1)


def feed(h, gf, expand, bias, shrink, rows, carry=None, dp=0):
    seq_len, width = h.shape
    hidden = expand.shape[1]
    tile = min(512, hidden)
    chunk = min(256, seq_len)
    whole_rows = whole((seq_len, width))
    row_shape = jax.ShapeDtypeStruct((seq_len, width), f32)
    in_specs = [
        whole_rows,
        whole_rows,
        pl.BlockSpec((width, tile), lambda i: (0, i)),
        pl.BlockSpec((1, tile), lambda i: (0, i)),
        pl.BlockSpec((tile, width), lambda i: (i, 0)),
    ]
    out_specs = [
        whole_rows,
        whole_rows,
        pl.BlockSpec((2, tile, width), lambda i: (0, i, 0)),
        pl.BlockSpec((1, tile), lambda i: (0, i)),
    ]
    out_shape = [
        row_shape,
        row_shape,
        jax.ShapeDtypeStruct((2, rows // 2, width), bf16),
        jax.ShapeDtypeStruct((1, hidden), f32),
    ]
    scratch = [pltpu.VMEM((seq_len, tile), bf16), pltpu.VMEM((seq_len, tile), bf16)]
    extra = ()
    if dp:
        extra = carry
        in_specs += [whole_rows, whole_rows, pl.BlockSpec(memory_space=pl.ANY)]
        out_specs += [whole((rows // dp, width))]
        out_shape += [jax.ShapeDtypeStruct((rows // dp, width), f32)]
        scratch += [pltpu.VMEM((rows // 2, width), bf16)] + Group.scratch(rows, width, dp)
    return pl.pallas_call(
        functools.partial(feed_kernel, chunk=chunk, dp=dp),
        grid=(hidden // tile,),
        in_specs=in_specs,
        out_specs=out_specs,
        out_shape=out_shape,
        scratch_shapes=scratch,
        compiler_params=remote_params(1) if dp else params(),
        cost_estimate=cost(22),
        name="feed_sum" if dp else "feed",
    )(h, gf, expand, bias, shrink, *extra)


def three_parts(values):
    first = values.astype(bf16).astype(f32)
    rest = values - first
    second = rest.astype(bf16).astype(f32)
    return first, second, rest - second


def attend_back(length, qkv, o, lse, go, acc_ref, seq, pair, local, block, between):
    seq_len = qkv.shape[1]
    scale = HD**-0.5

    def columns(part):
        return pl.ds(pl.multiple_of(part * local + pair * PAIR, PAIR), PAIR)

    lane = lane_index(seq_len)
    position = lax.broadcasted_iota(jnp.int32, (seq_len, PAIR), 0)
    inside = position < length
    key_bias = jnp.where(inside, 0.0, masked_fill)
    row, column = causal_block(block)
    keep = row <= column
    q = qkv[seq, :, columns(0)]
    k = qkv[seq, :, columns(1)]
    v = qkv[seq, :, columns(2)]
    grad_o = go[seq, :, columns(0)]
    q_wide = q.astype(f32) * scale
    k_wide = k.astype(f32)
    v_wide = v.astype(f32)
    go_wide = grad_o.astype(f32)
    both = go_wide * o[:, columns(0)].astype(f32)
    lse_parts = three_parts(-lse[:, columns(0)])
    low = lane < HD
    zero = jnp.zeros_like(q)
    acc_ref[...] = jnp.zeros_like(acc_ref)
    count = seq_len // block
    grads_k = [None] * count
    grads_v = [None] * count
    for head in range(2):
        mine = low if head == 0 else jnp.logical_not(low)
        spare = HD if head == 0 else 0
        delta = jnp.sum(jnp.where(mine, both, 0.0), axis=-1, keepdims=True)
        delta_parts = three_parts(-jnp.broadcast_to(delta, (seq_len, PAIR)))

        def extras(parts):
            return jnp.where(
                lane == spare + 1,
                parts[0],
                jnp.where(lane == spare + 2, parts[1], jnp.where(lane == spare + 3, parts[2], 0.0)),
            )

        ones = jnp.where((lane > spare) & (lane < spare + 4), 1.0, 0.0)
        q_aug = jnp.where(mine, q_wide, jnp.where(lane == spare, 1.0, extras(lse_parts))).astype(bf16)
        k_aug = jnp.where(mine, k_wide, jnp.where(lane == spare, key_bias, ones)).astype(bf16)
        v_aug = jnp.where(mine, v_wide, ones).astype(bf16)
        go_aug = jnp.where(mine, go_wide, extras(delta_parts)).astype(bf16)
        q_own = jnp.where(mine, q, zero)
        k_own = jnp.where(mine, k, zero)
        go_own = jnp.where(mine, grad_o, zero)
        for index in range(count):
            start, end = index * block, (index + 1) * block
            scores = dot_nt(k_aug[start:end], q_aug[start:])
            first = jnp.where(keep, scores[:, :block], masked_fill)
            if index + 1 < count:
                scores = jnp.concatenate([first, scores[:, block:]], axis=1)
            else:
                scores = first
            shares = jnp.exp(scores)
            moved = dot_nt(v_aug[start:end], go_aug[start:])
            grad_scores = (shares * moved).astype(bf16)
            grad_v = dot_nn(shares.astype(bf16), go_own[start:])
            grad_k = dot_nn(grad_scores, q_own[start:])
            grads_v[index] = grad_v if head == 0 else grads_v[index] + grad_v
            grads_k[index] = grad_k if head == 0 else grads_k[index] + grad_k
            acc_ref[start:, :] += dot_tn(grad_scores, k_own[start:end])
        between(head)
    qkv[seq, :, columns(0)] = (acc_ref[...] * scale).astype(bf16)
    qkv[seq, :, columns(1)] = (jnp.concatenate(grads_k, axis=0) * scale).astype(bf16)
    qkv[seq, :, columns(2)] = jnp.where(inside, jnp.concatenate(grads_v, axis=0), 0.0).astype(bf16)


def back_kernel(
    len_ref, tokens, token_own, token_far, qkv_own, qkv_far, o_own, o_far, lse_own, lse_far,
    go_own, go_send, h_own, h_far, grad_in, weight, gain_ref, feed_far, feed_own, more_far, more_own,
    feed_out, more_out, query_out, input_out,
    load_sems, y_sems, qkv, o, lse, go, x, h, w, acc_ref, sums, sums_got,
    row_send, row_got, feed_own_shard, feed_shard, feed_got, more_shard, more_got,
    feed_acc, more_far_acc, more_own_acc, query_local, *rest, dp
):
    rest = list(rest)

    def take(count):
        taken = rest[:count]
        del rest[:count]
        return taken

    half, width = token_own.shape
    seq_len = 2 * half
    local = qkv.shape[2] // 3
    pairs = local // PAIR
    block = min(256, half)
    ring = Ring(dp)
    here = ring.tensor
    there = 1 - here
    feed_group = Group(ring, feed_far, feed_acc, take(5))
    more_far_group = Group(ring, more_far, more_far_acc, take(5))
    more_own_group = Group(ring, more_own, more_own_acc, take(5))
    query_group = Group(ring, query_local, None, take(5))
    feed_spread = Spread(ring, feed_out, take(2))
    more_spread = Spread(ring, more_out, take(2))
    query_spread = Spread(ring, query_out, take(2))
    groups = (feed_group, more_far_group, more_own_group)

    def load(source, target, number):
        return pltpu.make_async_copy(source, target, load_sems.at[number])

    rows_here = pl.ds(pl.multiple_of(here * half, 16), half)
    rows_there = pl.ds(pl.multiple_of(there * half, 16), half)
    first_loads = [
        load(qkv_own, qkv.at[0], 0),
        load(o_own, o, 1),
        load(lse_own, lse, 2),
        load(go_own, go.at[0], 3),
    ]
    later_loads = [
        load(weight, w, 4),
        load(tokens.at[here], x.at[rows_here], 5),
        load(token_own, x.at[rows_there], 6),
        load(grad_in.at[rows_here], input_out.at[here], 7),
        load(grad_in.at[rows_there], input_out.at[there], 11),
    ]
    spare_loads = [
        load(qkv_far, qkv.at[1], 8),
        load(h_own, h.at[0], 13),
        load(h_far, h.at[1], 14),
    ]
    shard_load = load(feed_own, feed_own_shard, 15)
    far_loads = [load(o_far, o, 9), load(lse_far, lse, 10)]
    far_rows = [
        load(tokens.at[there], x.at[rows_here], 16),
        load(token_far, x.at[rows_there], 12),
    ]

    def cross(source, target, number):
        return send(source, target, y_sems, number, ring.partner())

    go_cross = cross(go_send, go.at[1], 0)
    feed_cross = cross(feed_shard, feed_got, 1)
    more_cross = cross(more_shard, more_got, 2)
    own_cross = cross(row_send.at[0], row_got.at[0], 3)
    far_cross = cross(row_send.at[1], row_got.at[1], 4)
    sums_cross = cross(sums, sums_got, 5)

    for group in groups:
        group.load().start()
    for copy in first_loads + later_loads + spare_loads + [shard_load]:
        copy.start()
    greet(ring.ahead(), ring.behind(), ring.sibling(), ring.partner())
    for group in groups:
        group.hand_over()
    go_cross.start()
    sums[...] = jnp.zeros_like(sums)

    def turn_rows(seq, copy):
        def one(index):
            rows = pl.ds(pl.multiple_of(index * block, 16), block)
            position = index * block + lax.broadcasted_iota(jnp.int32, (block, 1), 0)
            partial = dot_nt(qkv[seq, rows, :], w[...])
            partial = jnp.where(position < len_ref[seq], partial, 0.0)
            unit, inverse = normalized(x[rows, :].astype(f32))
            value = norm_back(unit, inverse, gain_ref[...], partial)
            sums[0:1] += jnp.sum(partial * unit, axis=0, keepdims=True)
            sums[1:2] += jnp.sum(partial, axis=0, keepdims=True)
            return value

        count = half // block

        def send_rows(index):
            rows = pl.ds(pl.multiple_of(index * block, 16), block)
            value = one(there * count + index)
            if seq == 0:
                value += input_out[there, rows, :]
            row_send[seq, rows, :] = value.astype(bf16)

        def keep_rows(index):
            rows = pl.ds(pl.multiple_of(index * block, 16), block)
            value = one(here * count + index)
            if seq == 0:
                input_out[here, rows, :] += value
            else:
                input_out[there, rows, :] = value

        loop(0, count, send_rows)
        copy.start()
        loop(0, count, keep_rows)

    def ring_begin():
        for group in groups:
            group.load().wait()
        for group in groups:
            group.both_steps(0, first=True)

    def ring_on(step):
        for group in groups:
            group.both_steps(step)

    def ring_cross():
        for group in groups:
            group.far_step(ring.far_hops - 1)

    def shards_cross():
        feed_shard[...] = feed_group.finish().astype(bf16)
        feed_cross.start()
        more_shard[...] = more_far_group.finish().astype(bf16)
        more_cross.start()

    def spread_begin():
        shard_load.wait()
        feed_cross.wait_recv()
        where = feed_spread.place(ring.core, ring.spot)
        feed_out[where, :] = (feed_own_shard[...] + feed_got[...].astype(f32)).astype(bf16)
        feed_spread.begin()
        value = more_own_group.finish()
        more_cross.wait_recv()
        where = more_spread.place(ring.core, ring.spot)
        more_out[where, :] = (value + more_got[...].astype(f32)).astype(bf16)
        more_spread.begin()

    for copy in first_loads:
        copy.wait()

    def attention(index):
        seq = index // pairs
        pair = index % pairs

        @pl.when(index == pairs)
        def _():
            go_cross.wait_recv()
            for copy in far_loads + spare_loads[:1]:
                copy.wait()

        def between(head):
            del head

        attend_back(len_ref[seq], qkv, o, lse, go, acc_ref, seq, pair, local, block, between)

        @pl.when(index == 0)
        def _():
            ring_begin()

        @pl.when(index == pairs - 1)
        def _():
            for copy in far_loads:
                copy.start()
            for copy in later_loads:
                copy.wait()
            turn_rows(0, own_cross)
            for copy in far_rows:
                copy.start()

        @pl.when((index >= 1) & (index < pairs))
        def _():
            ring_on(index)

        @pl.when(index == pairs)
        def _():
            loop(pairs, ring.near_hops, ring_on)
            ring_cross()

        @pl.when(index == pairs + 1)
        def _():
            shards_cross()

        @pl.when(index == 2 * pairs - 1)
        def _():
            spread_begin()

    loop(0, 2 * pairs, attention)
    for copy in far_rows + spare_loads[1:]:
        copy.wait()
    ones = jnp.ones((16, seq_len), bf16)
    biases = dot_nn(ones, qkv[0]) + dot_nn(ones, qkv[1])
    turn_rows(1, far_cross)
    sums_cross.start()
    for spread in (feed_spread, more_spread):
        spread.both_steps(1)
    for part in range(3):
        columns = pl.ds(part * local, local)
        value = dot_tn(qkv[0, :, columns], h[0]) + dot_tn(qkv[1, :, columns], h[1])
        query_local[columns, :] = value.astype(bf16)
    rows = query_local.shape[0] - 3 * local
    sums_cross.wait_recv()
    tile_row = lax.broadcasted_iota(jnp.int32, (16, width), 0)
    both = sums[...] + sums_got[...]
    own_biases = jnp.concatenate([biases[0:1, :local], biases[0:1, 2 * local :]], axis=1)
    last = jnp.where(
        tile_row == 0, both[0:1], jnp.where(tile_row == 1, both[1:2], jnp.where(tile_row == 2, own_biases, 0.0))
    )
    query_local[pl.ds(3 * local, 16), :] = last.astype(bf16)
    query_local[pl.ds(3 * local + 16, rows - 16), :] = jnp.zeros((rows - 16, width), bf16)

    query_group.hand_over()

    def onward(step):
        for spread in (feed_spread, more_spread):
            spread.both_steps(step)

    loop(2, ring.near_hops, onward)
    query_group.both_steps(0, first=True)
    for spread in (feed_spread, more_spread):
        spread.close()
    loop(1, ring.near_hops, query_group.both_steps)
    query_group.far_step(ring.far_hops - 1)
    for spread in (feed_spread, more_spread):
        spread.far_step(ring.far_hops, last=True)
    query_out[query_spread.place(ring.core, ring.spot), :] = query_group.finish().astype(bf16)
    query_spread.begin()
    own_cross.wait_recv()
    input_out[there] += row_got[0].astype(f32)
    far_cross.wait_recv()
    input_out[here] += row_got[1].astype(f32)
    loop(1, ring.near_hops, query_spread.both_steps)
    query_spread.close()
    query_spread.far_step(ring.far_hops, last=True)
    for group in groups + (query_group,):
        group.sent()
    for copy in (go_cross, feed_cross, more_cross, own_cross, far_cross, sums_cross):
        copy.wait_send()
    for spread in (feed_spread, more_spread, query_spread):
        spread.sent()


def back(
    lens, tokens, token_own, token_far, qkv_own, qkv_far, o_own, o_far, lse_own, lse_far, go_own, go_send,
    h_own, h_far, grad, weight, gain, feed_far, feed_own, more_far, more_own, dp
):
    half, width = token_own.shape
    seq_len = 2 * half
    columns = qkv_own.shape[1]
    local = columns // 3
    feed_rows = feed_far.shape[0]
    more_rows = more_far.shape[0]
    query_rows = padded(columns + 16, dp)
    anywhere = pl.BlockSpec(memory_space=pl.ANY)
    inside = pl.BlockSpec(memory_space=pltpu.VMEM)
    feed_size, more_size = feed_rows // dp, more_rows // dp
    return pl.pallas_call(
        functools.partial(back_kernel, dp=dp),
        in_specs=[pl.BlockSpec(memory_space=pltpu.SMEM)]
        + [anywhere] * 15
        + [inside]
        + [anywhere] * 4,
        out_specs=[inside] * 4,
        out_shape=[
            jax.ShapeDtypeStruct((feed_rows, width), bf16),
            jax.ShapeDtypeStruct((more_rows, width), bf16),
            jax.ShapeDtypeStruct((query_rows, width), bf16),
            jax.ShapeDtypeStruct((2, half, width), f32),
        ],
        scratch_shapes=[
            pltpu.SemaphoreType.DMA((17,)),
            pltpu.SemaphoreType.DMA((2, 6)),
            pltpu.VMEM((2, seq_len, columns), bf16),
            pltpu.VMEM((seq_len, local), bf16),
            pltpu.VMEM((seq_len, local), f32),
            pltpu.VMEM((2, seq_len, local), bf16),
            pltpu.VMEM((seq_len, width), bf16),
            pltpu.VMEM((2, seq_len, width), bf16),
            pltpu.VMEM((width, columns), bf16),
            pltpu.VMEM((seq_len, PAIR), f32),
            pltpu.VMEM((8, width), f32),
            pltpu.VMEM((8, width), f32),
            pltpu.VMEM((2, half, width), bf16),
            pltpu.VMEM((2, half, width), bf16),
            pltpu.VMEM((feed_size, width), f32),
            pltpu.VMEM((feed_size, width), bf16),
            pltpu.VMEM((feed_size, width), bf16),
            pltpu.VMEM((more_size, width), bf16),
            pltpu.VMEM((more_size, width), bf16),
            pltpu.VMEM((feed_rows // 2, width), bf16),
            pltpu.VMEM((more_rows // 2, width), bf16),
            pltpu.VMEM((more_rows // 2, width), bf16),
            pltpu.VMEM((query_rows, width), bf16),
        ]
        + Group.scratch(feed_rows, width, dp)
        + Group.scratch(more_rows, width, dp)
        + Group.scratch(more_rows, width, dp)
        + Group.scratch(query_rows, width, dp)
        + Spread.scratch(dp) * 3,
        compiler_params=remote_params(2),
        cost_estimate=cost(80),
        name="back",
    )(
        lens, tokens, token_own, token_far, qkv_own, qkv_far, o_own, o_far, lse_own, lse_far,
        go_own, go_send, h_own, h_far, grad, weight, gain, feed_far, feed_own, more_far, more_own,
    )


def body(
    tokens,
    lengths,
    layer_index,
    norm_one_gain,
    norm_one_bias,
    attend_weight,
    query_bias,
    value_bias,
    output_weight,
    output_bias,
    norm_two_gain,
    norm_two_bias,
    expand_weight,
    expand_bias,
    shrink_weight,
    shrink_bias,
    cotangent,
):
    seq_dev, half, width = tokens.shape
    dp = lax.axis_size("dp")
    here = lax.axis_index("tensor")
    there = 1 - here
    place = lax.axis_index("dp")

    def exchange(values):
        return lax.ppermute(values, "tensor", [(0, 1), (1, 0)])

    def pick(values, index):
        return lax.dynamic_index_in_dim(values, index, 0, keepdims=False)

    def layer(stack):
        return select_layer(stack, layer_index)

    def wide(stack):
        return layer(stack).astype(f32)[None]

    def after(values, earlier):
        return lax.optimization_barrier((values, earlier))[0]

    def share(matrix):
        rows = matrix.shape[0] // dp
        return lax.dynamic_slice_in_dim(matrix, place * rows, rows, 0)

    def gather(piece):
        return lax.all_gather(piece, "dp", axis=0, tiled=False)

    out_mat = layer(output_weight)
    expand_mat = layer(expand_weight)
    shrink_mat = layer(shrink_weight)
    proj_rows = out_mat.shape[0] // dp
    first_got = exchange(jnp.concatenate([share(out_mat), share(shrink_mat)], axis=0))
    expand_got = exchange(share(expand_mat))
    mine_own, mine_far = pick(tokens, here), pick(tokens, there)
    cot_mine = pick(cotangent, here)
    token_far = exchange(mine_own)
    token_own = exchange(after(mine_far, token_far))
    cot_got = exchange(after(pick(cotangent, there), token_own))
    first_all = gather(first_got)
    out_far = first_all[:, :proj_rows].reshape(out_mat.shape)
    shrink_far = first_all[:, proj_rows:].reshape(shrink_mat.shape)
    expand_far = gather(expand_got).reshape(expand_mat.shape)
    expand_shift_far = exchange(after(layer(expand_bias), token_far))[None].astype(f32)

    len_own = lax.dynamic_slice_in_dim(lengths, here, 1, 0)
    len_far = lax.dynamic_slice_in_dim(lengths, there, 1, 0)
    at_own = jnp.concatenate([here[None].astype(jnp.int32), len_own])
    at_far = jnp.concatenate([here[None].astype(jnp.int32), len_far])
    lens = jnp.concatenate([len_own, len_far])

    gain_one, shift_one = wide(norm_one_gain), wide(norm_one_bias)
    gain_two, shift_two = wide(norm_two_gain), wide(norm_two_bias)
    attend_flat = layer(attend_weight).reshape(width, -1)
    local = attend_flat.shape[1] // 3
    qkv_bias = jnp.concatenate(
        [wide(query_bias), jnp.zeros((1, local), f32), wide(value_bias)], axis=1
    )

    h_far, qkv_far = project(at_far, mine_far, token_far, gain_one, shift_one, attend_flat, qkv_bias)
    o_far, lse_far = attend(len_far, qkv_far)
    o_got = exchange(o_far)
    h_own, qkv_own = project(at_own, mine_own, token_own, gain_one, shift_one, attend_flat, qkv_bias)
    o_own, lse_own = attend(len_own, qkv_own)

    h_two, gf, resid, sums = resid_norm(
        at_own, mine_own, token_own, cot_mine, cot_got, o_own, o_got, out_mat, out_far,
        wide(output_bias), gain_two, shift_two,
    )
    hidden = expand_mat.shape[1]
    span = min(dp, 16)
    feed_rows = padded(2 * hidden, span)
    f_part, gh_part, grads_own, db_own = feed(
        h_two, gf, expand_mat, wide(expand_bias), shrink_mat, feed_rows
    )
    f_sum, gh_two, grads_far, db_far, feed_own = feed(
        h_two, gf, expand_far, expand_shift_far, shrink_far, feed_rows,
        (f_part, gh_part, grads_own.reshape(feed_rows, width)), span,
    )

    def bias_rows(grad):
        count = hidden // width
        return jnp.pad(grad.reshape(count, width), ((0, 8 - count), (0, 0)))

    more_rows = padded(out_mat.shape[0] + 16, span)
    result, grad_resid, go_own, go_send, more_own, more_far = turn(
        at_own, cot_mine, cot_got, resid, f_sum, gh_two, o_own, o_got, out_mat, out_far,
        wide(shrink_bias), gain_two, sums, bias_rows(db_own), bias_rows(db_far), more_rows,
    )
    result_got = exchange(lax.dynamic_slice_in_dim(result, there * half, half, 0).astype(bf16))

    feed_sum, more_sum, query_sum, input_grad = back(
        lens, tokens, token_own, token_far, qkv_own, qkv_far, o_own, o_far, lse_own, lse_far,
        go_own, go_send, h_own, h_far, grad_resid, attend_flat, gain_one,
        grads_far.reshape(feed_rows, width), feed_own, more_far, more_own, span,
    )
    if dp > span:
        spans = [[base + index for base in range(0, dp, span)] for index in range(span)]
        feed_sum, more_sum, query_sum = (
            lax.psum(part.astype(f32), "dp", axis_index_groups=spans)
            for part in (feed_sum, more_sum, query_sum)
        )

    result_own = lax.dynamic_slice_in_dim(result, here * half, half, 0)
    result_far = result_got.astype(f32)
    block_output = jnp.where(
        here == 0, jnp.stack([result_own, result_far]), jnp.stack([result_far, result_own])
    )
    expand_grad = feed_sum[:hidden].astype(f32).T
    shrink_grad = feed_sum[feed_rows // 2 : feed_rows // 2 + hidden].astype(f32)
    proj = out_mat.shape[0]
    out_grad = more_sum[:proj].astype(f32)
    small = more_sum[proj : proj + 16].astype(f32)
    attend_grad = query_sum[: 3 * local].astype(f32).T.reshape(width, 3, local)
    last = query_sum[3 * local : 3 * local + 16].astype(f32)
    squares = jnp.sum(small[4:8], axis=1)
    rms_values = jnp.sqrt(squares[:3] / (squares[3] * width))
    return (
        block_output,
        input_grad,
        last[0],
        last[1],
        attend_grad,
        last[2, :local],
        last[2, local:],
        out_grad,
        small[0],
        small[1],
        small[2],
        expand_grad,
        small[8 : 8 + hidden // width].reshape(hidden),
        shrink_grad,
        small[3],
        rms_values,
    )


def solution(mesh):
    in_specs = (
        P("dp", "tensor", None),
        P("dp"),
        P(),
        P(),
        P(),
        P(None, None, None, "tensor"),
        P(None, "tensor"),
        P(None, "tensor"),
        P(None, "tensor", None),
        P(),
        P(),
        P(),
        P(None, None, "tensor"),
        P(None, "tensor"),
        P(None, "tensor", None),
        P(),
        P("dp", "tensor", None),
    )
    out_specs = (
        P("dp", "tensor", None),
        P("dp", "tensor", None),
        P(),
        P(),
        P(None, None, "tensor"),
        P("tensor"),
        P("tensor"),
        P("tensor", None),
        P(),
        P(),
        P(),
        P(None, "tensor"),
        P("tensor"),
        P("tensor", None),
        P(),
        P(),
    )
    return jax.shard_map(body, mesh=mesh, in_specs=in_specs, out_specs=out_specs, check_vma=False)
```

```python
import functools

import jax
import jax.numpy as jnp
from jax import lax
from jax.experimental import pallas as pl
from jax.experimental.pallas import tpu as pltpu
from jax.sharding import PartitionSpec as P

HD = 64
PAIR = 2 * HD
epsilon = 1e-05
masked_fill = -1e30
VMEM_LIMIT = 56 * 1024 * 1024
f32 = jnp.float32
bf16 = jnp.bfloat16


def dot_nn(left, right):
    return lax.dot_general(left, right, (((1,), (0,)), ((), ())), preferred_element_type=f32)


def dot_nt(left, right):
    return lax.dot_general(left, right, (((1,), (1,)), ((), ())), preferred_element_type=f32)


def dot_tn(left, right):
    return lax.dot_general(left, right, (((0,), (0,)), ((), ())), preferred_element_type=f32)


def select_layer(stack, layer_index):
    return lax.dynamic_index_in_dim(stack, layer_index[0], 0, keepdims=False)


def whole(shape):
    return pl.BlockSpec(shape, lambda *index: (0,) * len(shape))


def params():
    return pltpu.CompilerParams(dimension_semantics=("arbitrary",), vmem_limit_bytes=VMEM_LIMIT)


def remote_params(number):
    return pltpu.CompilerParams(
        collective_id=number, has_side_effects=True, vmem_limit_bytes=VMEM_LIMIT
    )


def cost(microseconds):
    return pl.CostEstimate(
        flops=int(microseconds * 1e9), bytes_accessed=int(microseconds * 3e6), transcendentals=0
    )


def normalized(x):
    center = jnp.mean(x, axis=-1, keepdims=True)
    x = x - center
    inverse = lax.rsqrt(jnp.mean(x * x, axis=-1, keepdims=True) + epsilon)
    return x * inverse, inverse


def norm_back(unit, inverse, gain, grad):
    scaled = grad * gain
    return inverse * (
        scaled
        - jnp.mean(scaled, axis=-1, keepdims=True)
        - unit * jnp.mean(scaled * unit, axis=-1, keepdims=True)
    )


class Halves:
    def __init__(self, half, block):
        self.count = half // block
        self.block = block

    def mine(self, i, at):
        return jnp.minimum(i, self.count - 1), 0

    def got(self, i, at):
        return jnp.maximum(i - self.count, 0), 0

    def whole(self, i, at):
        first = i < self.count
        side = jnp.where(first, at[0], 1 - at[0])
        return side * self.count + jnp.where(first, i, i - self.count), 0

    def position(self, at):
        i = pl.program_id(0)
        return self.whole(i, at)[0] * self.block + lax.broadcasted_iota(
            jnp.int32, (self.block, 1), 0
        )

    def pick(self, mine, got):
        return jnp.where(pl.program_id(0) < self.count, mine[...], got[...]).astype(f32)

    def specs(self, width, kind):
        return pl.BlockSpec((self.block, width), getattr(self, kind))


def fixed(shape):
    return pl.BlockSpec(shape, lambda i, at: (0,) * len(shape))


def project_kernel(at, mine, got, gain_ref, shift_ref, weight_ref, bias_ref, h_ref, qkv_ref, *, halves):
    unit, _ = normalized(halves.pick(mine, got))
    h = unit * gain_ref[...] + shift_ref[...]
    h = jnp.where(halves.position(at) < at[1], h, 0.0).astype(bf16)
    h_ref[...] = h
    qkv_ref[...] = (dot_nn(h, weight_ref[...]) + bias_ref[...]).astype(bf16)


def project(at, mine, got, gain, shift, weight, bias):
    half, width = mine.shape
    columns = weight.shape[1]
    halves = Halves(half, min(256, half))
    return pl.pallas_call(
        functools.partial(project_kernel, halves=halves),
        grid_spec=pltpu.PrefetchScalarGridSpec(
            num_scalar_prefetch=1,
            grid=(2 * halves.count,),
            in_specs=[
                halves.specs(width, "mine"),
                halves.specs(width, "got"),
                fixed((1, width)),
                fixed((1, width)),
                fixed((width, columns)),
                fixed((1, columns)),
            ],
            out_specs=[halves.specs(width, "whole"), halves.specs(columns, "whole")],
        ),
        out_shape=[
            jax.ShapeDtypeStruct((2 * half, width), bf16),
            jax.ShapeDtypeStruct((2 * half, columns), bf16),
        ],
        compiler_params=params(),
        cost_estimate=cost(7),
        name="project",
    )(at, mine, got, gain, shift, weight, bias)


def lane_index(rows):
    return lax.broadcasted_iota(jnp.int32, (rows, PAIR), 1)


def causal_block(block):
    row = lax.broadcasted_iota(jnp.int32, (block, block), 0)
    column = lax.broadcasted_iota(jnp.int32, (block, block), 1)
    return row, column


def attend_kernel(at, q_ref, k_ref, v_ref, o_ref, lse_ref, *, block, half):
    seq_len = k_ref.shape[0]
    row, column = causal_block(block)
    keep = column <= row

    def query_half(side):
        end_all = (side + 1) * half
        lane = lane_index(end_all)
        lane_q = lane_index(half)
        position = lax.broadcasted_iota(jnp.int32, (end_all, PAIR), 0)
        key_bias = jnp.where(position < at[1], 0.0, masked_fill)
        q = q_ref[...].astype(f32) * (HD**-0.5)
        k = k_ref[:end_all, :].astype(f32)
        values = v_ref[:end_all, :]
        low = lane < HD
        low_q = lane_q < HD
        outs = []
        stats = []
        for head in range(2):
            mine = low if head == 0 else jnp.logical_not(low)
            mine_q = low_q if head == 0 else jnp.logical_not(low_q)
            spare = HD if head == 0 else 0
            q_aug = jnp.where(mine_q, q, jnp.where(lane_q == spare, 1.0, 0.0)).astype(bf16)
            k_aug = jnp.where(mine, k, jnp.where(lane == spare, key_bias, 0.0)).astype(bf16)
            v_own = jnp.where(mine, values, jnp.zeros_like(values))
            pieces = []
            notes = []
            for index in range(half // block):
                start = side * half + index * block
                end = start + block
                scores = dot_nt(q_aug[index * block : (index + 1) * block], k_aug[:end])
                last = jnp.where(keep, scores[:, start:end], masked_fill)
                scores = jnp.concatenate([scores[:, :start], last], axis=1) if start else last
                top = jnp.max(scores, axis=-1, keepdims=True)
                weights = jnp.exp(scores - top)
                total = jnp.sum(weights, axis=-1, keepdims=True)
                mixed = dot_nn(weights.astype(bf16), v_own[:end])
                pieces.append(mixed * (1.0 / total))
                notes.append(jnp.broadcast_to(top + jnp.log(total), (block, PAIR)))
            outs.append(jnp.concatenate(pieces, axis=0))
            stats.append(jnp.concatenate(notes, axis=0))
        o_ref[...] = (outs[0] + outs[1]).astype(bf16)
        lse_ref[...] = jnp.where(low_q, stats[1], stats[0])

    for side in range(seq_len // half):
        pl.when(at[0] == side)(functools.partial(query_half, side))


def attend(at, qkv, microseconds):
    seq_len = qkv.shape[0]
    half = seq_len // 2
    width = qkv.shape[1] // 3
    pairs = width // PAIR

    def columns(part):
        return pl.BlockSpec((seq_len, PAIR), lambda i, at: (0, part * pairs + i))

    out = pl.BlockSpec((half, PAIR), lambda i, at: (0, i))
    return pl.pallas_call(
        functools.partial(attend_kernel, block=min(256, half), half=half),
        grid_spec=pltpu.PrefetchScalarGridSpec(
            num_scalar_prefetch=1,
            grid=(pairs,),
            in_specs=[
                pl.BlockSpec((half, PAIR), lambda i, at: (at[0], i)),
                columns(1),
                columns(2),
            ],
            out_specs=[out, out],
        ),
        out_shape=[
            jax.ShapeDtypeStruct((half, width), bf16),
            jax.ShapeDtypeStruct((half, width), f32),
        ],
        compiler_params=params(),
        cost_estimate=cost(microseconds),
        name="attend",
    )(at, qkv, qkv, qkv)


class Pair:
    def __init__(self, half, block):
        self.count = half // block
        self.block = block

    def first(self, i, at):
        return jnp.minimum(i, self.count - 1), 0

    def second(self, i, at):
        return jnp.maximum(i - self.count, 0), 0

    def both(self, i, at):
        return i, 0

    def valid(self, at):
        i = pl.program_id(0)
        second = (i >= self.count).astype(jnp.int32)
        start = (at[0] * self.count + i - second * self.count) * self.block
        position = start + lax.broadcasted_iota(jnp.int32, (self.block, 1), 0)
        return (position < jnp.where(i < self.count, at[1], at[2])).astype(f32)

    def pick(self, first, second):
        return jnp.where(pl.program_id(0) < self.count, first[...], second[...])

    def specs(self, width, kind):
        return pl.BlockSpec((self.block, width), getattr(self, kind))


def resid_kernel(
    at, x_ref, cot_ref, o_first, o_second, got_first, got_second, w_ref, w_far, shift_out, gain,
    shift, h_ref, gf_ref, resid_ref, sums_ref, *, pair
):
    valid = pair.valid(at)
    attn = (
        dot_nn(pair.pick(o_first, o_second), w_ref[...])
        + dot_nn(pair.pick(got_first, got_second), w_far[...])
        + shift_out[...]
    )
    resid = x_ref[...].astype(f32) + valid * attn
    resid_ref[...] = resid
    unit, _ = normalized(resid)
    h_ref[...] = (valid * (unit * gain[...] + shift[...])).astype(bf16)
    gf = valid * cot_ref[...].astype(f32)
    gf_ref[...] = gf.astype(bf16)

    @pl.when(pl.program_id(0) == 0)
    def _():
        sums_ref[...] = jnp.zeros_like(sums_ref)

    sums_ref[0:1] += jnp.sum(valid * attn * attn, axis=0, keepdims=True)
    sums_ref[1:2] += jnp.sum(gf, axis=0, keepdims=True)


def resid_norm(at, x, cot, o_first, o_second, got_first, got_second, w, w_far, shift_out, gain, shift):
    rows, width = x.shape
    local = o_first.shape[1]
    pair = Pair(rows // 2, min(256, rows // 2))
    return pl.pallas_call(
        functools.partial(resid_kernel, pair=pair),
        grid_spec=pltpu.PrefetchScalarGridSpec(
            num_scalar_prefetch=1,
            grid=(2 * pair.count,),
            in_specs=[
                pair.specs(width, "both"),
                pair.specs(width, "both"),
                pair.specs(local, "first"),
                pair.specs(local, "second"),
                pair.specs(local, "first"),
                pair.specs(local, "second"),
                fixed((local, width)),
                fixed((local, width)),
                fixed((1, width)),
                fixed((1, width)),
                fixed((1, width)),
            ],
            out_specs=[pair.specs(width, "both")] * 3 + [fixed((8, width))],
        ),
        out_shape=[
            jax.ShapeDtypeStruct((rows, width), bf16),
            jax.ShapeDtypeStruct((rows, width), bf16),
            jax.ShapeDtypeStruct((rows, width), f32),
            jax.ShapeDtypeStruct((8, width), f32),
        ],
        compiler_params=params(),
        cost_estimate=cost(8),
        name="resid_norm",
    )(at, x, cot, o_first, o_second, got_first, got_second, w, w_far, shift_out, gain, shift)


class Ring:
    def __init__(self, dp):
        self.chips = dp // 2
        self.far_hops = self.chips // 2
        self.near_hops = self.chips - 1 - self.far_hops
        place = lax.axis_index("dp")
        self.tensor = lax.axis_index("tensor")
        self.base = place // dp * dp
        place = place % dp
        self.core = place % 2
        chip = place // 2
        depth = chip // 2
        self.spot = depth + (chip % 2) * (self.chips - 1 - 2 * depth)
        self.turn = 1 - 2 * self.core

    def device(self, spot, core):
        spot = (spot + self.chips) % self.chips
        side = spot // (self.chips // 2)
        chip = 2 * (spot + side * (self.chips - 1 - 2 * spot)) + side
        return (self.base + chip * 2 + core, self.tensor)

    def ahead(self):
        return self.device(self.spot + self.turn, self.core)

    def behind(self):
        return self.device(self.spot - self.turn, self.core)

    def sibling(self):
        return self.device(self.spot, 1 - self.core)

    def partner(self):
        return (lax.axis_index("dp"), 1 - self.tensor)

    def chunk(self, offset):
        return (self.spot + self.turn * offset + 2 * self.chips) % self.chips


def send(source, target, sems, index, device):
    copy = pltpu.make_async_remote_copy(
        src_ref=source,
        dst_ref=target,
        send_sem=sems.at[0, index],
        recv_sem=sems.at[1, index],
        device_id=device,
        device_id_type=pl.DeviceIdType.MESH,
    )
    return copy


def loop(start, stop, step):
    def run(index, carry):
        step(index)
        return carry

    lax.fori_loop(start, stop, run, 0)


class Group:
    def __init__(self, ring, source, acc, scratch):
        self.ring = ring
        self.source = source
        self.acc = acc
        self.pair, self.slots, self.pair_sems, self.ring_sems, self.load_sem = scratch
        self.rows = source.shape[0] // (2 * ring.chips)

    @staticmethod
    def scratch(rows, width, dp):
        chips = dp // 2
        size = rows // (2 * chips)
        return [
            pltpu.VMEM((chips, size, width), bf16),
            pltpu.VMEM((chips - 1, size, width), bf16),
            pltpu.SemaphoreType.DMA((2, chips)),
            pltpu.SemaphoreType.DMA((2, chips - 1)),
            pltpu.SemaphoreType.DMA((1,)),
        ]

    def place(self, core, chunk):
        start = (core * self.ring.chips + chunk) * self.rows
        return pl.ds(pl.multiple_of(start, 16), self.rows)

    def mine(self, chunk):
        if self.acc is None:
            return self.source.at[self.place(self.ring.core, chunk)]
        return self.acc.at[pl.ds(pl.multiple_of(chunk * self.rows, 16), self.rows)]

    def load(self):
        count = self.rows * self.ring.chips
        start = pl.multiple_of(self.ring.core * count, 16)
        return pltpu.make_async_copy(
            self.source.at[pl.ds(start, count)], self.acc, self.load_sem.at[0]
        )

    def to_sibling(self, chunk):
        source = self.source.at[self.place(1 - self.ring.core, chunk)]
        return send(source, self.pair.at[chunk], self.pair_sems, chunk, self.ring.sibling())

    def hand_over(self):
        ring = self.ring

        def both(step):
            self.to_sibling(ring.chunk(step - ring.far_hops)).start()
            self.to_sibling(ring.chunk(ring.near_hops - step)).start()

        loop(0, ring.near_hops, both)
        self.to_sibling(ring.chunk(-1)).start()
        self.to_sibling(ring.chunk(0)).start()

    def term(self, chunk):
        self.to_sibling(chunk).wait_recv()
        return self.mine(chunk)[...].astype(f32) + self.pair[chunk].astype(f32)

    def far_copy(self, step):
        chunk = self.ring.chunk(self.ring.far_hops - step)
        return send(
            self.mine(chunk), self.slots.at[step], self.ring_sems, step, self.ring.ahead()
        )

    def near_copy(self, step):
        slot = self.ring.far_hops + step
        chunk = self.ring.chunk(step - self.ring.near_hops)
        return send(
            self.mine(chunk), self.slots.at[slot], self.ring_sems, slot, self.ring.behind()
        )

    def far_step(self, step, first=False):
        chunk = self.ring.chunk(self.ring.far_hops - step)
        value = self.term(chunk)
        if not first:
            self.far_copy(step - 1).wait_recv()
            value += self.slots[step - 1].astype(f32)
        self.mine(chunk)[...] = value.astype(bf16)
        self.far_copy(step).start()

    def near_step(self, step, first=False):
        slot = self.ring.far_hops + step
        chunk = self.ring.chunk(step - self.ring.near_hops)
        value = self.term(chunk)
        if not first:
            self.near_copy(step - 1).wait_recv()
            value += self.slots[slot - 1].astype(f32)
        self.mine(chunk)[...] = value.astype(bf16)
        self.near_copy(step).start()

    def both_steps(self, step, first=False):
        self.far_step(step, first)
        self.near_step(step, first)

    def finish(self):
        ring = self.ring
        value = self.term(ring.chunk(0))
        self.far_copy(ring.far_hops - 1).wait_recv()
        self.near_copy(ring.near_hops - 1).wait_recv()
        value += self.slots[ring.far_hops - 1].astype(f32)
        return value + self.slots[ring.chips - 2].astype(f32)

    def sent(self):
        ring = self.ring
        loop(0, ring.chips, lambda chunk: self.to_sibling(chunk).wait_send())
        loop(0, ring.far_hops, lambda step: self.far_copy(step).wait_send())
        loop(0, ring.near_hops, lambda step: self.near_copy(step).wait_send())


class Spread:
    def __init__(self, ring, out, scratch):
        self.ring = ring
        self.out = out
        self.pair_sems, self.ring_sems = scratch
        self.rows = out.shape[0] // (2 * ring.chips)

    @staticmethod
    def scratch(dp):
        chips = dp // 2
        return [pltpu.SemaphoreType.DMA((2, chips)), pltpu.SemaphoreType.DMA((2, chips))]

    def place(self, core, chunk):
        start = (core * self.ring.chips + chunk) * self.rows
        return pl.ds(pl.multiple_of(start, 16), self.rows)

    def pass_on(self, chunk, slot, device):
        where = self.out.at[self.place(self.ring.core, chunk)]
        return send(where, where, self.ring_sems, slot, device)

    def to_sibling(self, chunk):
        where = self.out.at[self.place(self.ring.core, chunk)]
        return send(where, where, self.pair_sems, chunk, self.ring.sibling())

    def from_sibling(self, chunk):
        where = self.out.at[self.place(1 - self.ring.core, chunk)]
        return send(where, where, self.pair_sems, chunk, self.ring.sibling())

    def far_copy(self, step):
        return self.pass_on(self.ring.chunk(-step), step, self.ring.ahead())

    def near_copy(self, step):
        return self.pass_on(self.ring.chunk(step), self.ring.far_hops + step, self.ring.behind())

    def far_landed(self, step):
        return self.pass_on(self.ring.chunk(-step - 1), step, self.ring.ahead())

    def near_landed(self, step):
        return self.pass_on(
            self.ring.chunk(step + 1), self.ring.far_hops + step, self.ring.behind()
        )

    def begin(self):
        self.far_copy(0).start()
        self.near_copy(0).start()
        self.to_sibling(self.ring.chunk(0)).start()

    def far_step(self, step, last=False):
        self.far_landed(step - 1).wait_recv()
        if not last:
            self.far_copy(step).start()
        self.to_sibling(self.ring.chunk(-step)).start()

    def near_step(self, step, last=False):
        self.near_landed(step - 1).wait_recv()
        if not last:
            self.near_copy(step).start()
        self.to_sibling(self.ring.chunk(step)).start()

    def both_steps(self, step):
        self.far_step(step)
        self.near_step(step)

    def close(self):
        self.far_step(self.ring.near_hops)
        self.near_step(self.ring.near_hops, last=True)

    def sent(self):
        ring = self.ring
        loop(0, ring.chips, lambda chunk: self.from_sibling(chunk).wait_recv())
        loop(0, ring.chips, lambda chunk: self.to_sibling(chunk).wait_send())
        loop(0, ring.far_hops, lambda step: self.far_copy(step).wait_send())
        loop(0, ring.near_hops, lambda step: self.near_copy(step).wait_send())


def greet(*devices):
    barrier = pltpu.get_barrier_semaphore()
    for device in devices:
        pl.semaphore_signal(barrier, inc=1, device_id=device, device_id_type=pl.DeviceIdType.MESH)
    pl.semaphore_wait(barrier, len(devices))


def padded(rows, dp):
    unit = 16 * dp
    return -(-rows // unit) * unit


def feed_kernel(
    h_ref, gf_ref, e_far, b_far, s_far, e_own, b_own, s_own,
    f_ref, gh_ref, grad_ref, db_far, db_own, shard_ref,
    act_ref, gu_ref, tiles, crossing, got, y_sems, *rest, chunk, dp
):
    seq_len = h_ref.shape[0]
    tile = e_own.shape[1]
    root = 0.7978845608
    cube = 0.044715
    step = pl.program_id(0)
    far_steps = tiles.shape[0]
    is_far = step < far_steps
    parts = seq_len // chunk
    ring = Ring(dp)
    groups = [
        Group(ring, tiles.at[index], None, rest[5 * index : 5 * index + 5])
        for index in range(far_steps)
    ]

    def cross(index):
        return send(crossing.at[index], got.at[index], y_sems, index, ring.partner())

    def finish(index):
        crossing[index] = groups[index].finish().astype(bf16)
        cross(index).start()

    plan = {}
    for index, group in enumerate(groups):
        slot = (parts + 1) * (index + 1) - 1
        plan.setdefault(slot, []).append(group.hand_over)
        for hop in range(ring.far_hops):
            slot_of_hop = slot + 2 + hop * ((2 * parts + 1) // ring.far_hops + 1)
            action = functools.partial(group.far_step, hop)
            if hop < ring.near_hops:
                action = functools.partial(group.both_steps, hop, hop == 0)
            plan.setdefault(slot_of_hop, []).append(action)
        slot += 2 + ring.far_hops * ((2 * parts + 1) // ring.far_hops + 1)
        plan.setdefault(slot, []).append(functools.partial(finish, index))

    def tick(part):
        for slot, actions in plan.items():
            if slot % (parts + 1) == part:

                @pl.when(step == slot // (parts + 1))
                def _():
                    for action in actions:
                        action()

    @pl.when(step == 0)
    def _():
        f_ref[...] = jnp.zeros_like(f_ref)
        gh_ref[...] = jnp.zeros_like(gh_ref)
        greet(ring.ahead(), ring.behind(), ring.sibling(), ring.partner())

    e = jnp.where(is_far, e_far[...], e_own[...])
    s = jnp.where(is_far, s_far[...], s_own[...])
    bias = jnp.where(is_far, b_far[...], b_own[...])
    total = jnp.zeros((1, tile), f32)
    for index in range(parts):
        rows = pl.ds(index * chunk, chunk)
        u = dot_nn(h_ref[rows, :], e) + bias
        ga = dot_nt(gf_ref[rows, :], s)
        square = u * u
        bent = jnp.tanh(u * (root + (root * cube) * square))
        half = 0.5 + 0.5 * bent
        act = (u * half).astype(bf16)
        slope = half + (0.5 * u) * (1.0 - bent * bent) * (root + (3.0 * root * cube) * square)
        gu_wide = (slope * ga).astype(bf16)
        act_ref[rows, :] = act
        gu_ref[rows, :] = gu_wide
        total += jnp.sum(gu_wide.astype(f32), axis=0, keepdims=True)
        f_ref[rows, :] += dot_nn(act, s)
        gh_ref[rows, :] += dot_nt(gu_wide, e)
        tick(index)
    grad_e = dot_tn(gu_ref[...], h_ref[...]).astype(bf16)
    grad_s = dot_tn(act_ref[...], gf_ref[...]).astype(bf16)

    @pl.when(is_far)
    def _():
        db_far[...] = total
        tiles[jnp.minimum(step, far_steps - 1), :tile, :] = grad_e
        tiles[jnp.minimum(step, far_steps - 1), tile:, :] = grad_s

    @pl.when(jnp.logical_not(is_far))
    def _():
        db_own[...] = total
        half_chunks, _, rows, width = grad_ref.shape
        grad_ref[: half_chunks // 2, 0] = grad_e.reshape(half_chunks // 2, rows, width)
        grad_ref[half_chunks // 2 :, 0] = grad_s.reshape(half_chunks // 2, rows, width)

    tick(parts)

    @pl.when(step == pl.num_programs(0) - 1)
    def _():
        for index in range(far_steps):
            cross(index).wait_recv()
            shard_ref[index] = got[index]
        for index, group in enumerate(groups):
            cross(index).wait_send()
            group.sent()


def feed(h, gf, e_far, b_far, s_far, e_own, b_own, s_own, dp):
    seq_len, width = h.shape
    hidden = e_own.shape[1]
    tile = min(512, hidden)
    steps = hidden // tile
    size = 2 * tile // dp
    whole_rows = whole((seq_len, width))

    def far(i):
        return jnp.minimum(i, steps - 1)

    def own(i):
        return jnp.maximum(i - steps, 0)

    def weights(of):
        return [
            pl.BlockSpec((width, tile), lambda i: (0, of(i))),
            pl.BlockSpec((1, tile), lambda i: (0, of(i))),
            pl.BlockSpec((tile, width), lambda i: (of(i), 0)),
        ]

    scratch = []
    for _ in range(steps):
        scratch += Group.scratch(2 * tile, width, dp)
    return pl.pallas_call(
        functools.partial(feed_kernel, chunk=min(256, seq_len), dp=dp),
        grid=(2 * steps,),
        in_specs=[whole_rows, whole_rows] + weights(far) + weights(own),
        out_specs=[
            whole_rows,
            whole_rows,
            pl.BlockSpec((dp, 1, size, width), lambda i: (0, own(i), 0, 0)),
            pl.BlockSpec((1, tile), lambda i: (0, far(i))),
            pl.BlockSpec((1, tile), lambda i: (0, own(i))),
            whole((steps, size, width)),
        ],
        out_shape=[
            jax.ShapeDtypeStruct((seq_len, width), f32),
            jax.ShapeDtypeStruct((seq_len, width), f32),
            jax.ShapeDtypeStruct((dp, steps, size, width), bf16),
            jax.ShapeDtypeStruct((1, hidden), f32),
            jax.ShapeDtypeStruct((1, hidden), f32),
            jax.ShapeDtypeStruct((steps, size, width), bf16),
        ],
        scratch_shapes=[
            pltpu.VMEM((seq_len, tile), bf16),
            pltpu.VMEM((seq_len, tile), bf16),
            pltpu.VMEM((steps, 2 * tile, width), bf16),
            pltpu.VMEM((steps, size, width), bf16),
            pltpu.VMEM((steps, size, width), bf16),
            pltpu.SemaphoreType.DMA((2, steps)),
        ]
        + scratch,
        compiler_params=remote_params(1),
        cost_estimate=cost(45),
        name="feed",
    )(h, gf, e_far, b_far, s_far, e_own, b_own, s_own)


def three_parts(values):
    first = values.astype(bf16).astype(f32)
    rest = values - first
    second = rest.astype(bf16).astype(f32)
    return first, second, rest - second


def attend_back(length, qkv, o, lse, go, acc_ref, seq, pair, local, block, between):
    seq_len = qkv.shape[1]
    scale = HD**-0.5

    def columns(part):
        return pl.ds(pl.multiple_of(part * local + pair * PAIR, PAIR), PAIR)

    lane = lane_index(seq_len)
    position = lax.broadcasted_iota(jnp.int32, (seq_len, PAIR), 0)
    inside = position < length
    key_bias = jnp.where(inside, 0.0, masked_fill)
    row, column = causal_block(block)
    keep = row <= column
    q = qkv[seq, :, columns(0)]
    k = qkv[seq, :, columns(1)]
    v = qkv[seq, :, columns(2)]
    grad_o = go[seq, :, columns(0)]
    q_wide = q.astype(f32) * scale
    k_wide = k.astype(f32)
    v_wide = v.astype(f32)
    go_wide = grad_o.astype(f32)
    both = go_wide * o[:, columns(0)].astype(f32)
    lse_parts = three_parts(-lse[:, columns(0)])
    low = lane < HD
    zero = jnp.zeros_like(q)
    acc_ref[...] = jnp.zeros_like(acc_ref)
    count = seq_len // block
    grads_k = [None] * count
    grads_v = [None] * count
    for head in range(2):
        mine = low if head == 0 else jnp.logical_not(low)
        spare = HD if head == 0 else 0
        delta = jnp.sum(jnp.where(mine, both, 0.0), axis=-1, keepdims=True)
        delta_parts = three_parts(-jnp.broadcast_to(delta, (seq_len, PAIR)))

        def extras(parts):
            return jnp.where(
                lane == spare + 1,
                parts[0],
                jnp.where(lane == spare + 2, parts[1], jnp.where(lane == spare + 3, parts[2], 0.0)),
            )

        ones = jnp.where((lane > spare) & (lane < spare + 4), 1.0, 0.0)
        q_aug = jnp.where(mine, q_wide, jnp.where(lane == spare, 1.0, extras(lse_parts))).astype(bf16)
        k_aug = jnp.where(mine, k_wide, jnp.where(lane == spare, key_bias, ones)).astype(bf16)
        v_aug = jnp.where(mine, v_wide, ones).astype(bf16)
        go_aug = jnp.where(mine, go_wide, extras(delta_parts)).astype(bf16)
        q_own = jnp.where(mine, q, zero)
        k_own = jnp.where(mine, k, zero)
        go_own = jnp.where(mine, grad_o, zero)
        for index in range(count):
            start, end = index * block, (index + 1) * block
            scores = dot_nt(k_aug[start:end], q_aug[start:])
            first = jnp.where(keep, scores[:, :block], masked_fill)
            if index + 1 < count:
                scores = jnp.concatenate([first, scores[:, block:]], axis=1)
            else:
                scores = first
            shares = jnp.exp(scores)
            moved = dot_nt(v_aug[start:end], go_aug[start:])
            grad_scores = (shares * moved).astype(bf16)
            grad_v = dot_nn(shares.astype(bf16), go_own[start:])
            grad_k = dot_nn(grad_scores, q_own[start:])
            grads_v[index] = grad_v if head == 0 else grads_v[index] + grad_v
            grads_k[index] = grad_k if head == 0 else grads_k[index] + grad_k
            acc_ref[start:, :] += dot_tn(grad_scores, k_own[start:end])
        between(head)
    qkv[seq, :, columns(0)] = (acc_ref[...] * scale).astype(bf16)
    qkv[seq, :, columns(1)] = (jnp.concatenate(grads_k, axis=0) * scale).astype(bf16)
    qkv[seq, :, columns(2)] = jnp.where(inside, jnp.concatenate(grads_v, axis=0), 0.0).astype(bf16)


def back_kernel(
    len_ref, sums_in, db_own, db_far, shift_mlp, gain_two, w_out, w_far, gain_ref, shift_ref,
    cot, resid, f_sum, gh_sum, tokens, qkv_first, qkv_second, h_first, h_second,
    o_keep, o_sent, lse_keep, lse_sent, o_keep_second, o_sent_second, lse_keep_second, lse_sent_second,
    got_first, got_second, weight, feed_own, feed_far,
    result_out, feed_out, more_out, query_out, last_out, input_out,
    load_sems, y_sems, block_sems, cot_buf, wide_bufs, result_buf, go_send, sums, gain_acc,
    qkv, o, lse, go, ga, mixed, h, w, acc_ref, row_send, row_got,
    feed_far_shard, feed_shard, more_shard, more_got, query_shard, last_shard, tile_send, tile_got,
    feed_acc, far_local, own_local, query_local, last_local, *rest, dp
):
    rest = list(rest)

    def take(count):
        taken = rest[:count]
        del rest[:count]
        return taken

    half, width = got_first.shape[0], tokens.shape[2]
    seq_len = 2 * half
    local = qkv.shape[2] // 3
    pairs = local // PAIR
    block = min(256, half)
    ring = Ring(dp)
    here = ring.tensor
    there = 1 - here
    feed_group = Group(ring, feed_own, feed_acc, take(5))
    far_group = Group(ring, far_local, None, take(5))
    own_group = Group(ring, own_local, None, take(5))
    query_group = Group(ring, query_local, None, take(5))
    last_group = Group(ring, last_local, None, take(5))
    feed_spread = Spread(ring, feed_out, take(2))
    more_spread = Spread(ring, more_out, take(2))
    query_spread = Spread(ring, query_out, take(2))
    last_spread = Spread(ring, last_out, take(2))

    def load(source, target, number):
        return pltpu.make_async_copy(source, target, load_sems.at[number])

    rows_here = pl.ds(pl.multiple_of(here * half, 16), half)
    rows_there = pl.ds(pl.multiple_of(there * half, 16), half)
    front, rear = pl.ds(0, half), pl.ds(half, half)
    mixed_loads = [
        load(o_keep, mixed.at[0, front], 1),
        load(o_keep_second, mixed.at[0, rear], 2),
        load(got_first, mixed.at[1, front], 3),
        load(got_second, mixed.at[1, rear], 4),
    ]
    first_loads = [
        load(qkv_first, qkv.at[0], 5),
        load(o_keep, o.at[rows_here], 6),
        load(o_sent, o.at[rows_there], 7),
        load(lse_keep, lse.at[rows_here], 8),
        load(lse_sent, lse.at[rows_there], 9),
    ]
    row_loads = [load(weight, w, 11)]
    second_loads = [load(qkv_second, qkv.at[1], 12)]
    late_loads = [load(h_first, h.at[0], 14), load(h_second, h.at[1], 15)]
    token_loads = [load(tokens.at[0], ga.at[front], 16), load(tokens.at[1], ga.at[rear], 17)]
    shard_load = load(feed_far, feed_far_shard, 18)
    reloads = [
        load(o_keep_second, o.at[rows_here], 19),
        load(o_sent_second, o.at[rows_there], 20),
        load(lse_keep_second, lse.at[rows_here], 21),
        load(lse_sent_second, lse.at[rows_there], 22),
    ]

    def cross(source, target, number):
        return send(source, target, y_sems, number, ring.partner())

    go_cross = [
        cross(go_send.at[front], go.at[0, rows_here], 0),
        cross(go_send.at[rear], go.at[1, rows_here], 1),
    ]
    go_landed = [
        cross(go_send.at[front], go.at[0, rows_there], 0),
        cross(go_send.at[rear], go.at[1, rows_there], 1),
    ]
    row_cross = [
        cross(row_send.at[0], row_got.at[0], 2),
        cross(row_send.at[1], row_got.at[1], 3),
    ]
    more_cross = cross(more_shard, more_got, 5)
    tile_cross = cross(tile_send, tile_got, 6)

    part = cot_buf.shape[1]
    parts = seq_len // part

    def fetch(index):
        slot = index % 2
        rows = pl.ds(pl.multiple_of(index * part, 16), part)
        copies = [pltpu.make_async_copy(cot.at[rows], cot_buf.at[slot], block_sems.at[slot, 0])]
        for number, source in enumerate((resid, f_sum, gh_sum)):
            copies.append(
                pltpu.make_async_copy(
                    source.at[rows], wide_bufs.at[slot, number], block_sems.at[slot, 1 + number]
                )
            )
        return copies

    def put(index):
        slot = index % 2
        rows = pl.ds(pl.multiple_of(index * part, 16), part)
        return pltpu.make_async_copy(result_buf.at[slot], result_out.at[rows], block_sems.at[slot, 6])

    def add(row, values):
        sums[row : row + 1] += jnp.sum(values, axis=0, keepdims=True)

    def turn(index):
        slot = index % 2
        for copy in fetch(index):
            copy.wait()

        @pl.when(index + 1 < parts)
        def _():
            for copy in fetch(index + 1):
                copy.start()

        @pl.when(index >= 2)
        def _():
            put(index - 2).wait()

        seq = index * part // half
        offset = index * part - seq * half
        rows = pl.ds(pl.multiple_of(offset, 16), part)
        flat = pl.ds(pl.multiple_of(index * part, 16), part)
        placed = pl.ds(pl.multiple_of(here * half + offset, 16), part)
        position = here * half + offset + lax.broadcasted_iota(jnp.int32, (part, 1), 0)
        valid = (position < len_ref[seq]).astype(f32)
        first = wide_bufs[slot, 0]
        mlp = wide_bufs[slot, 1] + shift_mlp[...]
        result = first + valid * mlp
        result_buf[slot] = result
        put(index).start()
        unit, inverse = normalized(first)
        grad_norm = valid * wide_bufs[slot, 2]
        grad = cot_buf[slot].astype(f32) + norm_back(unit, inverse, gain_two[...], grad_norm)
        input_out[seq, rows, :] = grad
        grad_attn = valid * grad
        low = grad_attn.astype(bf16)
        ga[flat, :] = low
        go_send[flat, :] = dot_nt(low, w_far[...]).astype(bf16)
        go[seq, placed, :] = dot_nt(low, w_out[...]).astype(bf16)
        add(0, grad_attn)
        add(1, grad_norm * unit)
        add(2, grad_norm)
        add(4, valid * result * result)
        add(6, valid * mlp * mlp)

        @pl.when(index == parts // 2 - 1)
        def _():
            go_cross[0].start()
            feed_group.load().wait()
            feed_group.both_steps(0, first=True)

    for copy in fetch(0):
        copy.start()
    feed_group.load().start()
    greet(ring.ahead(), ring.behind(), ring.sibling(), ring.partner())
    feed_group.hand_over()
    for copy in mixed_loads + first_loads + row_loads + second_loads + [shard_load] + late_loads:
        copy.start()
    sums[...] = jnp.zeros_like(sums)
    gain_acc[...] = jnp.zeros_like(gain_acc)
    loop(0, parts, turn)
    go_cross[1].start()
    feed_group.both_steps(1)
    put(parts - 2).wait()
    put(parts - 1).wait()

    lane = lax.broadcasted_iota(jnp.int32, (1, width), 1)
    count = jnp.zeros((1, width), f32)
    for start in range(0, half, width):
        position = here * half + lane + start
        for seq in range(2):
            count += ((lane + start < half) & (position < len_ref[seq])).astype(f32)
    sums[3:4] = sums_in[1:2]
    sums[5:6] = sums_in[0:1]
    sums[7:8] = count
    for copy in mixed_loads:
        copy.wait()
    tail = far_local.shape[0] - local - 16
    for target, index, small in ((far_local, 1, db_far), (own_local, 0, db_own)):
        target[pl.ds(0, local), :] = dot_tn(mixed[index], ga[...]).astype(bf16)
        target[pl.ds(local, 16), :] = jnp.concatenate([sums[0:8], small[...]], axis=0).astype(bf16)
        target[pl.ds(local + 16, tail), :] = jnp.zeros((tail, width), bf16)
    for copy in token_loads:
        copy.start()
    far_group.hand_over()
    own_group.hand_over()
    for copy in first_loads:
        copy.wait()
    go_landed[0].wait_recv()

    def store(spread, shard, number):
        copy = load(shard, spread.out.at[spread.place(ring.core, ring.spot)], number)
        copy.start()
        copy.wait()
        spread.begin()

    def feed_begin():
        shard_load.wait()
        value = feed_group.finish() + feed_far_shard[...].astype(f32)
        feed_shard[...] = value.astype(bf16)
        store(feed_spread, feed_shard, 0)

    def more_shard_cross():
        more_shard[...] = far_group.finish().astype(bf16)
        more_cross.start()

    def more_begin():
        value = own_group.finish()
        more_cross.wait_recv()
        more_cross.wait_send()
        more_shard[...] = (value + more_got[...].astype(f32)).astype(bf16)
        store(more_spread, more_shard, 10)

    def hop(group, step):
        if step == ring.far_hops - 1:
            group.far_step(step)
        else:
            group.both_steps(step, first=step == 0)

    def spread_step(spread, step):
        if step == ring.far_hops:
            spread.far_step(step, last=True)
        elif step == ring.near_hops:
            spread.close()
        else:
            spread.both_steps(step)

    def query_begin():
        query_shard[...] = query_group.finish().astype(bf16)
        store(query_spread, query_shard, 13)

    size = last_group.rows
    owner, offset = (3 * PAIR) // size, (3 * PAIR) % size
    mine = ring.core * ring.chips + ring.spot == owner
    tile_row = lax.broadcasted_iota(jnp.int32, (16, width), 0)

    def last_cross():
        value = last_group.finish()
        last_shard[...] = value.astype(bf16)
        tile_send[...] = value[offset : offset + 16].astype(bf16)
        tile_cross.start()

    def last_begin():
        tile_cross.wait_recv()
        added = jnp.where((tile_row < 2) & mine, tile_got[...].astype(f32), 0.0)
        rows = pl.ds(offset, 16)
        last_shard[rows, :] = (last_shard[rows, :].astype(f32) + added).astype(bf16)
        store(last_spread, last_shard, 13)

    def send_rows(seq):
        def one(index):
            rows = pl.ds(pl.multiple_of(index * block, 16), block)
            from_rows = pl.ds(pl.multiple_of(there * half + index * block, 16), block)
            row_send[seq, rows, :] = dot_nn(qkv[seq, from_rows, :], w[...]).astype(bf16)

        loop(0, half // block, one)
        row_cross[seq].start()

    def keep_rows(seq):
        row_cross[seq].wait_recv()

        def one(index):
            rows = pl.ds(pl.multiple_of(index * block, 16), block)
            from_rows = pl.ds(pl.multiple_of(here * half + index * block, 16), block)
            position = here * half + index * block
            position += lax.broadcasted_iota(jnp.int32, (block, 1), 0)
            grad = dot_nn(qkv[seq, from_rows, :], w[...]) + row_got[seq, rows, :].astype(f32)
            grad = jnp.where(position < len_ref[seq], grad, 0.0)
            x_rows = pl.ds(pl.multiple_of(seq * half + index * block, 16), block)
            unit, inverse = normalized(ga[x_rows, :].astype(f32))
            input_out[seq, rows, :] += norm_back(unit, inverse, gain_ref[...], grad)

        loop(0, half // block, one)

    def query_rows(pair):
        if pair == 0:
            for copy in late_loads + token_loads:
                copy.wait()
        for index in range(3):
            columns = pl.ds(index * local + pair * PAIR, PAIR)
            value = dot_tn(qkv[0, :, columns], h[0]) + dot_tn(qkv[1, :, columns], h[1])
            target = last_local if pair == pairs - 1 else query_local
            start = 0 if pair == pairs - 1 else 3 * pair * PAIR
            target[pl.ds(start + index * PAIR, PAIR), :] = value.astype(bf16)
            weighted = value * w[columns, :].astype(f32)
            gain_acc[0:1] += jnp.sum(weighted, axis=0, keepdims=True)
        if pair == pairs - 2:
            used = 3 * (pairs - 1) * PAIR
            if query_local.shape[0] > used:
                rows = query_local.shape[0] - used
                query_local[pl.ds(used, rows), :] = jnp.zeros((rows, width), bf16)
            query_group.hand_over()
        if pair == pairs - 1:
            rows = last_local.shape[0] - 3 * PAIR
            last_local[pl.ds(3 * PAIR, rows), :] = jnp.zeros((rows, width), bf16)
            ones = jnp.ones((16, seq_len), bf16)
            totals = dot_nn(ones, qkv[0]) + dot_nn(ones, qkv[1])
            high = totals.astype(bf16)
            low = (totals - high.astype(f32)).astype(bf16)
            shift_grad = (dot_nn(high, w[...]) + dot_nn(low, w[...]))[0:1]
            gain_grad = (gain_acc[0:1] - shift_ref[...] * shift_grad) / gain_ref[...]
            biases = jnp.concatenate([totals[0:1, :local], totals[0:1, 2 * local :]], axis=1)
            last = jnp.where(tile_row == 2, biases, 0.0)
            last = jnp.where(tile_row == 1, shift_grad, last)
            last = jnp.where(tile_row == 0, gain_grad, last)
            last_local[pl.ds(3 * PAIR, 16), :] = last.astype(bf16)
            last_group.hand_over()

    plan = {}

    def chain(tick, *actions):
        for number, action in enumerate(actions):
            if action is not None:
                plan.setdefault(tick + number, []).append(action)

    def hops(first, *groups):
        def one(step):
            for group in groups:
                hop(group, step)

        return [functools.partial(one, step) for step in range(first, ring.far_hops)]

    def spreads(spread):
        steps = range(1, ring.far_hops + 1)
        return [functools.partial(spread_step, spread, step) for step in steps]

    ticks = [1, 4, 7, 9, 11]
    free = len(ticks)
    chain(0, *hops(2, feed_group), feed_begin, *spreads(feed_spread))
    chain(0, *hops(0, far_group, own_group), more_shard_cross, more_begin, *spreads(more_spread))
    chain(free - 1, *hops(0, query_group), query_begin, *spreads(query_spread))
    chain(free, functools.partial(send_rows, 1), functools.partial(keep_rows, 0))
    plan[free].insert(0, plan[free].pop())
    chain(free, *hops(0, last_group), last_cross)
    chain(free + ring.far_hops, functools.partial(keep_rows, 1))
    chain(free + ring.far_hops, last_begin, *spreads(last_spread))

    def attention(index):
        seq = index // pairs
        pair = index % pairs

        @pl.when(index == pairs)
        def _():
            for copy in reloads:
                copy.start()
            for copy in row_loads:
                copy.wait()
            send_rows(0)
            for copy in second_loads + reloads:
                copy.wait()
            go_landed[1].wait_recv()

        def between(head):
            for tick, slot in enumerate(ticks):
                if slot % 2 == head:

                    @pl.when(index == slot // 2)
                    def _():
                        for action in plan[tick]:
                            action()

        attend_back(len_ref[seq], qkv, o, lse, go, acc_ref, seq, pair, local, block, between)
        for number in range(pairs):
            pl.when(index == pairs + number)(functools.partial(query_rows, number))

    loop(0, 2 * pairs, attention)
    for number in sorted(plan):
        if number >= free:
            for action in plan[number]:
                action()
    for group in (feed_group, far_group, own_group, query_group, last_group):
        group.sent()
    for copy in go_cross + row_cross + [tile_cross]:
        copy.wait_send()
    for spread in (feed_spread, more_spread, query_spread, last_spread):
        spread.sent()


def back(
    lens, sums, db_own, db_far, shift_mlp, gain_two, w_out, w_far, gain, shift, rows, tokens, qkvs, hs,
    attended, gots, weight, feed_own, feed_far, dp
):
    _, half, width = tokens.shape
    seq_len = 2 * half
    columns = weight.shape[0]
    local = columns // 3
    pairs = local // PAIR
    feed_rows = feed_own.shape[0]
    more_rows = padded(local + 32, dp)
    query_rows = padded(3 * (pairs - 1) * PAIR, dp)
    last_rows = padded(3 * PAIR + 32, dp)
    anywhere = pl.BlockSpec(memory_space=pl.ANY)
    inside = pl.BlockSpec(memory_space=pltpu.VMEM)
    feed_size, more_size, query_size = feed_rows // dp, more_rows // dp, query_rows // dp
    last_size = last_rows // dp
    both_rows = pltpu.VMEM((2, half, width), bf16)
    part = min(128, half)
    return pl.pallas_call(
        functools.partial(back_kernel, dp=dp),
        in_specs=[pl.BlockSpec(memory_space=pltpu.SMEM)] + [inside] * 9 + [anywhere] * 22,
        out_specs=[anywhere] * 5 + [inside],
        out_shape=[
            jax.ShapeDtypeStruct((seq_len, width), f32),
            jax.ShapeDtypeStruct((feed_rows, width), bf16),
            jax.ShapeDtypeStruct((more_rows, width), bf16),
            jax.ShapeDtypeStruct((query_rows, width), bf16),
            jax.ShapeDtypeStruct((last_rows, width), bf16),
            jax.ShapeDtypeStruct((2, half, width), f32),
        ],
        scratch_shapes=[
            pltpu.SemaphoreType.DMA((23,)),
            pltpu.SemaphoreType.DMA((2, 7)),
            pltpu.SemaphoreType.DMA((2, 7)),
            pltpu.VMEM((2, part, width), bf16),
            pltpu.VMEM((2, 3, part, width), f32),
            pltpu.VMEM((2, part, width), f32),
            pltpu.VMEM((seq_len, local), bf16),
            pltpu.VMEM((8, width), f32),
            pltpu.VMEM((8, width), f32),
            pltpu.VMEM((2, seq_len, columns), bf16),
            pltpu.VMEM((seq_len, local), bf16),
            pltpu.VMEM((seq_len, local), f32),
            pltpu.VMEM((2, seq_len, local), bf16),
            pltpu.VMEM((seq_len, width), bf16),
            pltpu.VMEM((2, seq_len, local), bf16),
            pltpu.VMEM((2, seq_len, width), bf16),
            pltpu.VMEM((columns, width), bf16),
            pltpu.VMEM((seq_len, PAIR), f32),
            both_rows,
            both_rows,
            pltpu.VMEM((feed_size, width), bf16),
            pltpu.VMEM((feed_size, width), bf16),
            pltpu.VMEM((more_size, width), bf16),
            pltpu.VMEM((more_size, width), bf16),
            pltpu.VMEM((query_size, width), bf16),
            pltpu.VMEM((last_size, width), bf16),
            pltpu.VMEM((16, width), bf16),
            pltpu.VMEM((16, width), bf16),
            pltpu.VMEM((feed_rows // 2, width), bf16),
            pltpu.VMEM((more_rows, width), bf16),
            pltpu.VMEM((more_rows, width), bf16),
            pltpu.VMEM((query_rows, width), bf16),
            pltpu.VMEM((last_rows, width), bf16),
        ]
        + Group.scratch(feed_rows, width, dp)
        + Group.scratch(more_rows, width, dp)
        + Group.scratch(more_rows, width, dp)
        + Group.scratch(query_rows, width, dp)
        + Group.scratch(last_rows, width, dp)
        + Spread.scratch(dp) * 4,
        compiler_params=remote_params(2),
        cost_estimate=cost(90),
        name="back",
    )(
        lens, sums, db_own, db_far, shift_mlp, gain_two, w_out, w_far, gain, shift, *rows, tokens, *qkvs,
        *hs, *attended, *gots, weight, feed_own, feed_far,
    )


def lay_out_kernel(
    e_ref, s_ref, out_ref, q_ref, last_ref, result_ref, input_ref, e_out, s_out, o_out, a_out, r_out, i_out, *, local
):
    flat = s_out.shape
    e_out[...] = e_ref[...].reshape(flat).astype(f32).T
    s_out[...] = s_ref[...].reshape(flat).astype(f32)
    o_out[...] = out_ref[...].astype(f32)
    r_out[...] = result_ref[...]
    i_out[...] = input_ref[...]
    step = pl.program_id(0)
    pairs = local // PAIR
    for part in range(3):
        for pair in range(pairs):

            @pl.when(step == part * pairs + pair)
            def _():
                source = last_ref if pair == pairs - 1 else q_ref
                start = (0 if pair == pairs - 1 else 3 * pair * PAIR) + part * PAIR
                value = source[start : start + PAIR, :].astype(f32).T
                a_out[part, :, pair * PAIR : (pair + 1) * PAIR] = value


def lay_out(feed_sum, more_sum, query_sum, last_sum, result, grad, hidden, local):
    chunks, tiles, feed_size, width = feed_sum.shape
    steps = hidden // PAIR
    turns = steps // tiles
    group = PAIR // feed_size
    rows = result.shape[0]
    size = rows * 3 // (2 * steps)
    blocks = rows // size
    proj = local // steps

    def some(i):
        return jnp.minimum(i, blocks - 1), 0

    return pl.pallas_call(
        functools.partial(lay_out_kernel, local=local),
        grid=(steps,),
        in_specs=[
            pl.BlockSpec((group, 1, feed_size, width), lambda i: (i % turns, i // turns, 0, 0)),
            pl.BlockSpec(
                (group, 1, feed_size, width), lambda i: (i % turns + turns, i // turns, 0, 0)
            ),
            pl.BlockSpec((proj, width), lambda i: (i, 0)),
            whole(query_sum.shape),
            whole(last_sum.shape),
            pl.BlockSpec((size, width), some),
            pl.BlockSpec((size, width), some),
        ],
        out_specs=[
            pl.BlockSpec((width, PAIR), lambda i: (0, i)),
            pl.BlockSpec((PAIR, width), lambda i: (i, 0)),
            pl.BlockSpec((proj, width), lambda i: (i, 0)),
            whole((3, width, local)),
            pl.BlockSpec((size, width), some),
            pl.BlockSpec((size, width), some),
        ],
        out_shape=[
            jax.ShapeDtypeStruct((width, hidden), f32),
            jax.ShapeDtypeStruct((hidden, width), f32),
            jax.ShapeDtypeStruct((local, width), f32),
            jax.ShapeDtypeStruct((3, width, local), f32),
            jax.ShapeDtypeStruct((rows, width), f32),
            jax.ShapeDtypeStruct((rows, width), f32),
        ],
        compiler_params=params(),
        cost_estimate=cost(10),
        name="lay_out",
    )(feed_sum, feed_sum, more_sum, query_sum, last_sum, result, grad)


def body(
    tokens,
    lengths,
    layer_index,
    norm_one_gain,
    norm_one_bias,
    attend_weight,
    query_bias,
    value_bias,
    output_weight,
    output_bias,
    norm_two_gain,
    norm_two_bias,
    expand_weight,
    expand_bias,
    shrink_weight,
    shrink_bias,
    cotangent,
):
    seq_dev, half, width = tokens.shape
    dp = lax.axis_size("dp")
    here = lax.axis_index("tensor")
    there = 1 - here
    place = lax.axis_index("dp")

    def exchange(values):
        return lax.ppermute(values, "tensor", [(0, 1), (1, 0)])

    def layer(stack):
        return select_layer(stack, layer_index)

    def wide(stack):
        return layer(stack).astype(f32)[None]

    def after(values, earlier):
        return lax.optimization_barrier((values, earlier))[0]

    def share(stack):
        rows = stack.shape[1] // dp
        piece = lax.dynamic_slice(
            stack, (layer_index[0], place * rows, 0), (1, rows, stack.shape[2])
        )
        return piece[0]

    def gather(piece):
        return lax.all_gather(piece, "dp", axis=0, tiled=False)

    out_mat = layer(output_weight)
    hidden = expand_weight.shape[2]
    proj_rows = out_mat.shape[0] // dp
    pieces = [
        tokens[0],
        jnp.concatenate([share(output_weight), share(shrink_weight)], axis=0),
        share(expand_weight),
    ]
    pieces = lax.optimization_barrier(pieces)
    token_got = [exchange(pieces[0])]
    first_got = exchange(pieces[1])
    expand_got = exchange(pieces[2])
    token_got.append(exchange(after(tokens[1], token_got[0])))
    first_all = gather(first_got)
    out_far = first_all[:, :proj_rows].reshape(out_mat.shape)
    shrink_far = first_all[:, proj_rows:].reshape(hidden, width)
    expand_far = gather(expand_got).reshape(width, hidden)
    expand_shift_far = exchange(after(layer(expand_bias), token_got[0]))[None].astype(f32)

    sides = jnp.stack([here, there]).astype(jnp.int32)

    def at(side, seq):
        return jnp.stack([sides[side], lengths[seq]])

    at_rows = jnp.concatenate([sides[:1], lengths])
    gain_one, shift_one = wide(norm_one_gain), wide(norm_one_bias)
    gain_two, shift_two = wide(norm_two_gain), wide(norm_two_bias)
    attend_flat = layer(attend_weight).reshape(width, -1)
    local = attend_flat.shape[1] // 3
    qkv_bias = jnp.concatenate(
        [wide(query_bias), jnp.zeros((1, local), f32), wide(value_bias)], axis=1
    )

    hs, qkvs, attended, kept, gots = [], [], [], [], []
    for seq in range(seq_dev):
        h, qkv = project(
            at(0, seq), tokens[seq], token_got[seq], gain_one, shift_one, attend_flat, qkv_bias
        )
        o_sent, lse_sent = attend(at(1, seq), qkv, 7)
        gots.append(exchange(o_sent))
        o_keep, lse_keep = attend(at(0, seq), qkv, 7)
        hs.append(h)
        qkvs.append(qkv)
        kept.append(o_keep)
        attended += [o_keep, o_sent, lse_keep, lse_sent]

    x_rows = tokens.reshape(-1, width)
    cot = cotangent.reshape(-1, width)
    h_two, gf, resid, sums = resid_norm(
        at_rows, x_rows, cot, *kept, *gots, out_mat, out_far, wide(output_bias), gain_two, shift_two
    )
    span = min(dp, 16)
    f_sum, gh_sum, grads_own, db_far, db_own, feed_far = feed(
        h_two, gf, expand_far, expand_shift_far, shrink_far, layer(expand_weight), wide(expand_bias),
        layer(shrink_weight), span,
    )

    def bias_rows(grad):
        count = hidden // width
        return jnp.pad(grad.reshape(count, width), ((0, 8 - count), (0, 0)))

    result, feed_sum, more_sum, query_sum, last_sum, input_grad = back(
        lengths, sums, bias_rows(db_own), bias_rows(db_far), wide(shrink_bias), gain_two, out_mat,
        out_far, gain_one, shift_one, (cot, resid, f_sum, gh_sum), tokens, qkvs, hs,
        attended, gots, attend_flat.T, grads_own.reshape(-1, width), feed_far.reshape(-1, width), span,
    )
    if dp > span:
        spans = [[base + index for base in range(0, dp, span)] for index in range(span)]
        feed_sum, more_sum, query_sum, last_sum = (
            lax.psum(part.astype(f32), "dp", axis_index_groups=spans)
            for part in (feed_sum, more_sum, query_sum, last_sum)
        )

    expand_grad, shrink_grad, out_grad, attend_grad, result, input_grad = lay_out(
        feed_sum.reshape(grads_own.shape), more_sum, query_sum, last_sum, result,
        input_grad.reshape(-1, width), hidden, local,
    )
    proj = out_mat.shape[0]
    small = more_sum[proj : proj + 16].astype(f32)
    last = last_sum[3 * PAIR : 3 * PAIR + 16].astype(f32)
    squares = jnp.sum(small[4:8], axis=1)
    rms_values = jnp.sqrt(squares[:3] / (squares[3] * width))
    return (
        result.reshape(tokens.shape),
        input_grad.reshape(tokens.shape),
        last[0],
        last[1],
        attend_grad.transpose(1, 0, 2),
        last[2, :local],
        last[2, local:],
        out_grad,
        small[0],
        small[1],
        small[2],
        expand_grad,
        small[8 : 8 + hidden // width].reshape(hidden),
        shrink_grad,
        small[3],
        rms_values,
    )


def solution(mesh):
    in_specs = (
        P("dp", "tensor", None),
        P("dp"),
        P(),
        P(),
        P(),
        P(None, None, None, "tensor"),
        P(None, "tensor"),
        P(None, "tensor"),
        P(None, "tensor", None),
        P(),
        P(),
        P(),
        P(None, None, "tensor"),
        P(None, "tensor"),
        P(None, "tensor", None),
        P(),
        P("dp", "tensor", None),
    )
    out_specs = (
        P("dp", "tensor", None),
        P("dp", "tensor", None),
        P(),
        P(),
        P(None, None, "tensor"),
        P("tensor"),
        P("tensor"),
        P("tensor", None),
        P(),
        P(),
        P(),
        P(None, "tensor"),
        P("tensor"),
        P("tensor", None),
        P(),
        P(),
    )
    return jax.shard_map(body, mesh=mesh, in_specs=in_specs, out_specs=out_specs, check_vma=False)
```

```python
import functools

import jax
import jax.numpy as jnp
from jax import lax
from jax.experimental import pallas as pl
from jax.experimental.pallas import tpu as pltpu
from jax.sharding import PartitionSpec as P

HD = 64
PAIR = 2 * HD
epsilon = 1e-05
masked_fill = -1e30
VMEM_LIMIT = 56 * 1024 * 1024
f32 = jnp.float32
bf16 = jnp.bfloat16


def dot_nn(left, right):
    return lax.dot_general(left, right, (((1,), (0,)), ((), ())), preferred_element_type=f32)


def dot_nt(left, right):
    return lax.dot_general(left, right, (((1,), (1,)), ((), ())), preferred_element_type=f32)


def dot_tn(left, right):
    return lax.dot_general(left, right, (((0,), (0,)), ((), ())), preferred_element_type=f32)


def select_layer(stack, layer_index):
    return lax.dynamic_index_in_dim(stack, layer_index[0], 0, keepdims=False)


def whole(shape):
    return pl.BlockSpec(shape, lambda *index: (0,) * len(shape))


def params():
    return pltpu.CompilerParams(dimension_semantics=("arbitrary",), vmem_limit_bytes=VMEM_LIMIT)


def remote_params(number):
    return pltpu.CompilerParams(
        collective_id=number, has_side_effects=True, vmem_limit_bytes=VMEM_LIMIT
    )


def cost(microseconds):
    return pl.CostEstimate(
        flops=int(microseconds * 1e9), bytes_accessed=int(microseconds * 3e6), transcendentals=0
    )


def normalized(x):
    center = jnp.mean(x, axis=-1, keepdims=True)
    x = x - center
    inverse = lax.rsqrt(jnp.mean(x * x, axis=-1, keepdims=True) + epsilon)
    return x * inverse, inverse


def norm_back(unit, inverse, gain, grad):
    scaled = grad * gain
    return inverse * (
        scaled
        - jnp.mean(scaled, axis=-1, keepdims=True)
        - unit * jnp.mean(scaled * unit, axis=-1, keepdims=True)
    )


class Halves:
    def __init__(self, half, block):
        self.count = half // block
        self.block = block

    def mine(self, i, at):
        return jnp.minimum(i, self.count - 1), 0

    def got(self, i, at):
        return jnp.maximum(i - self.count, 0), 0

    def whole(self, i, at):
        first = i < self.count
        side = jnp.where(first, at[0], 1 - at[0])
        return side * self.count + jnp.where(first, i, i - self.count), 0

    def position(self, at):
        i = pl.program_id(0)
        return self.whole(i, at)[0] * self.block + lax.broadcasted_iota(
            jnp.int32, (self.block, 1), 0
        )

    def pick(self, mine, got):
        return jnp.where(pl.program_id(0) < self.count, mine[...], got[...]).astype(f32)

    def specs(self, width, kind):
        return pl.BlockSpec((self.block, width), getattr(self, kind))


def fixed(shape):
    return pl.BlockSpec(shape, lambda i, at: (0,) * len(shape))


def project_kernel(at, mine, got, gain_ref, shift_ref, weight_ref, bias_ref, h_ref, qkv_ref, *, halves):
    unit, _ = normalized(halves.pick(mine, got))
    h = unit * gain_ref[...] + shift_ref[...]
    h = jnp.where(halves.position(at) < at[1], h, 0.0).astype(bf16)
    h_ref[...] = h
    local = weight_ref.shape[2]
    for part in range(3):
        columns = slice(part * local, (part + 1) * local)
        value = dot_nn(h, weight_ref[part]) + bias_ref[:, columns]
        qkv_ref[:, columns] = value.astype(bf16)


def project(at, mine, got, gain, shift, weight, bias):
    half, width = mine.shape
    columns = 3 * weight.shape[2]
    halves = Halves(half, min(256, half))
    return pl.pallas_call(
        functools.partial(project_kernel, halves=halves),
        grid_spec=pltpu.PrefetchScalarGridSpec(
            num_scalar_prefetch=1,
            grid=(2 * halves.count,),
            in_specs=[
                halves.specs(width, "mine"),
                halves.specs(width, "got"),
                fixed((1, width)),
                fixed((1, width)),
                fixed(weight.shape),
                fixed((1, columns)),
            ],
            out_specs=[halves.specs(width, "whole"), halves.specs(columns, "whole")],
        ),
        out_shape=[
            jax.ShapeDtypeStruct((2 * half, width), bf16),
            jax.ShapeDtypeStruct((2 * half, columns), bf16),
        ],
        compiler_params=params(),
        cost_estimate=cost(7),
        name="project",
    )(at, mine, got, gain, shift, weight, bias)


def lane_index(rows):
    return lax.broadcasted_iota(jnp.int32, (rows, PAIR), 1)


def causal_block(block):
    row = lax.broadcasted_iota(jnp.int32, (block, block), 0)
    column = lax.broadcasted_iota(jnp.int32, (block, block), 1)
    return row, column


def attend_kernel(at, q_ref, k_ref, v_ref, o_ref, lse_ref, *, block, half):
    seq_len = k_ref.shape[0]
    row, column = causal_block(block)
    keep = column <= row

    def query_half(side):
        end_all = (side + 1) * half
        lane = lane_index(end_all)
        lane_q = lane_index(half)
        position = lax.broadcasted_iota(jnp.int32, (end_all, PAIR), 0)
        key_bias = jnp.where(position < at[1], 0.0, masked_fill)
        q = q_ref[...].astype(f32) * (HD**-0.5)
        k = k_ref[:end_all, :].astype(f32)
        values = v_ref[:end_all, :]
        low = lane < HD
        low_q = lane_q < HD
        outs = []
        stats = []
        for head in range(2):
            mine = low if head == 0 else jnp.logical_not(low)
            mine_q = low_q if head == 0 else jnp.logical_not(low_q)
            spare = HD if head == 0 else 0
            q_aug = jnp.where(mine_q, q, jnp.where(lane_q == spare, 1.0, 0.0)).astype(bf16)
            k_aug = jnp.where(mine, k, jnp.where(lane == spare, key_bias, 0.0)).astype(bf16)
            v_own = jnp.where(mine, values, jnp.zeros_like(values))
            pieces = []
            notes = []
            for index in range(half // block):
                start = side * half + index * block
                end = start + block
                scores = dot_nt(q_aug[index * block : (index + 1) * block], k_aug[:end])
                last = jnp.where(keep, scores[:, start:end], masked_fill)
                scores = jnp.concatenate([scores[:, :start], last], axis=1) if start else last
                top = jnp.max(scores, axis=-1, keepdims=True)
                weights = jnp.exp(scores - top)
                total = jnp.sum(weights, axis=-1, keepdims=True)
                mixed = dot_nn(weights.astype(bf16), v_own[:end])
                pieces.append(mixed * (1.0 / total))
                notes.append(jnp.broadcast_to(top + jnp.log(total), (block, PAIR)))
            outs.append(jnp.concatenate(pieces, axis=0))
            stats.append(jnp.concatenate(notes, axis=0))
        o_ref[...] = (outs[0] + outs[1]).astype(bf16)
        lse_ref[...] = jnp.where(low_q, stats[1], stats[0])

    for side in range(seq_len // half):
        pl.when(at[0] == side)(functools.partial(query_half, side))


def attend(at, qkv, microseconds):
    seq_len = qkv.shape[0]
    half = seq_len // 2
    width = qkv.shape[1] // 3
    pairs = width // PAIR

    def columns(part):
        return pl.BlockSpec((seq_len, PAIR), lambda i, at: (0, part * pairs + i))

    out = pl.BlockSpec((half, PAIR), lambda i, at: (0, i))
    return pl.pallas_call(
        functools.partial(attend_kernel, block=min(256, half), half=half),
        grid_spec=pltpu.PrefetchScalarGridSpec(
            num_scalar_prefetch=1,
            grid=(pairs,),
            in_specs=[
                pl.BlockSpec((half, PAIR), lambda i, at: (at[0], i)),
                columns(1),
                columns(2),
            ],
            out_specs=[out, out],
        ),
        out_shape=[
            jax.ShapeDtypeStruct((half, width), bf16),
            jax.ShapeDtypeStruct((half, width), f32),
        ],
        compiler_params=params(),
        cost_estimate=cost(microseconds),
        name="attend",
    )(at, qkv, qkv, qkv)


class Pair:
    def __init__(self, half, block):
        self.count = half // block
        self.block = block

    def first(self, i, at):
        return jnp.minimum(i, self.count - 1), 0

    def second(self, i, at):
        return jnp.maximum(i - self.count, 0), 0

    def both(self, i, at):
        return i, 0

    def valid(self, at):
        i = pl.program_id(0)
        second = (i >= self.count).astype(jnp.int32)
        start = (at[0] * self.count + i - second * self.count) * self.block
        position = start + lax.broadcasted_iota(jnp.int32, (self.block, 1), 0)
        return (position < jnp.where(i < self.count, at[1], at[2])).astype(f32)

    def pick(self, first, second):
        return jnp.where(pl.program_id(0) < self.count, first[...], second[...])

    def specs(self, width, kind):
        return pl.BlockSpec((self.block, width), getattr(self, kind))


def resid_kernel(
    at, x_ref, cot_ref, o_first, o_second, got_first, got_second, w_ref, w_far, shift_out, gain,
    shift, h_ref, gf_ref, resid_ref, sums_ref, *, pair
):
    valid = pair.valid(at)
    attn = (
        dot_nn(pair.pick(o_first, o_second), w_ref[...])
        + dot_nn(pair.pick(got_first, got_second), w_far[...])
        + shift_out[...]
    )
    resid = x_ref[...].astype(f32) + valid * attn
    resid_ref[...] = resid
    unit, _ = normalized(resid)
    h_ref[...] = (valid * (unit * gain[...] + shift[...])).astype(bf16)
    gf = valid * cot_ref[...].astype(f32)
    gf_ref[...] = gf.astype(bf16)

    @pl.when(pl.program_id(0) == 0)
    def _():
        sums_ref[...] = jnp.zeros_like(sums_ref)

    sums_ref[0:1] += jnp.sum(valid * attn * attn, axis=0, keepdims=True)
    sums_ref[1:2] += jnp.sum(gf, axis=0, keepdims=True)


def resid_norm(at, x, cot, o_first, o_second, got_first, got_second, w, w_far, shift_out, gain, shift):
    rows, width = x.shape
    local = o_first.shape[1]
    pair = Pair(rows // 2, min(256, rows // 2))
    return pl.pallas_call(
        functools.partial(resid_kernel, pair=pair),
        grid_spec=pltpu.PrefetchScalarGridSpec(
            num_scalar_prefetch=1,
            grid=(2 * pair.count,),
            in_specs=[
                pair.specs(width, "both"),
                pair.specs(width, "both"),
                pair.specs(local, "first"),
                pair.specs(local, "second"),
                pair.specs(local, "first"),
                pair.specs(local, "second"),
                fixed((local, width)),
                fixed((local, width)),
                fixed((1, width)),
                fixed((1, width)),
                fixed((1, width)),
            ],
            out_specs=[pair.specs(width, "both")] * 3 + [fixed((8, width))],
        ),
        out_shape=[
            jax.ShapeDtypeStruct((rows, width), bf16),
            jax.ShapeDtypeStruct((rows, width), bf16),
            jax.ShapeDtypeStruct((rows, width), f32),
            jax.ShapeDtypeStruct((8, width), f32),
        ],
        compiler_params=params(),
        cost_estimate=cost(8),
        name="resid_norm",
    )(at, x, cot, o_first, o_second, got_first, got_second, w, w_far, shift_out, gain, shift)


class Ring:
    def __init__(self, dp):
        self.chips = dp // 2
        self.far_hops = self.chips // 2
        self.near_hops = self.chips - 1 - self.far_hops
        place = lax.axis_index("dp")
        self.tensor = lax.axis_index("tensor")
        self.base = place // dp * dp
        place = place % dp
        self.core = place % 2
        chip = place // 2
        depth = chip // 2
        self.spot = depth + (chip % 2) * (self.chips - 1 - 2 * depth)
        self.turn = 1 - 2 * self.core

    def device(self, spot, core):
        spot = (spot + self.chips) % self.chips
        side = spot // (self.chips // 2)
        chip = 2 * (spot + side * (self.chips - 1 - 2 * spot)) + side
        return (self.base + chip * 2 + core, self.tensor)

    def ahead(self):
        return self.device(self.spot + self.turn, self.core)

    def behind(self):
        return self.device(self.spot - self.turn, self.core)

    def sibling(self):
        return self.device(self.spot, 1 - self.core)

    def partner(self):
        return (lax.axis_index("dp"), 1 - self.tensor)

    def chunk(self, offset):
        return (self.spot + self.turn * offset + 2 * self.chips) % self.chips


def send(source, target, sems, index, device):
    copy = pltpu.make_async_remote_copy(
        src_ref=source,
        dst_ref=target,
        send_sem=sems.at[0, index],
        recv_sem=sems.at[1, index],
        device_id=device,
        device_id_type=pl.DeviceIdType.MESH,
    )
    return copy


def loop(start, stop, step):
    def run(index, carry):
        step(index)
        return carry

    lax.fori_loop(start, stop, run, 0)


class Group:
    def __init__(self, ring, source, acc, scratch):
        self.ring = ring
        self.source = source
        self.acc = acc
        self.pair, self.slots, self.pair_sems, self.ring_sems, self.load_sem = scratch
        self.rows = source.shape[0] // (2 * ring.chips)

    @staticmethod
    def scratch(rows, width, dp):
        chips = dp // 2
        size = rows // (2 * chips)
        return [
            pltpu.VMEM((chips, size, width), bf16),
            pltpu.VMEM((chips - 1, size, width), bf16),
            pltpu.SemaphoreType.DMA((2, chips)),
            pltpu.SemaphoreType.DMA((2, chips - 1)),
            pltpu.SemaphoreType.DMA((1,)),
        ]

    def place(self, core, chunk):
        start = (core * self.ring.chips + chunk) * self.rows
        return pl.ds(pl.multiple_of(start, 16), self.rows)

    def mine(self, chunk):
        if self.acc is None:
            return self.source.at[self.place(self.ring.core, chunk)]
        return self.acc.at[pl.ds(pl.multiple_of(chunk * self.rows, 16), self.rows)]

    def load(self):
        count = self.rows * self.ring.chips
        start = pl.multiple_of(self.ring.core * count, 16)
        return pltpu.make_async_copy(
            self.source.at[pl.ds(start, count)], self.acc, self.load_sem.at[0]
        )

    def to_sibling(self, chunk):
        source = self.source.at[self.place(1 - self.ring.core, chunk)]
        return send(source, self.pair.at[chunk], self.pair_sems, chunk, self.ring.sibling())

    def hand_over(self):
        ring = self.ring

        def both(step):
            self.to_sibling(ring.chunk(step - ring.far_hops)).start()
            self.to_sibling(ring.chunk(ring.near_hops - step)).start()

        loop(0, ring.near_hops, both)
        self.to_sibling(ring.chunk(-1)).start()
        self.to_sibling(ring.chunk(0)).start()

    def term(self, chunk):
        self.to_sibling(chunk).wait_recv()
        return self.mine(chunk)[...].astype(f32) + self.pair[chunk].astype(f32)

    def far_copy(self, step):
        chunk = self.ring.chunk(self.ring.far_hops - step)
        return send(
            self.mine(chunk), self.slots.at[step], self.ring_sems, step, self.ring.ahead()
        )

    def near_copy(self, step):
        slot = self.ring.far_hops + step
        chunk = self.ring.chunk(step - self.ring.near_hops)
        return send(
            self.mine(chunk), self.slots.at[slot], self.ring_sems, slot, self.ring.behind()
        )

    def far_step(self, step, first=False):
        chunk = self.ring.chunk(self.ring.far_hops - step)
        value = self.term(chunk)
        if not first:
            self.far_copy(step - 1).wait_recv()
            value += self.slots[step - 1].astype(f32)
        self.mine(chunk)[...] = value.astype(bf16)
        self.far_copy(step).start()

    def near_step(self, step, first=False):
        slot = self.ring.far_hops + step
        chunk = self.ring.chunk(step - self.ring.near_hops)
        value = self.term(chunk)
        if not first:
            self.near_copy(step - 1).wait_recv()
            value += self.slots[slot - 1].astype(f32)
        self.mine(chunk)[...] = value.astype(bf16)
        self.near_copy(step).start()

    def both_steps(self, step, first=False):
        self.far_step(step, first)
        self.near_step(step, first)

    def finish(self):
        ring = self.ring
        value = self.term(ring.chunk(0))
        self.far_copy(ring.far_hops - 1).wait_recv()
        self.near_copy(ring.near_hops - 1).wait_recv()
        value += self.slots[ring.far_hops - 1].astype(f32)
        return value + self.slots[ring.chips - 2].astype(f32)

    def sent(self):
        ring = self.ring
        loop(0, ring.chips, lambda chunk: self.to_sibling(chunk).wait_send())
        loop(0, ring.far_hops, lambda step: self.far_copy(step).wait_send())
        loop(0, ring.near_hops, lambda step: self.near_copy(step).wait_send())


class Spread:
    def __init__(self, ring, out, scratch):
        self.ring = ring
        self.out = out
        self.pair_sems, self.ring_sems = scratch
        self.rows = out.shape[0] // (2 * ring.chips)

    @staticmethod
    def scratch(dp):
        chips = dp // 2
        return [pltpu.SemaphoreType.DMA((2, chips)), pltpu.SemaphoreType.DMA((2, chips))]

    def place(self, core, chunk):
        start = (core * self.ring.chips + chunk) * self.rows
        return pl.ds(pl.multiple_of(start, 16), self.rows)

    def pass_on(self, chunk, slot, device):
        where = self.out.at[self.place(self.ring.core, chunk)]
        return send(where, where, self.ring_sems, slot, device)

    def to_sibling(self, chunk):
        where = self.out.at[self.place(self.ring.core, chunk)]
        return send(where, where, self.pair_sems, chunk, self.ring.sibling())

    def from_sibling(self, chunk):
        where = self.out.at[self.place(1 - self.ring.core, chunk)]
        return send(where, where, self.pair_sems, chunk, self.ring.sibling())

    def far_copy(self, step):
        return self.pass_on(self.ring.chunk(-step), step, self.ring.ahead())

    def near_copy(self, step):
        return self.pass_on(self.ring.chunk(step), self.ring.far_hops + step, self.ring.behind())

    def far_landed(self, step):
        return self.pass_on(self.ring.chunk(-step - 1), step, self.ring.ahead())

    def near_landed(self, step):
        return self.pass_on(
            self.ring.chunk(step + 1), self.ring.far_hops + step, self.ring.behind()
        )

    def begin(self):
        self.far_copy(0).start()
        self.near_copy(0).start()
        self.to_sibling(self.ring.chunk(0)).start()

    def far_step(self, step, last=False):
        self.far_landed(step - 1).wait_recv()
        if not last:
            self.far_copy(step).start()
        self.to_sibling(self.ring.chunk(-step)).start()

    def near_step(self, step, last=False):
        self.near_landed(step - 1).wait_recv()
        if not last:
            self.near_copy(step).start()
        self.to_sibling(self.ring.chunk(step)).start()

    def both_steps(self, step):
        self.far_step(step)
        self.near_step(step)

    def close(self):
        self.far_step(self.ring.near_hops)
        self.near_step(self.ring.near_hops, last=True)

    def sent(self):
        ring = self.ring
        loop(0, ring.chips, lambda chunk: self.from_sibling(chunk).wait_recv())
        loop(0, ring.chips, lambda chunk: self.to_sibling(chunk).wait_send())
        loop(0, ring.far_hops, lambda step: self.far_copy(step).wait_send())
        loop(0, ring.near_hops, lambda step: self.near_copy(step).wait_send())


def greet(*devices):
    barrier = pltpu.get_barrier_semaphore()
    for device in devices:
        pl.semaphore_signal(barrier, inc=1, device_id=device, device_id_type=pl.DeviceIdType.MESH)
    pl.semaphore_wait(barrier, len(devices))


def padded(rows, dp):
    unit = 16 * dp
    return -(-rows // unit) * unit


def feed_kernel(
    h_ref, gf_ref, e_far, b_far, s_far, e_own, b_own, s_own,
    f_ref, gh_ref, grad_ref, db_far, db_own, shard_ref,
    act_ref, gu_ref, tiles, crossing, got, y_sems, *rest, chunk, dp
):
    seq_len = h_ref.shape[0]
    tile = e_own.shape[1]
    root = 0.7978845608
    cube = 0.044715
    step = pl.program_id(0)
    far_steps = tiles.shape[0]
    is_far = step < far_steps
    parts = seq_len // chunk
    ring = Ring(dp)
    groups = [
        Group(ring, tiles.at[index], None, rest[5 * index : 5 * index + 5])
        for index in range(far_steps)
    ]

    def cross(index):
        return send(crossing.at[index], got.at[index], y_sems, index, ring.partner())

    def finish(index):
        crossing[index] = groups[index].finish().astype(bf16)
        cross(index).start()

    plan = {}

    def spacing(index):
        left = (parts + 1) * (2 * far_steps - 1 - index) - 2
        return min(parts, left // ring.far_hops)

    for index, group in enumerate(groups):
        slot = (parts + 1) * (index + 1) - 1
        plan.setdefault(slot, []).append(group.hand_over)
        for hop in range(ring.far_hops):
            slot_of_hop = slot + 2 + hop * spacing(index)
            action = functools.partial(group.far_step, hop)
            if hop < ring.near_hops:
                action = functools.partial(group.both_steps, hop, hop == 0)
            plan.setdefault(slot_of_hop, []).append(action)
        slot += 2 + ring.far_hops * spacing(index)
        plan.setdefault(slot, []).append(functools.partial(finish, index))

    def tick(part):
        for slot, actions in plan.items():
            if slot % (parts + 1) == part:

                @pl.when(step == slot // (parts + 1))
                def _():
                    for action in actions:
                        action()

    @pl.when(step == 0)
    def _():
        f_ref[...] = jnp.zeros_like(f_ref)
        gh_ref[...] = jnp.zeros_like(gh_ref)
        greet(ring.ahead(), ring.behind(), ring.sibling(), ring.partner())

    e = jnp.where(is_far, e_far[...], e_own[...])
    s = jnp.where(is_far, s_far[...].reshape(s_own.shape), s_own[...])
    bias = jnp.where(is_far, b_far[...], b_own[...])
    total = jnp.zeros((1, tile), f32)
    for index in range(parts):
        rows = pl.ds(index * chunk, chunk)
        u = dot_nn(h_ref[rows, :], e) + bias
        ga = dot_nt(gf_ref[rows, :], s)
        square = u * u
        bent = jnp.tanh(u * (root + (root * cube) * square))
        half = 0.5 + 0.5 * bent
        act = (u * half).astype(bf16)
        slope = half + (0.5 * u) * (1.0 - bent * bent) * (root + (3.0 * root * cube) * square)
        gu_wide = (slope * ga).astype(bf16)
        act_ref[rows, :] = act
        gu_ref[rows, :] = gu_wide
        total += jnp.sum(gu_wide.astype(f32), axis=0, keepdims=True)
        f_ref[rows, :] += dot_nn(act, s)
        gh_ref[rows, :] += dot_nt(gu_wide, e)
        tick(index)
    grad_e = dot_tn(gu_ref[...], h_ref[...]).astype(bf16)
    grad_s = dot_tn(act_ref[...], gf_ref[...]).astype(bf16)

    @pl.when(is_far)
    def _():
        db_far[...] = total
        tiles[jnp.minimum(step, far_steps - 1), :tile, :] = grad_e
        tiles[jnp.minimum(step, far_steps - 1), tile:, :] = grad_s

    @pl.when(jnp.logical_not(is_far))
    def _():
        db_own[...] = total
        half_chunks, _, rows, width = grad_ref.shape
        grad_ref[: half_chunks // 2, 0] = grad_e.reshape(half_chunks // 2, rows, width)
        grad_ref[half_chunks // 2 :, 0] = grad_s.reshape(half_chunks // 2, rows, width)

    tick(parts)

    @pl.when(step == pl.num_programs(0) - 1)
    def _():
        for index in range(far_steps):
            cross(index).wait_recv()
            shard_ref[index] = got[index]
        for index, group in enumerate(groups):
            cross(index).wait_send()
            group.sent()


def feed(h, gf, e_far, b_far, s_far, e_own, b_own, s_own, dp):
    seq_len, width = h.shape
    hidden = e_own.shape[1]
    tile = min(512, hidden)
    steps = hidden // tile
    size = 2 * tile // dp
    shares = s_far.shape[0]
    whole_rows = whole((seq_len, width))

    def far(i):
        return jnp.minimum(i, steps - 1)

    def own(i):
        return jnp.maximum(i - steps, 0)

    def weights(of):
        return [
            pl.BlockSpec((width, tile), lambda i: (0, of(i))),
            pl.BlockSpec((1, tile), lambda i: (0, of(i))),
            pl.BlockSpec((tile, width), lambda i: (of(i), 0)),
        ]

    scratch = []
    for _ in range(steps):
        scratch += Group.scratch(2 * tile, width, dp)
    return pl.pallas_call(
        functools.partial(feed_kernel, chunk=min(256, seq_len), dp=dp),
        grid=(2 * steps,),
        in_specs=[whole_rows, whole_rows]
        + weights(far)[:2]
        + [pl.BlockSpec((shares, tile // shares, width), lambda i: (0, far(i), 0))]
        + weights(own),
        out_specs=[
            whole_rows,
            whole_rows,
            pl.BlockSpec((dp, 1, size, width), lambda i: (0, own(i), 0, 0)),
            pl.BlockSpec((1, tile), lambda i: (0, far(i))),
            pl.BlockSpec((1, tile), lambda i: (0, own(i))),
            whole((steps, size, width)),
        ],
        out_shape=[
            jax.ShapeDtypeStruct((seq_len, width), f32),
            jax.ShapeDtypeStruct((seq_len, width), f32),
            jax.ShapeDtypeStruct((dp, steps, size, width), bf16),
            jax.ShapeDtypeStruct((1, hidden), f32),
            jax.ShapeDtypeStruct((1, hidden), f32),
            jax.ShapeDtypeStruct((steps, size, width), bf16),
        ],
        scratch_shapes=[
            pltpu.VMEM((seq_len, tile), bf16),
            pltpu.VMEM((seq_len, tile), bf16),
            pltpu.VMEM((steps, 2 * tile, width), bf16),
            pltpu.VMEM((steps, size, width), bf16),
            pltpu.VMEM((steps, size, width), bf16),
            pltpu.SemaphoreType.DMA((2, steps)),
        ]
        + scratch,
        compiler_params=remote_params(1),
        cost_estimate=cost(45),
        name="feed",
    )(h, gf, e_far, b_far, s_far, e_own, b_own, s_own)


def three_parts(values):
    first = values.astype(bf16).astype(f32)
    rest = values - first
    second = rest.astype(bf16).astype(f32)
    return first, second, rest - second


def attend_back(length, qkv, o, lse, go, acc_ref, seq, pair, local, block, between):
    seq_len = qkv.shape[1]
    scale = HD**-0.5

    def columns(part):
        return pl.ds(pl.multiple_of(part * local + pair * PAIR, PAIR), PAIR)

    lane = lane_index(seq_len)
    position = lax.broadcasted_iota(jnp.int32, (seq_len, PAIR), 0)
    inside = position < length
    key_bias = jnp.where(inside, 0.0, masked_fill)
    row, column = causal_block(block)
    keep = row <= column
    q = qkv[seq, :, columns(0)]
    k = qkv[seq, :, columns(1)]
    v = qkv[seq, :, columns(2)]
    grad_o = go[seq, :, columns(0)]
    q_wide = q.astype(f32) * scale
    k_wide = k.astype(f32)
    v_wide = v.astype(f32)
    go_wide = grad_o.astype(f32)
    both = go_wide * o[:, columns(0)].astype(f32)
    lse_parts = three_parts(-lse[:, columns(0)])
    low = lane < HD
    zero = jnp.zeros_like(q)
    acc_ref[...] = jnp.zeros_like(acc_ref)
    count = seq_len // block
    grads_k = [None] * count
    grads_v = [None] * count
    for head in range(2):
        mine = low if head == 0 else jnp.logical_not(low)
        spare = HD if head == 0 else 0
        delta = jnp.sum(jnp.where(mine, both, 0.0), axis=-1, keepdims=True)
        delta_parts = three_parts(-jnp.broadcast_to(delta, (seq_len, PAIR)))

        def extras(parts):
            return jnp.where(
                lane == spare + 1,
                parts[0],
                jnp.where(lane == spare + 2, parts[1], jnp.where(lane == spare + 3, parts[2], 0.0)),
            )

        ones = jnp.where((lane > spare) & (lane < spare + 4), 1.0, 0.0)
        q_aug = jnp.where(mine, q_wide, jnp.where(lane == spare, 1.0, extras(lse_parts))).astype(bf16)
        k_aug = jnp.where(mine, k_wide, jnp.where(lane == spare, key_bias, ones)).astype(bf16)
        v_aug = jnp.where(mine, v_wide, ones).astype(bf16)
        go_aug = jnp.where(mine, go_wide, extras(delta_parts)).astype(bf16)
        q_own = jnp.where(mine, q, zero)
        k_own = jnp.where(mine, k, zero)
        go_own = jnp.where(mine, grad_o, zero)
        for index in range(count):
            start, end = index * block, (index + 1) * block
            scores = dot_nt(k_aug[start:end], q_aug[start:])
            first = jnp.where(keep, scores[:, :block], masked_fill)
            if index + 1 < count:
                scores = jnp.concatenate([first, scores[:, block:]], axis=1)
            else:
                scores = first
            shares = jnp.exp(scores)
            moved = dot_nt(v_aug[start:end], go_aug[start:])
            grad_scores = (shares * moved).astype(bf16)
            grad_v = dot_nn(shares.astype(bf16), go_own[start:])
            grad_k = dot_nn(grad_scores, q_own[start:])
            grads_v[index] = grad_v if head == 0 else grads_v[index] + grad_v
            grads_k[index] = grad_k if head == 0 else grads_k[index] + grad_k
            acc_ref[start:, :] += dot_tn(grad_scores, k_own[start:end])
        between(head)
    qkv[seq, :, columns(0)] = (acc_ref[...] * scale).astype(bf16)
    qkv[seq, :, columns(1)] = (jnp.concatenate(grads_k, axis=0) * scale).astype(bf16)
    qkv[seq, :, columns(2)] = jnp.where(inside, jnp.concatenate(grads_v, axis=0), 0.0).astype(bf16)


def back_kernel(
    len_ref, sums_in, db_own, db_far, shift_mlp, gain_two, w_out, w_far, gain_ref, shift_ref,
    cot, resid, f_sum, gh_sum, tokens, qkv_first, qkv_second, h_first, h_second,
    o_keep, o_sent, lse_keep, lse_sent, o_keep_second, o_sent_second, lse_keep_second, lse_sent_second,
    got_first, got_second, weight, feed_own, feed_far,
    result_out, feed_out, more_out, query_out, last_out, input_out,
    load_sems, y_sems, block_sems, cot_buf, wide_bufs, result_buf, go_send, sums, gain_acc,
    qkv, o, lse, go, ga, mixed, h, w, acc_ref, row_send, row_got,
    feed_far_shard, feed_shard, more_shard, more_got, query_shard, last_shard, tile_send, tile_got,
    feed_acc, far_local, own_local, query_local, last_local, *rest, dp
):
    rest = list(rest)

    def take(count):
        taken = rest[:count]
        del rest[:count]
        return taken

    half, width = got_first.shape[0], tokens.shape[2]
    seq_len = 2 * half
    local = qkv.shape[2] // 3
    pairs = local // PAIR
    block = min(256, half)
    ring = Ring(dp)
    here = ring.tensor
    there = 1 - here
    feed_group = Group(ring, feed_own, feed_acc, take(5))
    far_group = Group(ring, far_local, None, take(5))
    own_group = Group(ring, own_local, None, take(5))
    query_group = Group(ring, query_local, None, take(5))
    last_group = Group(ring, last_local, None, take(5))
    feed_spread = Spread(ring, feed_out, take(2))
    more_spread = Spread(ring, more_out, take(2))
    query_spread = Spread(ring, query_out, take(2))
    last_spread = Spread(ring, last_out, take(2))

    def load(source, target, number):
        return pltpu.make_async_copy(source, target, load_sems.at[number])

    rows_here = pl.ds(pl.multiple_of(here * half, 16), half)
    rows_there = pl.ds(pl.multiple_of(there * half, 16), half)
    front, rear = pl.ds(0, half), pl.ds(half, half)
    mixed_loads = [
        load(o_keep, mixed.at[0, front], 1),
        load(o_keep_second, mixed.at[0, rear], 2),
        load(got_first, mixed.at[1, front], 3),
        load(got_second, mixed.at[1, rear], 4),
    ]
    first_loads = [
        load(qkv_first, qkv.at[0], 5),
        load(o_keep, o.at[rows_here], 6),
        load(o_sent, o.at[rows_there], 7),
        load(lse_keep, lse.at[rows_here], 8),
        load(lse_sent, lse.at[rows_there], 9),
    ]
    row_loads = [load(weight, w, 11)]
    second_loads = [load(qkv_second, qkv.at[1], 12)]
    late_loads = [load(h_first, h.at[0], 14), load(h_second, h.at[1], 15)]
    token_loads = [load(tokens.at[0], ga.at[front], 16), load(tokens.at[1], ga.at[rear], 17)]
    shard_load = load(feed_far, feed_far_shard, 18)
    reloads = [
        load(o_keep_second, o.at[rows_here], 19),
        load(o_sent_second, o.at[rows_there], 20),
        load(lse_keep_second, lse.at[rows_here], 21),
        load(lse_sent_second, lse.at[rows_there], 22),
    ]

    def cross(source, target, number):
        return send(source, target, y_sems, number, ring.partner())

    go_cross = [
        cross(go_send.at[front], go.at[0, rows_here], 0),
        cross(go_send.at[rear], go.at[1, rows_here], 1),
    ]
    go_landed = [
        cross(go_send.at[front], go.at[0, rows_there], 0),
        cross(go_send.at[rear], go.at[1, rows_there], 1),
    ]
    row_cross = [
        cross(row_send.at[0], row_got.at[0], 2),
        cross(row_send.at[1], row_got.at[1], 3),
    ]
    more_cross = cross(more_shard, more_got, 5)
    tile_cross = cross(tile_send, tile_got, 6)

    part = cot_buf.shape[1]
    parts = seq_len // part

    def fetch(index):
        slot = index % 2
        rows = pl.ds(pl.multiple_of(index * part, 16), part)
        copies = [pltpu.make_async_copy(cot.at[rows], cot_buf.at[slot], block_sems.at[slot, 0])]
        for number, source in enumerate((resid, f_sum, gh_sum)):
            copies.append(
                pltpu.make_async_copy(
                    source.at[rows], wide_bufs.at[slot, number], block_sems.at[slot, 1 + number]
                )
            )
        return copies

    def put(index):
        slot = index % 2
        rows = pl.ds(pl.multiple_of(index * part, 16), part)
        return pltpu.make_async_copy(result_buf.at[slot], result_out.at[rows], block_sems.at[slot, 6])

    def add(row, values):
        sums[row : row + 1] += jnp.sum(values, axis=0, keepdims=True)

    def turn(index):
        slot = index % 2
        for copy in fetch(index):
            copy.wait()

        @pl.when(index + 1 < parts)
        def _():
            for copy in fetch(index + 1):
                copy.start()

        @pl.when(index >= 2)
        def _():
            put(index - 2).wait()

        seq = index * part // half
        offset = index * part - seq * half
        rows = pl.ds(pl.multiple_of(offset, 16), part)
        flat = pl.ds(pl.multiple_of(index * part, 16), part)
        placed = pl.ds(pl.multiple_of(here * half + offset, 16), part)
        position = here * half + offset + lax.broadcasted_iota(jnp.int32, (part, 1), 0)
        valid = (position < len_ref[seq]).astype(f32)
        first = wide_bufs[slot, 0]
        mlp = wide_bufs[slot, 1] + shift_mlp[...]
        result = first + valid * mlp
        result_buf[slot] = result
        put(index).start()
        unit, inverse = normalized(first)
        grad_norm = valid * wide_bufs[slot, 2]
        grad = cot_buf[slot].astype(f32) + norm_back(unit, inverse, gain_two[...], grad_norm)
        input_out[seq, rows, :] = grad
        grad_attn = valid * grad
        low = grad_attn.astype(bf16)
        ga[flat, :] = low
        go_send[flat, :] = dot_nt(low, w_far[...]).astype(bf16)
        go[seq, placed, :] = dot_nt(low, w_out[...]).astype(bf16)
        add(0, grad_attn)
        add(1, grad_norm * unit)
        add(2, grad_norm)
        add(4, valid * result * result)
        add(6, valid * mlp * mlp)

        @pl.when(index == parts // 2 - 1)
        def _():
            go_cross[0].start()
            feed_group.load().wait()
            feed_group.both_steps(0, first=True)

    for copy in fetch(0):
        copy.start()
    feed_group.load().start()
    greet(ring.ahead(), ring.behind(), ring.sibling(), ring.partner())
    feed_group.hand_over()
    for copy in mixed_loads + first_loads + row_loads + second_loads + [shard_load] + late_loads:
        copy.start()
    sums[...] = jnp.zeros_like(sums)
    gain_acc[...] = jnp.zeros_like(gain_acc)
    loop(0, parts, turn)
    go_cross[1].start()
    feed_group.both_steps(1)
    put(parts - 2).wait()
    put(parts - 1).wait()

    lane = lax.broadcasted_iota(jnp.int32, (1, width), 1)
    count = jnp.zeros((1, width), f32)
    for start in range(0, half, width):
        position = here * half + lane + start
        for seq in range(2):
            count += ((lane + start < half) & (position < len_ref[seq])).astype(f32)
    sums[3:4] = sums_in[1:2]
    sums[5:6] = sums_in[0:1]
    sums[7:8] = count
    for copy in mixed_loads:
        copy.wait()
    tail = far_local.shape[0] - local - 16
    for target, index, small in ((far_local, 1, db_far), (own_local, 0, db_own)):
        target[pl.ds(0, local), :] = dot_tn(mixed[index], ga[...]).astype(bf16)
        target[pl.ds(local, 16), :] = jnp.concatenate([sums[0:8], small[...]], axis=0).astype(bf16)
        target[pl.ds(local + 16, tail), :] = jnp.zeros((tail, width), bf16)
    for copy in token_loads:
        copy.start()
    far_group.hand_over()
    own_group.hand_over()
    for copy in first_loads:
        copy.wait()
    go_landed[0].wait_recv()

    def store(spread, shard, number):
        copy = load(shard, spread.out.at[spread.place(ring.core, ring.spot)], number)
        copy.start()
        copy.wait()
        spread.begin()

    def feed_begin():
        shard_load.wait()
        value = feed_group.finish() + feed_far_shard[...].astype(f32)
        feed_shard[...] = value.astype(bf16)
        store(feed_spread, feed_shard, 0)

    def more_shard_cross():
        more_shard[...] = far_group.finish().astype(bf16)
        more_cross.start()

    def more_begin():
        value = own_group.finish()
        more_cross.wait_recv()
        more_cross.wait_send()
        more_shard[...] = (value + more_got[...].astype(f32)).astype(bf16)
        store(more_spread, more_shard, 10)

    def hop(group, step):
        if step == ring.far_hops - 1:
            group.far_step(step)
        else:
            group.both_steps(step, first=step == 0)

    def spread_step(spread, step):
        if step == ring.far_hops:
            spread.far_step(step, last=True)
        elif step == ring.near_hops:
            spread.close()
        else:
            spread.both_steps(step)

    def query_begin():
        query_shard[...] = query_group.finish().astype(bf16)
        store(query_spread, query_shard, 13)

    tile_row = lax.broadcasted_iota(jnp.int32, (16, width), 0)

    def last_hand_over():
        tile_cross.wait_recv()
        added = jnp.where(tile_row < 2, tile_got[...], 0.0)
        last_local[pl.ds(3 * PAIR, 16), :] = (tile_send[...] + added).astype(bf16)
        last_group.hand_over()

    def last_begin():
        last_shard[...] = last_group.finish().astype(bf16)
        store(last_spread, last_shard, 13)

    def through(rows):
        total = dot_nt(rows[:, :local], w[0])
        for index in range(1, 3):
            total += dot_nt(rows[:, index * local : (index + 1) * local], w[index])
        return total

    def send_rows(seq):
        def one(index):
            rows = pl.ds(pl.multiple_of(index * block, 16), block)
            from_rows = pl.ds(pl.multiple_of(there * half + index * block, 16), block)
            row_send[seq, rows, :] = through(qkv[seq, from_rows, :]).astype(bf16)

        loop(0, half // block, one)
        row_cross[seq].start()

    def keep_rows(seq):
        row_cross[seq].wait_recv()

        def one(index):
            rows = pl.ds(pl.multiple_of(index * block, 16), block)
            from_rows = pl.ds(pl.multiple_of(here * half + index * block, 16), block)
            position = here * half + index * block
            position += lax.broadcasted_iota(jnp.int32, (block, 1), 0)
            grad = through(qkv[seq, from_rows, :]) + row_got[seq, rows, :].astype(f32)
            grad = jnp.where(position < len_ref[seq], grad, 0.0)
            x_rows = pl.ds(pl.multiple_of(seq * half + index * block, 16), block)
            unit, inverse = normalized(ga[x_rows, :].astype(f32))
            input_out[seq, rows, :] += norm_back(unit, inverse, gain_ref[...], grad)

        loop(0, half // block, one)

    def query_rows(pair):
        if pair == 0:
            for copy in late_loads + token_loads:
                copy.wait()
        for index in range(3):
            columns = pl.ds(index * local + pair * PAIR, PAIR)
            value = dot_tn(qkv[0, :, columns], h[0]) + dot_tn(qkv[1, :, columns], h[1])
            target = last_local if pair == pairs - 1 else query_local
            start = 0 if pair == pairs - 1 else 3 * pair * PAIR
            target[pl.ds(start + index * PAIR, PAIR), :] = value.astype(bf16)
            weighted = value * w[index, :, pl.ds(pair * PAIR, PAIR)].astype(f32).T
            gain_acc[0:1] += jnp.sum(weighted, axis=0, keepdims=True)
        if pair == pairs - 2:
            used = 3 * (pairs - 1) * PAIR
            if query_local.shape[0] > used:
                rows = query_local.shape[0] - used
                query_local[pl.ds(used, rows), :] = jnp.zeros((rows, width), bf16)
            query_group.hand_over()
        if pair == pairs - 1:
            rows = last_local.shape[0] - 3 * PAIR
            last_local[pl.ds(3 * PAIR, rows), :] = jnp.zeros((rows, width), bf16)
            ones = jnp.ones((16, seq_len), bf16)
            totals = dot_nn(ones, qkv[0]) + dot_nn(ones, qkv[1])
            high = totals.astype(bf16)
            low = (totals - high.astype(f32)).astype(bf16)
            shift_grad = (through(high) + through(low))[0:1]
            gain_grad = (gain_acc[0:1] - shift_ref[...] * shift_grad) / gain_ref[...]
            biases = jnp.concatenate([totals[0:1, :local], totals[0:1, 2 * local :]], axis=1)
            last = jnp.where(tile_row == 2, biases, 0.0)
            last = jnp.where(tile_row == 1, shift_grad, last)
            last = jnp.where(tile_row == 0, gain_grad, last)
            tile_send[...] = last
            tile_cross.start()

    plan = {}

    def chain(tick, *actions):
        for number, action in enumerate(actions):
            if action is not None:
                plan.setdefault(tick + number, []).append(action)

    def hops(first, *groups):
        def one(step):
            for group in groups:
                hop(group, step)

        return [functools.partial(one, step) for step in range(first, ring.far_hops)]

    def spreads(spread):
        steps = range(1, ring.far_hops + 1)
        return [functools.partial(spread_step, spread, step) for step in steps]

    ticks = [1, 4, 7, 9, 11]
    free = len(ticks)
    chain(0, *hops(2, feed_group), feed_begin, *spreads(feed_spread))
    chain(0, *hops(0, far_group, own_group), more_shard_cross, more_begin, *spreads(more_spread))
    chain(free - 1, *hops(0, query_group), query_begin, *spreads(query_spread))
    chain(free, functools.partial(send_rows, 1))
    plan[free].insert(0, plan[free].pop())
    plan[free].insert(1, last_hand_over)
    chain(free, *hops(0, last_group), last_begin, *spreads(last_spread))
    chain(free + 1, functools.partial(keep_rows, 0))
    chain(free + ring.far_hops - 1, functools.partial(keep_rows, 1))

    def attention(index):
        seq = index // pairs
        pair = index % pairs

        @pl.when(index == pairs)
        def _():
            for copy in reloads:
                copy.start()
            for copy in row_loads:
                copy.wait()
            send_rows(0)
            for copy in second_loads + reloads:
                copy.wait()
            go_landed[1].wait_recv()

        def between(head):
            for tick, slot in enumerate(ticks):
                if slot % 2 == head:

                    @pl.when(index == slot // 2)
                    def _():
                        for action in plan[tick]:
                            action()

        attend_back(len_ref[seq], qkv, o, lse, go, acc_ref, seq, pair, local, block, between)
        for number in range(pairs):
            pl.when(index == pairs + number)(functools.partial(query_rows, number))

    loop(0, 2 * pairs, attention)
    for number in sorted(plan):
        if number >= free:
            for action in plan[number]:
                action()
    for group in (feed_group, far_group, own_group, query_group, last_group):
        group.sent()
    for copy in go_cross + row_cross + [tile_cross]:
        copy.wait_send()
    for spread in (feed_spread, more_spread, query_spread, last_spread):
        spread.sent()


def back(
    lens, sums, db_own, db_far, shift_mlp, gain_two, w_out, w_far, gain, shift, rows, tokens, qkvs, hs,
    attended, gots, weight, feed_own, feed_far, dp
):
    _, half, width = tokens.shape
    seq_len = 2 * half
    local = weight.shape[2]
    columns = 3 * local
    pairs = local // PAIR
    feed_rows = feed_own.shape[0]
    more_rows = padded(local + 32, dp)
    query_rows = padded(3 * (pairs - 1) * PAIR, dp)
    last_rows = padded(3 * PAIR + 32, dp)
    anywhere = pl.BlockSpec(memory_space=pl.ANY)
    inside = pl.BlockSpec(memory_space=pltpu.VMEM)
    feed_size, more_size, query_size = feed_rows // dp, more_rows // dp, query_rows // dp
    last_size = last_rows // dp
    both_rows = pltpu.VMEM((2, half, width), bf16)
    part = min(128, half)
    return pl.pallas_call(
        functools.partial(back_kernel, dp=dp),
        in_specs=[pl.BlockSpec(memory_space=pltpu.SMEM)] + [inside] * 9 + [anywhere] * 22,
        out_specs=[anywhere] * 5 + [inside],
        out_shape=[
            jax.ShapeDtypeStruct((seq_len, width), f32),
            jax.ShapeDtypeStruct((feed_rows, width), bf16),
            jax.ShapeDtypeStruct((more_rows, width), bf16),
            jax.ShapeDtypeStruct((query_rows, width), bf16),
            jax.ShapeDtypeStruct((last_rows, width), bf16),
            jax.ShapeDtypeStruct((2, half, width), f32),
        ],
        scratch_shapes=[
            pltpu.SemaphoreType.DMA((23,)),
            pltpu.SemaphoreType.DMA((2, 7)),
            pltpu.SemaphoreType.DMA((2, 7)),
            pltpu.VMEM((2, part, width), bf16),
            pltpu.VMEM((2, 3, part, width), f32),
            pltpu.VMEM((2, part, width), f32),
            pltpu.VMEM((seq_len, local), bf16),
            pltpu.VMEM((8, width), f32),
            pltpu.VMEM((8, width), f32),
            pltpu.VMEM((2, seq_len, columns), bf16),
            pltpu.VMEM((seq_len, local), bf16),
            pltpu.VMEM((seq_len, local), f32),
            pltpu.VMEM((2, seq_len, local), bf16),
            pltpu.VMEM((seq_len, width), bf16),
            pltpu.VMEM((2, seq_len, local), bf16),
            pltpu.VMEM((2, seq_len, width), bf16),
            pltpu.VMEM(weight.shape, bf16),
            pltpu.VMEM((seq_len, PAIR), f32),
            both_rows,
            both_rows,
            pltpu.VMEM((feed_size, width), bf16),
            pltpu.VMEM((feed_size, width), bf16),
            pltpu.VMEM((more_size, width), bf16),
            pltpu.VMEM((more_size, width), bf16),
            pltpu.VMEM((query_size, width), bf16),
            pltpu.VMEM((last_size, width), bf16),
            pltpu.VMEM((16, width), f32),
            pltpu.VMEM((16, width), f32),
            pltpu.VMEM((feed_rows // 2, width), bf16),
            pltpu.VMEM((more_rows, width), bf16),
            pltpu.VMEM((more_rows, width), bf16),
            pltpu.VMEM((query_rows, width), bf16),
            pltpu.VMEM((last_rows, width), bf16),
        ]
        + Group.scratch(feed_rows, width, dp)
        + Group.scratch(more_rows, width, dp)
        + Group.scratch(more_rows, width, dp)
        + Group.scratch(query_rows, width, dp)
        + Group.scratch(last_rows, width, dp)
        + Spread.scratch(dp) * 4,
        compiler_params=remote_params(2),
        cost_estimate=cost(90),
        name="back",
    )(
        lens, sums, db_own, db_far, shift_mlp, gain_two, w_out, w_far, gain, shift, *rows, tokens, *qkvs,
        *hs, *attended, *gots, weight, feed_own, feed_far,
    )


def lay_out_kernel(
    e_ref, s_ref, out_ref, q_ref, last_ref, result_ref, input_ref, small_ref, tail_ref,
    e_out, s_out, o_out, a_out, r_out, i_out, *vectors, local
):
    flat = s_out.shape
    e_out[...] = e_ref[...].reshape(flat).T.astype(f32)
    s_out[...] = s_ref[...].reshape(flat).astype(f32)
    o_out[...] = out_ref[...].astype(f32)
    r_out[...] = result_ref[...]
    i_out[...] = input_ref[...]
    step = pl.program_id(0)

    @pl.when(step == 0)
    def _():
        small = small_ref[...].astype(f32)
        tail = tail_ref[...].astype(f32)
        for index in range(4):
            vectors[index][...] = small[index]
        vectors[4][...] = tail[0]
        vectors[5][...] = tail[1]
        vectors[6][...] = tail[2, :local]
        vectors[7][...] = tail[2, local:]
        width = small.shape[1]
        for index in range(vectors[8].shape[0] // width):
            vectors[8][index * width : (index + 1) * width] = small[8 + index]
        vectors[9][...] = small[4:8]

    pairs = local // PAIR
    each = pl.num_programs(0) // 3
    for part in range(3):
        for pair in range(pairs):

            @pl.when(step == part * each + pair)
            def _():
                source = last_ref if pair == pairs - 1 else q_ref
                start = (0 if pair == pairs - 1 else 3 * pair * PAIR) + part * PAIR
                value = source[start : start + PAIR, :].T
                a_out[0, :, pair * PAIR : (pair + 1) * PAIR] = value.astype(f32)


def lay_out(feed_sum, more_sum, query_sum, last_sum, result, grad, hidden, local):
    chunks, tiles, feed_size, width = feed_sum.shape
    steps = hidden // PAIR
    turns = steps // tiles
    group = PAIR // feed_size
    rows = result.shape[0]
    size = rows * 3 // (2 * steps)
    blocks = rows // size
    proj = local // steps
    vectors = [(width,)] * 6 + [(local,)] * 2 + [(hidden,), (4, width)]

    def some(i):
        return jnp.minimum(i, blocks - 1), 0

    return pl.pallas_call(
        functools.partial(lay_out_kernel, local=local),
        grid=(steps,),
        in_specs=[
            pl.BlockSpec((group, 1, feed_size, width), lambda i: (i % turns, i // turns, 0, 0)),
            pl.BlockSpec(
                (group, 1, feed_size, width), lambda i: (i % turns + turns, i // turns, 0, 0)
            ),
            pl.BlockSpec((proj, width), lambda i: (i, 0)),
            whole(query_sum.shape),
            whole(last_sum.shape),
            pl.BlockSpec((size, width), some),
            pl.BlockSpec((size, width), some),
            pl.BlockSpec((16, width), lambda i: (local // 16, 0)),
            pl.BlockSpec((16, width), lambda i: (3 * PAIR // 16, 0)),
        ],
        out_specs=[
            pl.BlockSpec((width, PAIR), lambda i: (0, i)),
            pl.BlockSpec((PAIR, width), lambda i: (i, 0)),
            pl.BlockSpec((proj, width), lambda i: (i, 0)),
            pl.BlockSpec((1, width, local), lambda i: (i // (steps // 3), 0, 0)),
            pl.BlockSpec((size, width), some),
            pl.BlockSpec((size, width), some),
        ]
        + [whole(shape) for shape in vectors],
        out_shape=[
            jax.ShapeDtypeStruct((width, hidden), f32),
            jax.ShapeDtypeStruct((hidden, width), f32),
            jax.ShapeDtypeStruct((local, width), f32),
            jax.ShapeDtypeStruct((3, width, local), f32),
            jax.ShapeDtypeStruct((rows, width), f32),
            jax.ShapeDtypeStruct((rows, width), f32),
        ]
        + [jax.ShapeDtypeStruct(shape, f32) for shape in vectors],
        compiler_params=params(),
        cost_estimate=cost(10),
        name="lay_out",
    )(feed_sum, feed_sum, more_sum, query_sum, last_sum, result, grad, more_sum, last_sum)


def body(
    tokens,
    lengths,
    layer_index,
    norm_one_gain,
    norm_one_bias,
    attend_weight,
    query_bias,
    value_bias,
    output_weight,
    output_bias,
    norm_two_gain,
    norm_two_bias,
    expand_weight,
    expand_bias,
    shrink_weight,
    shrink_bias,
    cotangent,
):
    seq_dev, half, width = tokens.shape
    dp = lax.axis_size("dp")
    here = lax.axis_index("tensor")
    there = 1 - here
    place = lax.axis_index("dp")

    def exchange(values):
        return lax.ppermute(values, "tensor", [(0, 1), (1, 0)])

    def layer(stack):
        return select_layer(stack, layer_index)

    def wide(stack):
        return layer(stack).astype(f32)[None]

    def after(values, earlier):
        return lax.optimization_barrier((values, earlier))[0]

    def share(stack):
        rows = stack.shape[1] // dp
        piece = lax.dynamic_slice(
            stack, (layer_index[0], place * rows, 0), (1, rows, stack.shape[2])
        )
        return piece[0]

    def tiled_share(stack):
        tiles = max(1, stack.shape[1] // 512)
        each = stack.shape[1] // tiles // dp
        return jnp.concatenate(
            [
                lax.dynamic_slice(
                    stack,
                    (layer_index[0], index * each * dp + place * each, 0),
                    (1, each, stack.shape[2]),
                )[0]
                for index in range(tiles)
            ],
            axis=0,
        )

    def gather(piece):
        return lax.all_gather(piece, "dp", axis=0, tiled=False)

    hidden = expand_weight.shape[2]
    shrink_rows = hidden // dp
    pieces = [
        tokens[0],
        jnp.concatenate([tiled_share(shrink_weight), share(output_weight)], axis=0),
        share(expand_weight),
    ]
    pieces = lax.optimization_barrier(pieces)
    token_got = [exchange(pieces[0])]
    first_got = exchange(pieces[1])
    expand_got = exchange(pieces[2])
    token_got.append(exchange(after(tokens[1], token_got[0])))
    first_all = gather(first_got)
    out_far = first_all[:, shrink_rows:].reshape(output_weight.shape[1:])
    expand_far = gather(expand_got).reshape(width, hidden)
    expand_shift_far = exchange(after(layer(expand_bias), token_got[0]))[None].astype(f32)

    sides = jnp.stack([here, there]).astype(jnp.int32)

    def at(side, seq):
        return jnp.stack([sides[side], lengths[seq]])

    at_rows = jnp.concatenate([sides[:1], lengths])
    gain_one, shift_one = wide(norm_one_gain), wide(norm_one_bias)
    gain_two, shift_two = wide(norm_two_gain), wide(norm_two_bias)
    attend_own = layer(attend_weight.transpose(0, 2, 1, 3))
    out_mat, expand_own, shrink_own = layer(output_weight), layer(expand_weight), layer(shrink_weight)
    local = attend_own.shape[2]
    qkv_bias = jnp.concatenate(
        [wide(query_bias), jnp.zeros((1, local), f32), wide(value_bias)], axis=1
    )

    hs, qkvs, attended, kept, gots = [], [], [], [], []
    for seq in range(seq_dev):
        h, qkv = project(
            at(0, seq), tokens[seq], token_got[seq], gain_one, shift_one, attend_own, qkv_bias
        )
        o_sent, lse_sent = attend(at(1, seq), qkv, 7)
        gots.append(exchange(o_sent))
        o_keep, lse_keep = attend(at(0, seq), qkv, 7)
        hs.append(h)
        qkvs.append(qkv)
        kept.append(o_keep)
        attended += [o_keep, o_sent, lse_keep, lse_sent]

    x_rows = tokens.reshape(-1, width)
    cot = cotangent.reshape(-1, width)
    shrink_all = first_all
    if shrink_rows * dp // max(1, hidden // 512) // dp % 16:
        tiles = max(1, hidden // 512)
        shrink_all = first_all[:, :shrink_rows].reshape(dp, tiles, -1, width)
        shrink_all = shrink_all.transpose(1, 0, 2, 3).reshape(1, hidden, width)
    h_two, gf, resid, sums = resid_norm(
        at_rows, x_rows, cot, *kept, *gots, out_mat, out_far, wide(output_bias), gain_two, shift_two
    )
    span = min(dp, 16)
    f_sum, gh_sum, grads_own, db_far, db_own, feed_far = feed(
        h_two, gf, expand_far, expand_shift_far, shrink_all, expand_own, wide(expand_bias), shrink_own,
        span,
    )

    def bias_rows(grad):
        count = hidden // width
        return jnp.pad(grad.reshape(count, width), ((0, 8 - count), (0, 0)))

    result, feed_sum, more_sum, query_sum, last_sum, input_grad = back(
        lengths, sums, bias_rows(db_own), bias_rows(db_far), wide(shrink_bias), gain_two, out_mat,
        out_far, gain_one, shift_one, (cot, resid, f_sum, gh_sum), tokens, qkvs, hs,
        attended, gots, attend_own, grads_own.reshape(-1, width), feed_far.reshape(-1, width), span,
    )
    if dp > span:
        spans = [[base + index for base in range(0, dp, span)] for index in range(span)]
        feed_sum, more_sum, query_sum, last_sum = (
            lax.psum(part.astype(f32), "dp", axis_index_groups=spans)
            for part in (feed_sum, more_sum, query_sum, last_sum)
        )

    expand_grad, shrink_grad, out_grad, attend_grad, result, input_grad, *small = lay_out(
        feed_sum.reshape(grads_own.shape), more_sum, query_sum, last_sum, result,
        input_grad.reshape(-1, width), hidden, local,
    )
    squares = jnp.sum(small[9], axis=1)
    rms_values = jnp.sqrt(squares[:3] / (squares[3] * width))
    return (
        result.reshape(tokens.shape),
        input_grad.reshape(tokens.shape),
        small[4],
        small[5],
        attend_grad.transpose(1, 0, 2),
        small[6],
        small[7],
        out_grad,
        small[0],
        small[1],
        small[2],
        expand_grad,
        small[8],
        shrink_grad,
        small[3],
        rms_values,
    )


def solution(mesh):
    in_specs = (
        P("dp", "tensor", None),
        P("dp"),
        P(),
        P(),
        P(),
        P(None, None, None, "tensor"),
        P(None, "tensor"),
        P(None, "tensor"),
        P(None, "tensor", None),
        P(),
        P(),
        P(),
        P(None, None, "tensor"),
        P(None, "tensor"),
        P(None, "tensor", None),
        P(),
        P("dp", "tensor", None),
    )
    out_specs = (
        P("dp", "tensor", None),
        P("dp", "tensor", None),
        P(),
        P(),
        P(None, None, "tensor"),
        P("tensor"),
        P("tensor"),
        P("tensor", None),
        P(),
        P(),
        P(),
        P(None, "tensor"),
        P("tensor"),
        P("tensor", None),
        P(),
        P(),
    )
    return jax.shard_map(body, mesh=mesh, in_specs=in_specs, out_specs=out_specs, check_vma=False)
```

```python
import functools

import jax
import jax.numpy as jnp
from jax import lax
from jax.experimental import pallas as pl
from jax.experimental.pallas import tpu as pltpu
from jax.sharding import PartitionSpec as P

HD = 64
PAIR = 2 * HD
epsilon = 1e-05
masked_fill = -1e30
VMEM_LIMIT = 56 * 1024 * 1024
f32 = jnp.float32
bf16 = jnp.bfloat16


def dot_nn(left, right):
    return lax.dot_general(left, right, (((1,), (0,)), ((), ())), preferred_element_type=f32)


def dot_nt(left, right):
    return lax.dot_general(left, right, (((1,), (1,)), ((), ())), preferred_element_type=f32)


def dot_tn(left, right):
    return lax.dot_general(left, right, (((0,), (0,)), ((), ())), preferred_element_type=f32)


def select_layer(stack, layer_index):
    return lax.dynamic_index_in_dim(stack, layer_index[0], 0, keepdims=False)


def whole(shape):
    return pl.BlockSpec(shape, lambda *index: (0,) * len(shape))


def params():
    return pltpu.CompilerParams(dimension_semantics=("arbitrary",), vmem_limit_bytes=VMEM_LIMIT)


def remote_params(number):
    return pltpu.CompilerParams(
        collective_id=number, has_side_effects=True, vmem_limit_bytes=VMEM_LIMIT
    )


def cost(microseconds):
    return pl.CostEstimate(
        flops=int(microseconds * 1e9), bytes_accessed=int(microseconds * 3e6), transcendentals=0
    )


def normalized(x):
    center = jnp.mean(x, axis=-1, keepdims=True)
    x = x - center
    inverse = lax.rsqrt(jnp.mean(x * x, axis=-1, keepdims=True) + epsilon)
    return x * inverse, inverse


def norm_back(unit, inverse, gain, grad):
    scaled = grad * gain
    return inverse * (
        scaled
        - jnp.mean(scaled, axis=-1, keepdims=True)
        - unit * jnp.mean(scaled * unit, axis=-1, keepdims=True)
    )


class Halves:
    def __init__(self, half, block):
        self.count = half // block
        self.block = block

    def mine(self, i, at):
        return jnp.minimum(i, self.count - 1), 0

    def got(self, i, at):
        return jnp.maximum(i - self.count, 0), 0

    def whole(self, i, at):
        first = i < self.count
        side = jnp.where(first, at[0], 1 - at[0])
        return side * self.count + jnp.where(first, i, i - self.count), 0

    def position(self, at):
        i = pl.program_id(0)
        return self.whole(i, at)[0] * self.block + lax.broadcasted_iota(
            jnp.int32, (self.block, 1), 0
        )

    def pick(self, mine, got):
        return jnp.where(pl.program_id(0) < self.count, mine[...], got[...]).astype(f32)

    def specs(self, width, kind):
        return pl.BlockSpec((self.block, width), getattr(self, kind))


def fixed(shape):
    return pl.BlockSpec(shape, lambda i, at: (0,) * len(shape))


def project_kernel(at, mine, got, gain_ref, shift_ref, weight_ref, bias_ref, h_ref, qkv_ref, *, halves):
    unit, _ = normalized(halves.pick(mine, got))
    h = unit * gain_ref[...] + shift_ref[...]
    h = jnp.where(halves.position(at) < at[1], h, 0.0).astype(bf16)
    h_ref[...] = h
    local = weight_ref.shape[2]
    for part in range(3):
        columns = slice(part * local, (part + 1) * local)
        value = dot_nn(h, weight_ref[part]) + bias_ref[:, columns]
        qkv_ref[:, columns] = value.astype(bf16)


def project(at, mine, got, gain, shift, weight, bias):
    half, width = mine.shape
    columns = 3 * weight.shape[2]
    halves = Halves(half, min(512, half))
    return pl.pallas_call(
        functools.partial(project_kernel, halves=halves),
        grid_spec=pltpu.PrefetchScalarGridSpec(
            num_scalar_prefetch=1,
            grid=(2 * halves.count,),
            in_specs=[
                halves.specs(width, "mine"),
                halves.specs(width, "got"),
                fixed((1, width)),
                fixed((1, width)),
                fixed(weight.shape),
                fixed((1, columns)),
            ],
            out_specs=[halves.specs(width, "whole"), halves.specs(columns, "whole")],
        ),
        out_shape=[
            jax.ShapeDtypeStruct((2 * half, width), bf16),
            jax.ShapeDtypeStruct((2 * half, columns), bf16),
        ],
        compiler_params=params(),
        cost_estimate=cost(7),
        name="project",
    )(at, mine, got, gain, shift, weight, bias)


def lane_index(rows):
    return lax.broadcasted_iota(jnp.int32, (rows, PAIR), 1)


def causal_block(block):
    row = lax.broadcasted_iota(jnp.int32, (block, block), 0)
    column = lax.broadcasted_iota(jnp.int32, (block, block), 1)
    return row, column


def attend_kernel(at, q_ref, k_ref, v_ref, o_ref, lse_ref, *, block, half):
    seq_len = k_ref.shape[0]
    row, column = causal_block(block)
    keep = column <= row

    def query_half(side):
        end_all = (side + 1) * half
        lane = lane_index(end_all)
        lane_q = lane_index(half)
        position = lax.broadcasted_iota(jnp.int32, (end_all, PAIR), 0)
        key_bias = jnp.where(position < at[1], 0.0, masked_fill)
        q = q_ref[...].astype(f32) * (HD**-0.5)
        k = k_ref[:end_all, :].astype(f32)
        values = v_ref[:end_all, :]
        low = lane < HD
        low_q = lane_q < HD
        outs = []
        stats = []
        for head in range(2):
            mine = low if head == 0 else jnp.logical_not(low)
            mine_q = low_q if head == 0 else jnp.logical_not(low_q)
            spare = HD if head == 0 else 0
            q_aug = jnp.where(mine_q, q, jnp.where(lane_q == spare, 1.0, 0.0)).astype(bf16)
            k_aug = jnp.where(mine, k, jnp.where(lane == spare, key_bias, 0.0)).astype(bf16)
            v_own = jnp.where(mine, values, jnp.zeros_like(values))
            pieces = []
            notes = []
            for index in range(half // block):
                start = side * half + index * block
                end = start + block
                scores = dot_nt(q_aug[index * block : (index + 1) * block], k_aug[:end])
                last = jnp.where(keep, scores[:, start:end], masked_fill)
                scores = jnp.concatenate([scores[:, :start], last], axis=1) if start else last
                top = jnp.max(scores, axis=-1, keepdims=True)
                weights = jnp.exp(scores - top)
                total = jnp.sum(weights, axis=-1, keepdims=True)
                mixed = dot_nn(weights.astype(bf16), v_own[:end])
                pieces.append(mixed * (1.0 / total))
                notes.append(jnp.broadcast_to(top + jnp.log(total), (block, PAIR)))
            outs.append(jnp.concatenate(pieces, axis=0))
            stats.append(jnp.concatenate(notes, axis=0))
        o_ref[...] = (outs[0] + outs[1]).astype(bf16)
        lse_ref[...] = jnp.where(low_q, stats[1], stats[0])

    for side in range(seq_len // half):
        pl.when(at[0] == side)(functools.partial(query_half, side))


def attend(at, qkv, microseconds):
    seq_len = qkv.shape[0]
    half = seq_len // 2
    width = qkv.shape[1] // 3
    pairs = width // PAIR

    def columns(part):
        return pl.BlockSpec((seq_len, PAIR), lambda i, at: (0, part * pairs + i))

    out = pl.BlockSpec((half, PAIR), lambda i, at: (0, i))
    return pl.pallas_call(
        functools.partial(attend_kernel, block=min(256, half), half=half),
        grid_spec=pltpu.PrefetchScalarGridSpec(
            num_scalar_prefetch=1,
            grid=(pairs,),
            in_specs=[
                pl.BlockSpec((half, PAIR), lambda i, at: (at[0], i)),
                columns(1),
                columns(2),
            ],
            out_specs=[out, out],
        ),
        out_shape=[
            jax.ShapeDtypeStruct((half, width), bf16),
            jax.ShapeDtypeStruct((half, width), f32),
        ],
        compiler_params=params(),
        cost_estimate=cost(microseconds),
        name="attend",
    )(at, qkv, qkv, qkv)


class Pair:
    def __init__(self, half, block):
        self.count = half // block
        self.block = block

    def first(self, i, at):
        return jnp.minimum(i, self.count - 1), 0

    def second(self, i, at):
        return jnp.maximum(i - self.count, 0), 0

    def both(self, i, at):
        return i, 0

    def valid(self, at):
        i = pl.program_id(0)
        second = (i >= self.count).astype(jnp.int32)
        start = (at[0] * self.count + i - second * self.count) * self.block
        position = start + lax.broadcasted_iota(jnp.int32, (self.block, 1), 0)
        return (position < jnp.where(i < self.count, at[1], at[2])).astype(f32)

    def pick(self, first, second):
        return jnp.where(pl.program_id(0) < self.count, first[...], second[...])

    def specs(self, width, kind):
        return pl.BlockSpec((self.block, width), getattr(self, kind))


def resid_kernel(
    at, x_ref, cot_ref, o_first, o_second, got_first, got_second, w_ref, w_far, shift_out, gain,
    shift, h_ref, gf_ref, resid_ref, sums_ref, *, pair
):
    valid = pair.valid(at)
    attn = (
        dot_nn(pair.pick(o_first, o_second), w_ref[...])
        + dot_nn(pair.pick(got_first, got_second), w_far[...])
        + shift_out[...]
    )
    resid = x_ref[...].astype(f32) + valid * attn
    resid_ref[...] = resid
    unit, _ = normalized(resid)
    h_ref[...] = (valid * (unit * gain[...] + shift[...])).astype(bf16)
    gf = valid * cot_ref[...].astype(f32)
    gf_ref[...] = gf.astype(bf16)

    @pl.when(pl.program_id(0) == 0)
    def _():
        sums_ref[...] = jnp.zeros_like(sums_ref)

    sums_ref[0:1] += jnp.sum(valid * attn * attn, axis=0, keepdims=True)
    sums_ref[1:2] += jnp.sum(gf, axis=0, keepdims=True)


def resid_norm(at, x, cot, o_first, o_second, got_first, got_second, w, w_far, shift_out, gain, shift):
    rows, width = x.shape
    local = o_first.shape[1]
    pair = Pair(rows // 2, min(256, rows // 2))
    return pl.pallas_call(
        functools.partial(resid_kernel, pair=pair),
        grid_spec=pltpu.PrefetchScalarGridSpec(
            num_scalar_prefetch=1,
            grid=(2 * pair.count,),
            in_specs=[
                pair.specs(width, "both"),
                pair.specs(width, "both"),
                pair.specs(local, "first"),
                pair.specs(local, "second"),
                pair.specs(local, "first"),
                pair.specs(local, "second"),
                fixed((local, width)),
                fixed((local, width)),
                fixed((1, width)),
                fixed((1, width)),
                fixed((1, width)),
            ],
            out_specs=[pair.specs(width, "both")] * 3 + [fixed((8, width))],
        ),
        out_shape=[
            jax.ShapeDtypeStruct((rows, width), bf16),
            jax.ShapeDtypeStruct((rows, width), bf16),
            jax.ShapeDtypeStruct((rows, width), f32),
            jax.ShapeDtypeStruct((8, width), f32),
        ],
        compiler_params=params(),
        cost_estimate=cost(8),
        name="resid_norm",
    )(at, x, cot, o_first, o_second, got_first, got_second, w, w_far, shift_out, gain, shift)


class Ring:
    def __init__(self, dp):
        self.chips = dp // 2
        self.far_hops = self.chips // 2
        self.near_hops = self.chips - 1 - self.far_hops
        place = lax.axis_index("dp")
        self.tensor = lax.axis_index("tensor")
        self.base = place // dp * dp
        place = place % dp
        self.core = place % 2
        chip = place // 2
        depth = chip // 2
        self.spot = depth + (chip % 2) * (self.chips - 1 - 2 * depth)
        self.turn = 1 - 2 * self.core

    def device(self, spot, core):
        spot = (spot + self.chips) % self.chips
        side = spot // (self.chips // 2)
        chip = 2 * (spot + side * (self.chips - 1 - 2 * spot)) + side
        return (self.base + chip * 2 + core, self.tensor)

    def ahead(self):
        return self.device(self.spot + self.turn, self.core)

    def behind(self):
        return self.device(self.spot - self.turn, self.core)

    def sibling(self):
        return self.device(self.spot, 1 - self.core)

    def partner(self):
        return (lax.axis_index("dp"), 1 - self.tensor)

    def chunk(self, offset):
        return (self.spot + self.turn * offset + 2 * self.chips) % self.chips


def send(source, target, sems, index, device):
    copy = pltpu.make_async_remote_copy(
        src_ref=source,
        dst_ref=target,
        send_sem=sems.at[0, index],
        recv_sem=sems.at[1, index],
        device_id=device,
        device_id_type=pl.DeviceIdType.MESH,
    )
    return copy


def loop(start, stop, step):
    def run(index, carry):
        step(index)
        return carry

    lax.fori_loop(start, stop, run, 0)


class Group:
    def __init__(self, ring, source, acc, scratch):
        self.ring = ring
        self.source = source
        self.acc = acc
        self.pair, self.slots, self.pair_sems, self.ring_sems, self.load_sem = scratch
        self.rows = source.shape[0] // (2 * ring.chips)

    @staticmethod
    def scratch(rows, width, dp):
        chips = dp // 2
        size = rows // (2 * chips)
        return [
            pltpu.VMEM((chips, size, width), bf16),
            pltpu.VMEM((chips - 1, size, width), bf16),
            pltpu.SemaphoreType.DMA((2, chips)),
            pltpu.SemaphoreType.DMA((2, chips - 1)),
            pltpu.SemaphoreType.DMA((1,)),
        ]

    def place(self, core, chunk):
        start = (core * self.ring.chips + chunk) * self.rows
        return pl.ds(pl.multiple_of(start, 16), self.rows)

    def mine(self, chunk):
        if self.acc is None:
            return self.source.at[self.place(self.ring.core, chunk)]
        return self.acc.at[pl.ds(pl.multiple_of(chunk * self.rows, 16), self.rows)]

    def load(self):
        count = self.rows * self.ring.chips
        start = pl.multiple_of(self.ring.core * count, 16)
        return pltpu.make_async_copy(
            self.source.at[pl.ds(start, count)], self.acc, self.load_sem.at[0]
        )

    def to_sibling(self, chunk):
        source = self.source.at[self.place(1 - self.ring.core, chunk)]
        return send(source, self.pair.at[chunk], self.pair_sems, chunk, self.ring.sibling())

    def hand_over(self):
        ring = self.ring

        def both(step):
            self.to_sibling(ring.chunk(step - ring.far_hops)).start()
            self.to_sibling(ring.chunk(ring.near_hops - step)).start()

        loop(0, ring.near_hops, both)
        self.to_sibling(ring.chunk(-1)).start()
        self.to_sibling(ring.chunk(0)).start()

    def term(self, chunk):
        self.to_sibling(chunk).wait_recv()
        return self.mine(chunk)[...].astype(f32) + self.pair[chunk].astype(f32)

    def far_copy(self, step):
        chunk = self.ring.chunk(self.ring.far_hops - step)
        return send(
            self.mine(chunk), self.slots.at[step], self.ring_sems, step, self.ring.ahead()
        )

    def near_copy(self, step):
        slot = self.ring.far_hops + step
        chunk = self.ring.chunk(step - self.ring.near_hops)
        return send(
            self.mine(chunk), self.slots.at[slot], self.ring_sems, slot, self.ring.behind()
        )

    def far_step(self, step, first=False):
        chunk = self.ring.chunk(self.ring.far_hops - step)
        value = self.term(chunk)
        if not first:
            self.far_copy(step - 1).wait_recv()
            value += self.slots[step - 1].astype(f32)
        self.mine(chunk)[...] = value.astype(bf16)
        self.far_copy(step).start()

    def near_step(self, step, first=False):
        slot = self.ring.far_hops + step
        chunk = self.ring.chunk(step - self.ring.near_hops)
        value = self.term(chunk)
        if not first:
            self.near_copy(step - 1).wait_recv()
            value += self.slots[slot - 1].astype(f32)
        self.mine(chunk)[...] = value.astype(bf16)
        self.near_copy(step).start()

    def both_steps(self, step, first=False):
        self.far_step(step, first)
        self.near_step(step, first)

    def finish(self):
        ring = self.ring
        value = self.term(ring.chunk(0))
        self.far_copy(ring.far_hops - 1).wait_recv()
        self.near_copy(ring.near_hops - 1).wait_recv()
        value += self.slots[ring.far_hops - 1].astype(f32)
        return value + self.slots[ring.chips - 2].astype(f32)

    def sent(self):
        ring = self.ring
        loop(0, ring.chips, lambda chunk: self.to_sibling(chunk).wait_send())
        loop(0, ring.far_hops, lambda step: self.far_copy(step).wait_send())
        loop(0, ring.near_hops, lambda step: self.near_copy(step).wait_send())


class Spread:
    def __init__(self, ring, out, scratch):
        self.ring = ring
        self.out = out
        self.pair_sems, self.ring_sems = scratch
        self.rows = out.shape[0] // (2 * ring.chips)

    @staticmethod
    def scratch(dp):
        chips = dp // 2
        return [pltpu.SemaphoreType.DMA((2, chips)), pltpu.SemaphoreType.DMA((2, chips))]

    def place(self, core, chunk):
        start = (core * self.ring.chips + chunk) * self.rows
        return pl.ds(pl.multiple_of(start, 16), self.rows)

    def pass_on(self, chunk, slot, device):
        where = self.out.at[self.place(self.ring.core, chunk)]
        return send(where, where, self.ring_sems, slot, device)

    def to_sibling(self, chunk):
        where = self.out.at[self.place(self.ring.core, chunk)]
        return send(where, where, self.pair_sems, chunk, self.ring.sibling())

    def from_sibling(self, chunk):
        where = self.out.at[self.place(1 - self.ring.core, chunk)]
        return send(where, where, self.pair_sems, chunk, self.ring.sibling())

    def far_copy(self, step):
        return self.pass_on(self.ring.chunk(-step), step, self.ring.ahead())

    def near_copy(self, step):
        return self.pass_on(self.ring.chunk(step), self.ring.far_hops + step, self.ring.behind())

    def far_landed(self, step):
        return self.pass_on(self.ring.chunk(-step - 1), step, self.ring.ahead())

    def near_landed(self, step):
        return self.pass_on(
            self.ring.chunk(step + 1), self.ring.far_hops + step, self.ring.behind()
        )

    def begin(self):
        self.far_copy(0).start()
        self.near_copy(0).start()
        self.to_sibling(self.ring.chunk(0)).start()

    def far_step(self, step, last=False):
        self.far_landed(step - 1).wait_recv()
        if not last:
            self.far_copy(step).start()
        self.to_sibling(self.ring.chunk(-step)).start()

    def near_step(self, step, last=False):
        self.near_landed(step - 1).wait_recv()
        if not last:
            self.near_copy(step).start()
        self.to_sibling(self.ring.chunk(step)).start()

    def both_steps(self, step):
        self.far_step(step)
        self.near_step(step)

    def close(self):
        self.far_step(self.ring.near_hops)
        self.near_step(self.ring.near_hops, last=True)

    def sent(self):
        ring = self.ring
        loop(0, ring.chips, lambda chunk: self.from_sibling(chunk).wait_recv())
        loop(0, ring.chips, lambda chunk: self.to_sibling(chunk).wait_send())
        loop(0, ring.far_hops, lambda step: self.far_copy(step).wait_send())
        loop(0, ring.near_hops, lambda step: self.near_copy(step).wait_send())


def greet(*devices):
    barrier = pltpu.get_barrier_semaphore()
    for device in devices:
        pl.semaphore_signal(barrier, inc=1, device_id=device, device_id_type=pl.DeviceIdType.MESH)
    pl.semaphore_wait(barrier, len(devices))


def padded(rows, dp):
    unit = 16 * dp
    return -(-rows // unit) * unit


def feed_kernel(
    h_ref, gf_ref, e_far, b_far, s_far, e_own, b_own, s_own,
    f_ref, gh_ref, grad_ref, db_far, db_own, shard_ref,
    act_ref, gu_ref, tiles, crossing, got, y_sems, *rest, chunk, dp
):
    seq_len = h_ref.shape[0]
    tile = e_own.shape[1]
    root = 0.7978845608
    cube = 0.044715
    step = pl.program_id(0)
    far_steps = tiles.shape[0]
    is_far = step < far_steps
    parts = seq_len // chunk
    ring = Ring(dp)
    groups = [
        Group(ring, tiles.at[index], None, rest[5 * index : 5 * index + 5])
        for index in range(far_steps)
    ]

    def cross(index):
        return send(crossing.at[index], got.at[index], y_sems, index, ring.partner())

    def finish(index):
        crossing[index] = groups[index].finish().astype(bf16)
        cross(index).start()

    plan = {}

    def spacing(index):
        left = (parts + 1) * (2 * far_steps - 1 - index) - 2
        return min(parts, left // ring.far_hops)

    for index, group in enumerate(groups):
        slot = (parts + 1) * (index + 1) - 1
        plan.setdefault(slot, []).append(group.hand_over)
        for hop in range(ring.far_hops):
            slot_of_hop = slot + 2 + hop * spacing(index)
            action = functools.partial(group.far_step, hop)
            if hop < ring.near_hops:
                action = functools.partial(group.both_steps, hop, hop == 0)
            plan.setdefault(slot_of_hop, []).append(action)
        slot += 2 + ring.far_hops * spacing(index)
        plan.setdefault(slot, []).append(functools.partial(finish, index))

    def tick(part):
        for slot, actions in plan.items():
            if slot % (parts + 1) == part:

                @pl.when(step == slot // (parts + 1))
                def _():
                    for action in actions:
                        action()

    @pl.when(step == 0)
    def _():
        f_ref[...] = jnp.zeros_like(f_ref)
        gh_ref[...] = jnp.zeros_like(gh_ref)
        greet(ring.ahead(), ring.behind(), ring.sibling(), ring.partner())

    e = jnp.where(is_far, e_far[...], e_own[...])
    s = jnp.where(is_far, s_far[...].reshape(s_own.shape), s_own[...])
    bias = jnp.where(is_far, b_far[...], b_own[...])
    total = jnp.zeros((1, tile), f32)
    for index in range(parts):
        rows = pl.ds(index * chunk, chunk)
        u = dot_nn(h_ref[rows, :], e) + bias
        ga = dot_nt(gf_ref[rows, :], s)
        square = u * u
        bent = jnp.tanh(u * (root + (root * cube) * square))
        half = 0.5 + 0.5 * bent
        act = (u * half).astype(bf16)
        slope = half + (0.5 * u) * (1.0 - bent * bent) * (root + (3.0 * root * cube) * square)
        gu_wide = (slope * ga).astype(bf16)
        act_ref[rows, :] = act
        gu_ref[rows, :] = gu_wide
        total += jnp.sum(gu_wide.astype(f32), axis=0, keepdims=True)
        f_ref[rows, :] += dot_nn(act, s)
        gh_ref[rows, :] += dot_nt(gu_wide, e)
        tick(index)
    grad_e = dot_tn(gu_ref[...], h_ref[...]).astype(bf16)
    grad_s = dot_tn(act_ref[...], gf_ref[...]).astype(bf16)

    @pl.when(is_far)
    def _():
        db_far[...] = total
        tiles[jnp.minimum(step, far_steps - 1), :tile, :] = grad_e
        tiles[jnp.minimum(step, far_steps - 1), tile:, :] = grad_s

    @pl.when(jnp.logical_not(is_far))
    def _():
        db_own[...] = total
        half_chunks, _, rows, width = grad_ref.shape
        grad_ref[: half_chunks // 2, 0] = grad_e.reshape(half_chunks // 2, rows, width)
        grad_ref[half_chunks // 2 :, 0] = grad_s.reshape(half_chunks // 2, rows, width)

    tick(parts)

    @pl.when(step == pl.num_programs(0) - 1)
    def _():
        for index in range(far_steps):
            cross(index).wait_recv()
            shard_ref[index] = got[index]
        for index, group in enumerate(groups):
            cross(index).wait_send()
            group.sent()


def feed(h, gf, e_far, b_far, s_far, e_own, b_own, s_own, dp):
    seq_len, width = h.shape
    hidden = e_own.shape[1]
    tile = min(512, hidden)
    steps = hidden // tile
    size = 2 * tile // dp
    shares = s_far.shape[0]
    whole_rows = whole((seq_len, width))

    def far(i):
        return jnp.minimum(i, steps - 1)

    def own(i):
        return jnp.maximum(i - steps, 0)

    def weights(of):
        return [
            pl.BlockSpec((width, tile), lambda i: (0, of(i))),
            pl.BlockSpec((1, tile), lambda i: (0, of(i))),
            pl.BlockSpec((tile, width), lambda i: (of(i), 0)),
        ]

    scratch = []
    for _ in range(steps):
        scratch += Group.scratch(2 * tile, width, dp)
    return pl.pallas_call(
        functools.partial(feed_kernel, chunk=min(256, seq_len), dp=dp),
        grid=(2 * steps,),
        in_specs=[whole_rows, whole_rows]
        + weights(far)[:2]
        + [pl.BlockSpec((shares, tile // shares, width), lambda i: (0, far(i), 0))]
        + weights(own),
        out_specs=[
            whole_rows,
            whole_rows,
            pl.BlockSpec((dp, 1, size, width), lambda i: (0, own(i), 0, 0)),
            pl.BlockSpec((1, tile), lambda i: (0, far(i))),
            pl.BlockSpec((1, tile), lambda i: (0, own(i))),
            whole((steps, size, width)),
        ],
        out_shape=[
            jax.ShapeDtypeStruct((seq_len, width), f32),
            jax.ShapeDtypeStruct((seq_len, width), f32),
            jax.ShapeDtypeStruct((dp, steps, size, width), bf16),
            jax.ShapeDtypeStruct((1, hidden), f32),
            jax.ShapeDtypeStruct((1, hidden), f32),
            jax.ShapeDtypeStruct((steps, size, width), bf16),
        ],
        scratch_shapes=[
            pltpu.VMEM((seq_len, tile), bf16),
            pltpu.VMEM((seq_len, tile), bf16),
            pltpu.VMEM((steps, 2 * tile, width), bf16),
            pltpu.VMEM((steps, size, width), bf16),
            pltpu.VMEM((steps, size, width), bf16),
            pltpu.SemaphoreType.DMA((2, steps)),
        ]
        + scratch,
        compiler_params=remote_params(1),
        cost_estimate=cost(45),
        name="feed",
    )(h, gf, e_far, b_far, s_far, e_own, b_own, s_own)


def three_parts(values):
    first = values.astype(bf16).astype(f32)
    rest = values - first
    second = rest.astype(bf16).astype(f32)
    return first, second, rest - second


def attend_back(length, qkv, o, lse, go, acc_ref, seq, pair, local, block, between):
    seq_len = qkv.shape[1]
    scale = HD**-0.5

    def columns(part):
        return pl.ds(pl.multiple_of(part * local + pair * PAIR, PAIR), PAIR)

    lane = lane_index(seq_len)
    position = lax.broadcasted_iota(jnp.int32, (seq_len, PAIR), 0)
    inside = position < length
    key_bias = jnp.where(inside, 0.0, masked_fill)
    row, column = causal_block(block)
    keep = row <= column
    q = qkv[seq, :, columns(0)]
    k = qkv[seq, :, columns(1)]
    v = qkv[seq, :, columns(2)]
    grad_o = go[seq, :, columns(0)]
    q_wide = q.astype(f32) * scale
    k_wide = k.astype(f32)
    v_wide = v.astype(f32)
    go_wide = grad_o.astype(f32)
    both = go_wide * o[:, columns(0)].astype(f32)
    lse_parts = three_parts(-lse[:, columns(0)])
    low = lane < HD
    zero = jnp.zeros_like(q)
    acc_ref[...] = jnp.zeros_like(acc_ref)
    count = seq_len // block
    grads_k = [None] * count
    grads_v = [None] * count
    for head in range(2):
        mine = low if head == 0 else jnp.logical_not(low)
        spare = HD if head == 0 else 0
        delta = jnp.sum(jnp.where(mine, both, 0.0), axis=-1, keepdims=True)
        delta_parts = three_parts(-jnp.broadcast_to(delta, (seq_len, PAIR)))

        def extras(parts):
            return jnp.where(
                lane == spare + 1,
                parts[0],
                jnp.where(lane == spare + 2, parts[1], jnp.where(lane == spare + 3, parts[2], 0.0)),
            )

        ones = jnp.where((lane > spare) & (lane < spare + 4), 1.0, 0.0)
        q_aug = jnp.where(mine, q_wide, jnp.where(lane == spare, 1.0, extras(lse_parts))).astype(bf16)
        k_aug = jnp.where(mine, k_wide, jnp.where(lane == spare, key_bias, ones)).astype(bf16)
        v_aug = jnp.where(mine, v_wide, ones).astype(bf16)
        go_aug = jnp.where(mine, go_wide, extras(delta_parts)).astype(bf16)
        q_own = jnp.where(mine, q, zero)
        k_own = jnp.where(mine, k, zero)
        go_own = jnp.where(mine, grad_o, zero)
        for index in range(count):
            start, end = index * block, (index + 1) * block
            scores = dot_nt(k_aug[start:end], q_aug[start:])
            first = jnp.where(keep, scores[:, :block], masked_fill)
            if index + 1 < count:
                scores = jnp.concatenate([first, scores[:, block:]], axis=1)
            else:
                scores = first
            shares = jnp.exp(scores)
            moved = dot_nt(v_aug[start:end], go_aug[start:])
            grad_scores = (shares * moved).astype(bf16)
            grad_v = dot_nn(shares.astype(bf16), go_own[start:])
            grad_k = dot_nn(grad_scores, q_own[start:])
            grads_v[index] = grad_v if head == 0 else grads_v[index] + grad_v
            grads_k[index] = grad_k if head == 0 else grads_k[index] + grad_k
            acc_ref[start:, :] += dot_tn(grad_scores, k_own[start:end])
        between(head)
    qkv[seq, :, columns(0)] = (acc_ref[...] * scale).astype(bf16)
    qkv[seq, :, columns(1)] = (jnp.concatenate(grads_k, axis=0) * scale).astype(bf16)
    qkv[seq, :, columns(2)] = jnp.where(inside, jnp.concatenate(grads_v, axis=0), 0.0).astype(bf16)


def back_kernel(
    len_ref, sums_in, db_own, db_far, shift_mlp, gain_two, w_out, w_far, gain_ref, shift_ref,
    cot, resid, f_sum, gh_sum, tokens, qkv_first, qkv_second, h_first, h_second,
    o_keep, o_sent, lse_keep, lse_sent, o_keep_second, o_sent_second, lse_keep_second, lse_sent_second,
    got_first, got_second, weight, feed_own, feed_far,
    result_out, feed_out, more_out, query_out, last_out, input_out,
    load_sems, y_sems, block_sems, cot_buf, wide_bufs, result_buf, go_send, sums, gain_acc,
    qkv, o, lse, go, ga, mixed, h, w, acc_ref, row_send, row_got,
    feed_far_shard, feed_shard, more_shard, more_got, query_shard, last_shard, tile_send, tile_got,
    feed_acc, far_local, own_local, query_local, last_local, *rest, dp
):
    rest = list(rest)

    def take(count):
        taken = rest[:count]
        del rest[:count]
        return taken

    half, width = got_first.shape[0], tokens.shape[2]
    seq_len = 2 * half
    local = qkv.shape[2] // 3
    pairs = local // PAIR
    block = min(256, half)
    ring = Ring(dp)
    here = ring.tensor
    there = 1 - here
    feed_group = Group(ring, feed_own, feed_acc, take(5))
    far_group = Group(ring, far_local, None, take(5))
    own_group = Group(ring, own_local, None, take(5))
    query_group = Group(ring, query_local, None, take(5))
    last_group = Group(ring, last_local, None, take(5))
    feed_spread = Spread(ring, feed_out, take(2))
    more_spread = Spread(ring, more_out, take(2))
    query_spread = Spread(ring, query_out, take(2))
    last_spread = Spread(ring, last_out, take(2))

    def load(source, target, number):
        return pltpu.make_async_copy(source, target, load_sems.at[number])

    rows_here = pl.ds(pl.multiple_of(here * half, 16), half)
    rows_there = pl.ds(pl.multiple_of(there * half, 16), half)
    front, rear = pl.ds(0, half), pl.ds(half, half)
    mixed_loads = [
        load(o_keep, mixed.at[0, front], 1),
        load(o_keep_second, mixed.at[0, rear], 2),
        load(got_first, mixed.at[1, front], 3),
        load(got_second, mixed.at[1, rear], 4),
    ]
    first_loads = [
        load(qkv_first, qkv.at[0], 5),
        load(o_keep, o.at[rows_here], 6),
        load(o_sent, o.at[rows_there], 7),
        load(lse_keep, lse.at[rows_here], 8),
        load(lse_sent, lse.at[rows_there], 9),
    ]
    row_loads = [load(weight, w, 11)]
    second_loads = [load(qkv_second, qkv.at[1], 12)]
    late_loads = [load(h_first, h.at[0], 14), load(h_second, h.at[1], 15)]
    token_loads = [load(tokens.at[0], ga.at[front], 16), load(tokens.at[1], ga.at[rear], 17)]
    shard_load = load(feed_far, feed_far_shard, 18)
    reloads = [
        load(o_keep_second, o.at[rows_here], 19),
        load(o_sent_second, o.at[rows_there], 20),
        load(lse_keep_second, lse.at[rows_here], 21),
        load(lse_sent_second, lse.at[rows_there], 22),
    ]

    def cross(source, target, number):
        return send(source, target, y_sems, number, ring.partner())

    go_cross = [
        cross(go_send.at[front], go.at[0, rows_here], 0),
        cross(go_send.at[rear], go.at[1, rows_here], 1),
    ]
    go_landed = [
        cross(go_send.at[front], go.at[0, rows_there], 0),
        cross(go_send.at[rear], go.at[1, rows_there], 1),
    ]
    row_cross = [
        cross(row_send.at[0], row_got.at[0], 2),
        cross(row_send.at[1], row_got.at[1], 3),
    ]
    more_cross = cross(more_shard, more_got, 5)
    tile_cross = cross(tile_send, tile_got, 6)

    part = cot_buf.shape[1]
    parts = seq_len // part

    def fetch(index):
        slot = index % 2
        rows = pl.ds(pl.multiple_of(index * part, 16), part)
        copies = [pltpu.make_async_copy(cot.at[rows], cot_buf.at[slot], block_sems.at[slot, 0])]
        for number, source in enumerate((resid, f_sum, gh_sum)):
            copies.append(
                pltpu.make_async_copy(
                    source.at[rows], wide_bufs.at[slot, number], block_sems.at[slot, 1 + number]
                )
            )
        return copies

    def put(index):
        slot = index % 2
        rows = pl.ds(pl.multiple_of(index * part, 16), part)
        return pltpu.make_async_copy(result_buf.at[slot], result_out.at[rows], block_sems.at[slot, 6])

    def add(row, values):
        sums[row : row + 1] += jnp.sum(values, axis=0, keepdims=True)

    def turn(index):
        slot = index % 2
        for copy in fetch(index):
            copy.wait()

        @pl.when(index + 1 < parts)
        def _():
            for copy in fetch(index + 1):
                copy.start()

        @pl.when(index >= 2)
        def _():
            put(index - 2).wait()

        seq = index * part // half
        offset = index * part - seq * half
        rows = pl.ds(pl.multiple_of(offset, 16), part)
        flat = pl.ds(pl.multiple_of(index * part, 16), part)
        placed = pl.ds(pl.multiple_of(here * half + offset, 16), part)
        position = here * half + offset + lax.broadcasted_iota(jnp.int32, (part, 1), 0)
        valid = (position < len_ref[seq]).astype(f32)
        first = wide_bufs[slot, 0]
        mlp = wide_bufs[slot, 1] + shift_mlp[...]
        result = first + valid * mlp
        result_buf[slot] = result
        put(index).start()
        unit, inverse = normalized(first)
        grad_norm = valid * wide_bufs[slot, 2]
        grad = cot_buf[slot].astype(f32) + norm_back(unit, inverse, gain_two[...], grad_norm)
        input_out[seq, rows, :] = grad
        grad_attn = valid * grad
        low = grad_attn.astype(bf16)
        ga[flat, :] = low
        go_send[flat, :] = dot_nt(low, w_far[...]).astype(bf16)
        go[seq, placed, :] = dot_nt(low, w_out[...]).astype(bf16)
        add(0, grad_attn)
        add(1, grad_norm * unit)
        add(2, grad_norm)
        add(4, valid * result * result)
        add(6, valid * mlp * mlp)

        @pl.when(index == parts // 2 - 1)
        def _():
            go_cross[0].start()
            feed_group.load().wait()
            feed_group.both_steps(0, first=True)

    for copy in fetch(0):
        copy.start()
    feed_group.load().start()
    greet(ring.ahead(), ring.behind(), ring.sibling(), ring.partner())
    feed_group.hand_over()
    for copy in mixed_loads + first_loads + row_loads + second_loads + [shard_load] + late_loads:
        copy.start()
    sums[...] = jnp.zeros_like(sums)
    gain_acc[...] = jnp.zeros_like(gain_acc)
    loop(0, parts, turn)
    go_cross[1].start()
    feed_group.both_steps(1)
    put(parts - 2).wait()
    put(parts - 1).wait()

    lane = lax.broadcasted_iota(jnp.int32, (1, width), 1)
    count = jnp.zeros((1, width), f32)
    for start in range(0, half, width):
        position = here * half + lane + start
        for seq in range(2):
            count += ((lane + start < half) & (position < len_ref[seq])).astype(f32)
    sums[3:4] = sums_in[1:2]
    sums[5:6] = sums_in[0:1]
    sums[7:8] = count
    for copy in mixed_loads:
        copy.wait()
    tail = far_local.shape[0] - local - 16
    for target, index, small in ((far_local, 1, db_far), (own_local, 0, db_own)):
        target[pl.ds(0, local), :] = dot_tn(mixed[index], ga[...]).astype(bf16)
        pieces = [small[:, start : start + width] for start in range(0, small.shape[1], width)]
        pieces.append(jnp.zeros((8 - len(pieces), width), f32))
        target[pl.ds(local, 16), :] = jnp.concatenate([sums[0:8], *pieces], axis=0).astype(bf16)
        target[pl.ds(local + 16, tail), :] = jnp.zeros((tail, width), bf16)
    for copy in token_loads:
        copy.start()
    far_group.hand_over()
    own_group.hand_over()
    for copy in first_loads:
        copy.wait()
    go_landed[0].wait_recv()

    def store(spread, shard, number):
        copy = load(shard, spread.out.at[spread.place(ring.core, ring.spot)], number)
        copy.start()
        copy.wait()
        spread.begin()

    def feed_begin():
        shard_load.wait()
        value = feed_group.finish() + feed_far_shard[...].astype(f32)
        feed_shard[...] = value.astype(bf16)
        store(feed_spread, feed_shard, 0)

    def more_shard_cross():
        more_shard[...] = far_group.finish().astype(bf16)
        more_cross.start()

    def more_begin():
        value = own_group.finish()
        more_cross.wait_recv()
        more_cross.wait_send()
        more_shard[...] = (value + more_got[...].astype(f32)).astype(bf16)
        store(more_spread, more_shard, 10)

    def hop(group, step):
        if step == ring.far_hops - 1:
            group.far_step(step)
        else:
            group.both_steps(step, first=step == 0)

    def spread_step(spread, step):
        if step == ring.far_hops:
            spread.far_step(step, last=True)
        elif step == ring.near_hops:
            spread.close()
        else:
            spread.both_steps(step)

    def query_begin():
        query_shard[...] = query_group.finish().astype(bf16)
        store(query_spread, query_shard, 13)

    tile_row = lax.broadcasted_iota(jnp.int32, (16, width), 0)

    def last_hand_over():
        tile_cross.wait_recv()
        added = jnp.where(tile_row < 2, tile_got[...], 0.0)
        last_local[pl.ds(3 * PAIR, 16), :] = (tile_send[...] + added).astype(bf16)
        last_group.hand_over()

    def last_begin():
        last_shard[...] = last_group.finish().astype(bf16)
        store(last_spread, last_shard, 13)

    def through(rows):
        total = dot_nt(rows[:, :local], w[0])
        for index in range(1, 3):
            total += dot_nt(rows[:, index * local : (index + 1) * local], w[index])
        return total

    def send_rows(seq):
        def one(index):
            rows = pl.ds(pl.multiple_of(index * block, 16), block)
            from_rows = pl.ds(pl.multiple_of(there * half + index * block, 16), block)
            row_send[seq, rows, :] = through(qkv[seq, from_rows, :]).astype(bf16)

        loop(0, half // block, one)
        row_cross[seq].start()

    def keep_rows(seq):
        row_cross[seq].wait_recv()

        def one(index):
            rows = pl.ds(pl.multiple_of(index * block, 16), block)
            from_rows = pl.ds(pl.multiple_of(here * half + index * block, 16), block)
            position = here * half + index * block
            position += lax.broadcasted_iota(jnp.int32, (block, 1), 0)
            grad = through(qkv[seq, from_rows, :]) + row_got[seq, rows, :].astype(f32)
            grad = jnp.where(position < len_ref[seq], grad, 0.0)
            x_rows = pl.ds(pl.multiple_of(seq * half + index * block, 16), block)
            unit, inverse = normalized(ga[x_rows, :].astype(f32))
            input_out[seq, rows, :] += norm_back(unit, inverse, gain_ref[...], grad)

        loop(0, half // block, one)

    def query_rows(pair):
        if pair == 0:
            for copy in late_loads + token_loads:
                copy.wait()
        for index in range(3):
            columns = pl.ds(index * local + pair * PAIR, PAIR)
            value = dot_tn(qkv[0, :, columns], h[0]) + dot_tn(qkv[1, :, columns], h[1])
            target = last_local if pair == pairs - 1 else query_local
            start = 0 if pair == pairs - 1 else 3 * pair * PAIR
            target[pl.ds(start + index * PAIR, PAIR), :] = value.astype(bf16)
            weighted = value * w[index, :, pl.ds(pair * PAIR, PAIR)].astype(f32).T
            gain_acc[0:1] += jnp.sum(weighted, axis=0, keepdims=True)
        if pair == pairs - 2:
            used = 3 * (pairs - 1) * PAIR
            if query_local.shape[0] > used:
                rows = query_local.shape[0] - used
                query_local[pl.ds(used, rows), :] = jnp.zeros((rows, width), bf16)
            query_group.hand_over()
        if pair == pairs - 1:
            rows = last_local.shape[0] - 3 * PAIR
            last_local[pl.ds(3 * PAIR, rows), :] = jnp.zeros((rows, width), bf16)
            ones = jnp.ones((16, seq_len), bf16)
            totals = dot_nn(ones, qkv[0]) + dot_nn(ones, qkv[1])
            high = totals.astype(bf16)
            low = (totals - high.astype(f32)).astype(bf16)
            shift_grad = (through(high) + through(low))[0:1]
            gain_grad = (gain_acc[0:1] - shift_ref[...] * shift_grad) / gain_ref[...]
            biases = jnp.concatenate([totals[0:1, :local], totals[0:1, 2 * local :]], axis=1)
            last = jnp.where(tile_row == 2, biases, 0.0)
            last = jnp.where(tile_row == 1, shift_grad, last)
            last = jnp.where(tile_row == 0, gain_grad, last)
            tile_send[...] = last
            tile_cross.start()

    plan = {}

    def chain(tick, *actions):
        for number, action in enumerate(actions):
            if action is not None:
                plan.setdefault(tick + number, []).append(action)

    def hops(first, *groups):
        def one(step):
            for group in groups:
                hop(group, step)

        return [functools.partial(one, step) for step in range(first, ring.far_hops)]

    def spreads(spread):
        steps = range(1, ring.far_hops + 1)
        return [functools.partial(spread_step, spread, step) for step in steps]

    ticks = [1, 4, 7, 9, 11]
    free = len(ticks)
    chain(0, *hops(2, feed_group), feed_begin, *spreads(feed_spread))
    chain(0, *hops(0, far_group, own_group), more_shard_cross, more_begin, *spreads(more_spread))
    chain(free - 1, *hops(0, query_group), query_begin, *spreads(query_spread))
    chain(free, functools.partial(send_rows, 1))
    plan[free].insert(0, plan[free].pop())
    plan[free].insert(1, last_hand_over)
    chain(free, *hops(0, last_group), last_begin, *spreads(last_spread))
    chain(free + 1, functools.partial(keep_rows, 0))
    chain(free + ring.far_hops - 1, functools.partial(keep_rows, 1))

    def attention(index):
        seq = index // pairs
        pair = index % pairs

        @pl.when(index == pairs)
        def _():
            for copy in reloads:
                copy.start()
            for copy in row_loads:
                copy.wait()
            send_rows(0)
            for copy in second_loads + reloads:
                copy.wait()
            go_landed[1].wait_recv()

        def between(head):
            for tick, slot in enumerate(ticks):
                if slot % 2 == head:

                    @pl.when(index == slot // 2)
                    def _():
                        for action in plan[tick]:
                            action()

        attend_back(len_ref[seq], qkv, o, lse, go, acc_ref, seq, pair, local, block, between)
        for number in range(pairs):
            pl.when(index == pairs + number)(functools.partial(query_rows, number))

    loop(0, 2 * pairs, attention)
    for number in sorted(plan):
        if number >= free:
            for action in plan[number]:
                action()
    for group in (feed_group, far_group, own_group, query_group, last_group):
        group.sent()
    for copy in go_cross + row_cross + [tile_cross]:
        copy.wait_send()
    for spread in (feed_spread, more_spread, query_spread, last_spread):
        spread.sent()


def back(
    lens, sums, db_own, db_far, shift_mlp, gain_two, w_out, w_far, gain, shift, rows, tokens, qkvs, hs,
    attended, gots, weight, feed_own, feed_far, dp
):
    _, half, width = tokens.shape
    seq_len = 2 * half
    local = weight.shape[2]
    columns = 3 * local
    pairs = local // PAIR
    feed_rows = feed_own.shape[0]
    more_rows = padded(local + 32, dp)
    query_rows = padded(3 * (pairs - 1) * PAIR, dp)
    last_rows = padded(3 * PAIR + 32, dp)
    anywhere = pl.BlockSpec(memory_space=pl.ANY)
    inside = pl.BlockSpec(memory_space=pltpu.VMEM)
    feed_size, more_size, query_size = feed_rows // dp, more_rows // dp, query_rows // dp
    last_size = last_rows // dp
    both_rows = pltpu.VMEM((2, half, width), bf16)
    part = min(128, half)
    return pl.pallas_call(
        functools.partial(back_kernel, dp=dp),
        in_specs=[pl.BlockSpec(memory_space=pltpu.SMEM)] + [inside] * 9 + [anywhere] * 22,
        out_specs=[anywhere] * 5 + [inside],
        out_shape=[
            jax.ShapeDtypeStruct((seq_len, width), f32),
            jax.ShapeDtypeStruct((feed_rows, width), bf16),
            jax.ShapeDtypeStruct((more_rows, width), bf16),
            jax.ShapeDtypeStruct((query_rows, width), bf16),
            jax.ShapeDtypeStruct((last_rows, width), bf16),
            jax.ShapeDtypeStruct((2, half, width), f32),
        ],
        scratch_shapes=[
            pltpu.SemaphoreType.DMA((23,)),
            pltpu.SemaphoreType.DMA((2, 7)),
            pltpu.SemaphoreType.DMA((2, 7)),
            pltpu.VMEM((2, part, width), bf16),
            pltpu.VMEM((2, 3, part, width), f32),
            pltpu.VMEM((2, part, width), f32),
            pltpu.VMEM((seq_len, local), bf16),
            pltpu.VMEM((8, width), f32),
            pltpu.VMEM((8, width), f32),
            pltpu.VMEM((2, seq_len, columns), bf16),
            pltpu.VMEM((seq_len, local), bf16),
            pltpu.VMEM((seq_len, local), f32),
            pltpu.VMEM((2, seq_len, local), bf16),
            pltpu.VMEM((seq_len, width), bf16),
            pltpu.VMEM((2, seq_len, local), bf16),
            pltpu.VMEM((2, seq_len, width), bf16),
            pltpu.VMEM(weight.shape, bf16),
            pltpu.VMEM((seq_len, PAIR), f32),
            both_rows,
            both_rows,
            pltpu.VMEM((feed_size, width), bf16),
            pltpu.VMEM((feed_size, width), bf16),
            pltpu.VMEM((more_size, width), bf16),
            pltpu.VMEM((more_size, width), bf16),
            pltpu.VMEM((query_size, width), bf16),
            pltpu.VMEM((last_size, width), bf16),
            pltpu.VMEM((16, width), f32),
            pltpu.VMEM((16, width), f32),
            pltpu.VMEM((feed_rows // 2, width), bf16),
            pltpu.VMEM((more_rows, width), bf16),
            pltpu.VMEM((more_rows, width), bf16),
            pltpu.VMEM((query_rows, width), bf16),
            pltpu.VMEM((last_rows, width), bf16),
        ]
        + Group.scratch(feed_rows, width, dp)
        + Group.scratch(more_rows, width, dp)
        + Group.scratch(more_rows, width, dp)
        + Group.scratch(query_rows, width, dp)
        + Group.scratch(last_rows, width, dp)
        + Spread.scratch(dp) * 4,
        compiler_params=remote_params(2),
        cost_estimate=cost(90),
        name="back",
    )(
        lens, sums, db_own, db_far, shift_mlp, gain_two, w_out, w_far, gain, shift, *rows, tokens, *qkvs,
        *hs, *attended, *gots, weight, feed_own, feed_far,
    )


def lay_out_kernel(
    e_ref, s_ref, out_ref, q_ref, last_ref, result_ref, input_ref, small_ref, tail_ref,
    e_out, s_out, o_out, a_out, r_out, i_out, *vectors, local
):
    flat = s_out.shape
    e_out[...] = e_ref[...].reshape(flat).T.astype(f32)
    s_out[...] = s_ref[...].reshape(flat).astype(f32)
    o_out[...] = out_ref[...].astype(f32)
    r_out[...] = result_ref[...]
    i_out[...] = input_ref[...]
    step = pl.program_id(0)

    @pl.when(step == 0)
    def _():
        small = small_ref[...].astype(f32)
        tail = tail_ref[...].astype(f32)
        for index in range(4):
            vectors[index][...] = small[index]
        vectors[4][...] = tail[0]
        vectors[5][...] = tail[1]
        vectors[6][...] = tail[2, :local]
        vectors[7][...] = tail[2, local:]
        width = small.shape[1]
        for index in range(vectors[8].shape[0] // width):
            vectors[8][index * width : (index + 1) * width] = small[8 + index]
        vectors[9][...] = small[4:8]

    pairs = local // PAIR
    each = pl.num_programs(0) // 3
    for part in range(3):
        for pair in range(pairs):

            @pl.when(step == part * each + min(pair, each - 1))
            def _():
                source = last_ref if pair == pairs - 1 else q_ref
                start = (0 if pair == pairs - 1 else 3 * pair * PAIR) + part * PAIR
                value = source[start : start + PAIR, :].T
                a_out[0, :, pair * PAIR : (pair + 1) * PAIR] = value.astype(f32)


def lay_out(feed_sum, more_sum, query_sum, last_sum, result, grad, hidden, local):
    chunks, tiles, feed_size, width = feed_sum.shape
    unit = 2 * PAIR
    steps = hidden // unit
    turns = steps // tiles
    group = unit // feed_size
    rows = result.shape[0]
    size = rows * 3 // (2 * steps)
    blocks = rows // size
    proj = local // steps
    vectors = [(width,)] * 6 + [(local,)] * 2 + [(hidden,), (4, width)]

    def some(i):
        return jnp.minimum(i, blocks - 1), 0

    return pl.pallas_call(
        functools.partial(lay_out_kernel, local=local),
        grid=(steps,),
        in_specs=[
            pl.BlockSpec((group, 1, feed_size, width), lambda i: (i % turns, i // turns, 0, 0)),
            pl.BlockSpec(
                (group, 1, feed_size, width), lambda i: (i % turns + turns, i // turns, 0, 0)
            ),
            pl.BlockSpec((proj, width), lambda i: (i, 0)),
            whole(query_sum.shape),
            whole(last_sum.shape),
            pl.BlockSpec((size, width), some),
            pl.BlockSpec((size, width), some),
            pl.BlockSpec((16, width), lambda i: (local // 16, 0)),
            pl.BlockSpec((16, width), lambda i: (3 * PAIR // 16, 0)),
        ],
        out_specs=[
            pl.BlockSpec((width, unit), lambda i: (0, i)),
            pl.BlockSpec((unit, width), lambda i: (i, 0)),
            pl.BlockSpec((proj, width), lambda i: (i, 0)),
            pl.BlockSpec((1, width, local), lambda i: (i // (steps // 3), 0, 0)),
            pl.BlockSpec((size, width), some),
            pl.BlockSpec((size, width), some),
        ]
        + [whole(shape) for shape in vectors],
        out_shape=[
            jax.ShapeDtypeStruct((width, hidden), f32),
            jax.ShapeDtypeStruct((hidden, width), f32),
            jax.ShapeDtypeStruct((local, width), f32),
            jax.ShapeDtypeStruct((3, width, local), f32),
            jax.ShapeDtypeStruct((rows, width), f32),
            jax.ShapeDtypeStruct((rows, width), f32),
        ]
        + [jax.ShapeDtypeStruct(shape, f32) for shape in vectors],
        compiler_params=params(),
        cost_estimate=cost(10),
        name="lay_out",
    )(feed_sum, feed_sum, more_sum, query_sum, last_sum, result, grad, more_sum, last_sum)


def body(
    tokens,
    lengths,
    layer_index,
    norm_one_gain,
    norm_one_bias,
    attend_weight,
    query_bias,
    value_bias,
    output_weight,
    output_bias,
    norm_two_gain,
    norm_two_bias,
    expand_weight,
    expand_bias,
    shrink_weight,
    shrink_bias,
    cotangent,
):
    seq_dev, half, width = tokens.shape
    dp = lax.axis_size("dp")
    here = lax.axis_index("tensor")
    there = 1 - here
    place = lax.axis_index("dp")

    def exchange(values):
        return lax.ppermute(values, "tensor", [(0, 1), (1, 0)])

    def layer(stack):
        return select_layer(stack, layer_index)

    def wide(stack):
        return layer(stack).astype(f32)[None]

    def after(values, earlier):
        return lax.optimization_barrier((values, earlier))[0]

    def share(stack):
        rows = stack.shape[1] // dp
        piece = lax.dynamic_slice(
            stack, (layer_index[0], place * rows, 0), (1, rows, stack.shape[2])
        )
        return piece[0]

    def tiled_share(stack):
        tiles = max(1, stack.shape[1] // 512)
        each = stack.shape[1] // tiles // dp
        return jnp.concatenate(
            [
                lax.dynamic_slice(
                    stack,
                    (layer_index[0], index * each * dp + place * each, 0),
                    (1, each, stack.shape[2]),
                )[0]
                for index in range(tiles)
            ],
            axis=0,
        )

    def gather(piece):
        return lax.all_gather(piece, "dp", axis=0, tiled=False)

    hidden = expand_weight.shape[2]
    shrink_rows = hidden // dp
    pieces = [
        tokens[0],
        jnp.concatenate([tiled_share(shrink_weight), share(output_weight)], axis=0),
        share(expand_weight),
    ]
    pieces = lax.optimization_barrier(pieces)
    token_got = [exchange(pieces[0])]
    first_got = exchange(pieces[1])
    expand_got = exchange(pieces[2])
    token_got.append(exchange(after(tokens[1], token_got[0])))
    first_all = gather(first_got)
    out_far = first_all[:, shrink_rows:].reshape(output_weight.shape[1:])
    expand_far = gather(expand_got).reshape(width, hidden)
    expand_shift_far = exchange(after(layer(expand_bias), token_got[0]))[None].astype(f32)

    sides = jnp.stack([here, there]).astype(jnp.int32)

    def at(side, seq):
        return jnp.stack([sides[side], lengths[seq]])

    at_rows = jnp.concatenate([sides[:1], lengths])
    gain_one, shift_one = wide(norm_one_gain), wide(norm_one_bias)
    gain_two, shift_two = wide(norm_two_gain), wide(norm_two_bias)
    attend_own = layer(attend_weight.transpose(0, 2, 1, 3))
    out_mat, expand_own, shrink_own = layer(output_weight), layer(expand_weight), layer(shrink_weight)
    local = attend_own.shape[2]
    qkv_bias = jnp.concatenate(
        [wide(query_bias), jnp.zeros((1, local), f32), wide(value_bias)], axis=1
    )

    hs, qkvs, attended, kept, gots = [], [], [], [], []
    for seq in range(seq_dev):
        h, qkv = project(
            at(0, seq), tokens[seq], token_got[seq], gain_one, shift_one, attend_own, qkv_bias
        )
        o_sent, lse_sent = attend(at(1, seq), qkv, 7)
        gots.append(exchange(o_sent))
        o_keep, lse_keep = attend(at(0, seq), qkv, 7)
        hs.append(h)
        qkvs.append(qkv)
        kept.append(o_keep)
        attended += [o_keep, o_sent, lse_keep, lse_sent]

    x_rows = tokens.reshape(-1, width)
    cot = cotangent.reshape(-1, width)
    shrink_all = first_all
    if shrink_rows * dp // max(1, hidden // 512) // dp % 16:
        tiles = max(1, hidden // 512)
        shrink_all = first_all[:, :shrink_rows].reshape(dp, tiles, -1, width)
        shrink_all = shrink_all.transpose(1, 0, 2, 3).reshape(1, hidden, width)
    h_two, gf, resid, sums = resid_norm(
        at_rows, x_rows, cot, *kept, *gots, out_mat, out_far, wide(output_bias), gain_two, shift_two
    )
    span = min(dp, 16)
    f_sum, gh_sum, grads_own, db_far, db_own, feed_far = feed(
        h_two, gf, expand_far, expand_shift_far, shrink_all, expand_own, wide(expand_bias), shrink_own,
        span,
    )

    result, feed_sum, more_sum, query_sum, last_sum, input_grad = back(
        lengths, sums, db_own, db_far, wide(shrink_bias), gain_two, out_mat,
        out_far, gain_one, shift_one, (cot, resid, f_sum, gh_sum), tokens, qkvs, hs,
        attended, gots, attend_own, grads_own.reshape(-1, width), feed_far.reshape(-1, width), span,
    )
    if dp > span:
        spans = [[base + index for base in range(0, dp, span)] for index in range(span)]
        feed_sum, more_sum, query_sum, last_sum = (
            lax.psum(part.astype(f32), "dp", axis_index_groups=spans)
            for part in (feed_sum, more_sum, query_sum, last_sum)
        )

    expand_grad, shrink_grad, out_grad, attend_grad, result, input_grad, *small = lay_out(
        feed_sum.reshape(grads_own.shape), more_sum, query_sum, last_sum, result,
        input_grad.reshape(-1, width), hidden, local,
    )
    squares = jnp.sum(small[9], axis=1)
    rms_values = jnp.sqrt(squares[:3] / (squares[3] * width))
    return (
        result.reshape(tokens.shape),
        input_grad.reshape(tokens.shape),
        small[4],
        small[5],
        attend_grad.transpose(1, 0, 2),
        small[6],
        small[7],
        out_grad,
        small[0],
        small[1],
        small[2],
        expand_grad,
        small[8],
        shrink_grad,
        small[3],
        rms_values,
    )


def solution(mesh):
    in_specs = (
        P("dp", "tensor", None),
        P("dp"),
        P(),
        P(),
        P(),
        P(None, None, None, "tensor"),
        P(None, "tensor"),
        P(None, "tensor"),
        P(None, "tensor", None),
        P(),
        P(),
        P(),
        P(None, None, "tensor"),
        P(None, "tensor"),
        P(None, "tensor", None),
        P(),
        P("dp", "tensor", None),
    )
    out_specs = (
        P("dp", "tensor", None),
        P("dp", "tensor", None),
        P(),
        P(),
        P(None, None, "tensor"),
        P("tensor"),
        P("tensor"),
        P("tensor", None),
        P(),
        P(),
        P(),
        P(None, "tensor"),
        P("tensor"),
        P("tensor", None),
        P(),
        P(),
    )
    return jax.shard_map(body, mesh=mesh, in_specs=in_specs, out_specs=out_specs, check_vma=False)
```

```python
import functools

import jax
import jax.numpy as jnp
from jax import lax
from jax.experimental import pallas as pl
from jax.experimental.pallas import tpu as pltpu
from jax.sharding import PartitionSpec as P

HD = 64
PAIR = 2 * HD
epsilon = 1e-05
masked_fill = -1e30
VMEM_LIMIT = 56 * 1024 * 1024
f32 = jnp.float32
bf16 = jnp.bfloat16


def dot_nn(left, right):
    return lax.dot_general(left, right, (((1,), (0,)), ((), ())), preferred_element_type=f32)


def dot_nt(left, right):
    return lax.dot_general(left, right, (((1,), (1,)), ((), ())), preferred_element_type=f32)


def dot_tn(left, right):
    return lax.dot_general(left, right, (((0,), (0,)), ((), ())), preferred_element_type=f32)


def select_layer(stack, layer_index):
    return lax.dynamic_index_in_dim(stack, layer_index[0], 0, keepdims=False)


def whole(shape):
    return pl.BlockSpec(shape, lambda *index: (0,) * len(shape))


def params():
    return pltpu.CompilerParams(dimension_semantics=("arbitrary",), vmem_limit_bytes=VMEM_LIMIT)


def remote_params(number):
    return pltpu.CompilerParams(
        collective_id=number, has_side_effects=True, vmem_limit_bytes=VMEM_LIMIT
    )


def cost(microseconds):
    return pl.CostEstimate(
        flops=int(microseconds * 1e9), bytes_accessed=int(microseconds * 3e6), transcendentals=0
    )


def normalized(x):
    center = jnp.mean(x, axis=-1, keepdims=True)
    x = x - center
    inverse = lax.rsqrt(jnp.mean(x * x, axis=-1, keepdims=True) + epsilon)
    return x * inverse, inverse


def norm_back(unit, inverse, gain, grad):
    scaled = grad * gain
    return inverse * (
        scaled
        - jnp.mean(scaled, axis=-1, keepdims=True)
        - unit * jnp.mean(scaled * unit, axis=-1, keepdims=True)
    )


class Halves:
    def __init__(self, half, block):
        self.count = half // block
        self.block = block

    def mine(self, i, at):
        return jnp.minimum(i, self.count - 1), 0

    def got(self, i, at):
        return jnp.maximum(i - self.count, 0), 0

    def whole(self, i, at):
        first = i < self.count
        side = jnp.where(first, at[0], 1 - at[0])
        return side * self.count + jnp.where(first, i, i - self.count), 0

    def position(self, at):
        i = pl.program_id(0)
        return self.whole(i, at)[0] * self.block + lax.broadcasted_iota(
            jnp.int32, (self.block, 1), 0
        )

    def pick(self, mine, got):
        return jnp.where(pl.program_id(0) < self.count, mine[...], got[...]).astype(f32)

    def specs(self, width, kind):
        return pl.BlockSpec((self.block, width), getattr(self, kind))


def fixed(shape):
    return pl.BlockSpec(shape, lambda i, at: (0,) * len(shape))


def project_kernel(at, mine, got, gain_ref, shift_ref, weight_ref, bias_ref, h_ref, qkv_ref, *, halves):
    unit, _ = normalized(halves.pick(mine, got))
    h = unit * gain_ref[...] + shift_ref[...]
    h = jnp.where(halves.position(at) < at[1], h, 0.0).astype(bf16)
    h_ref[...] = h
    local = weight_ref.shape[2]
    for part in range(3):
        columns = slice(part * local, (part + 1) * local)
        value = dot_nn(h, weight_ref[part]) + bias_ref[:, columns]
        qkv_ref[:, columns] = value.astype(bf16)


def project(at, mine, got, gain, shift, weight, bias):
    half, width = mine.shape
    columns = 3 * weight.shape[2]
    halves = Halves(half, min(512, half))
    return pl.pallas_call(
        functools.partial(project_kernel, halves=halves),
        grid_spec=pltpu.PrefetchScalarGridSpec(
            num_scalar_prefetch=1,
            grid=(2 * halves.count,),
            in_specs=[
                halves.specs(width, "mine"),
                halves.specs(width, "got"),
                fixed((1, width)),
                fixed((1, width)),
                fixed(weight.shape),
                fixed((1, columns)),
            ],
            out_specs=[halves.specs(width, "whole"), halves.specs(columns, "whole")],
        ),
        out_shape=[
            jax.ShapeDtypeStruct((2 * half, width), bf16),
            jax.ShapeDtypeStruct((2 * half, columns), bf16),
        ],
        compiler_params=params(),
        cost_estimate=cost(7),
        name="project",
    )(at, mine, got, gain, shift, weight, bias)


def lane_index(rows):
    return lax.broadcasted_iota(jnp.int32, (rows, PAIR), 1)


def causal_block(block):
    row = lax.broadcasted_iota(jnp.int32, (block, block), 0)
    column = lax.broadcasted_iota(jnp.int32, (block, block), 1)
    return row, column


def attend_kernel(at, q_ref, k_ref, v_ref, o_ref, lse_ref, *, blocks, half):
    seq_len = k_ref.shape[0]
    def query_half(side):
        block = blocks[min(side, len(blocks) - 1)]
        row, column = causal_block(block)
        keep = column <= row
        end_all = (side + 1) * half
        lane = lane_index(end_all)
        lane_q = lane_index(half)
        position = lax.broadcasted_iota(jnp.int32, (end_all, PAIR), 0)
        key_bias = jnp.where(position < at[1], 0.0, masked_fill)
        q = q_ref[...].astype(f32) * (HD**-0.5)
        k = k_ref[:end_all, :].astype(f32)
        values = v_ref[:end_all, :]
        low = lane < HD
        low_q = lane_q < HD
        outs = []
        stats = []
        for head in range(2):
            mine = low if head == 0 else jnp.logical_not(low)
            mine_q = low_q if head == 0 else jnp.logical_not(low_q)
            spare = HD if head == 0 else 0
            q_aug = jnp.where(mine_q, q, jnp.where(lane_q == spare, 1.0, 0.0)).astype(bf16)
            k_aug = jnp.where(mine, k, jnp.where(lane == spare, key_bias, 0.0)).astype(bf16)
            v_own = jnp.where(mine, values, jnp.zeros_like(values))
            pieces = []
            notes = []
            for index in range(half // block):
                start = side * half + index * block
                end = start + block
                scores = dot_nt(q_aug[index * block : (index + 1) * block], k_aug[:end])
                last = jnp.where(keep, scores[:, start:end], masked_fill)
                scores = jnp.concatenate([scores[:, :start], last], axis=1) if start else last
                top = jnp.max(scores, axis=-1, keepdims=True)
                weights = jnp.exp(scores - top)
                total = jnp.sum(weights, axis=-1, keepdims=True)
                mixed = dot_nn(weights.astype(bf16), v_own[:end])
                pieces.append(mixed * (1.0 / total))
                notes.append(jnp.broadcast_to(top + jnp.log(total), (block, PAIR)))
            outs.append(jnp.concatenate(pieces, axis=0))
            stats.append(jnp.concatenate(notes, axis=0))
        o_ref[...] = (outs[0] + outs[1]).astype(bf16)
        lse_ref[...] = jnp.where(low_q, stats[1], stats[0])

    for side in range(seq_len // half):
        pl.when(at[0] == side)(functools.partial(query_half, side))


def attend(at, qkv, microseconds):
    seq_len = qkv.shape[0]
    half = seq_len // 2
    width = qkv.shape[1] // 3
    pairs = width // PAIR

    def columns(part):
        return pl.BlockSpec((seq_len, PAIR), lambda i, at: (0, part * pairs + i))

    out = pl.BlockSpec((half, PAIR), lambda i, at: (0, i))
    return pl.pallas_call(
        functools.partial(attend_kernel, blocks=(min(512, half), min(256, half)), half=half),
        grid_spec=pltpu.PrefetchScalarGridSpec(
            num_scalar_prefetch=1,
            grid=(pairs,),
            in_specs=[
                pl.BlockSpec((half, PAIR), lambda i, at: (at[0], i)),
                columns(1),
                columns(2),
            ],
            out_specs=[out, out],
        ),
        out_shape=[
            jax.ShapeDtypeStruct((half, width), bf16),
            jax.ShapeDtypeStruct((half, width), f32),
        ],
        compiler_params=params(),
        cost_estimate=cost(microseconds),
        name="attend",
    )(at, qkv, qkv, qkv)


class Pair:
    def __init__(self, half, block):
        self.count = half // block
        self.block = block

    def first(self, i, at):
        return jnp.minimum(i, self.count - 1), 0

    def second(self, i, at):
        return jnp.maximum(i - self.count, 0), 0

    def both(self, i, at):
        return i, 0

    def valid(self, at):
        i = pl.program_id(0)
        second = (i >= self.count).astype(jnp.int32)
        start = (at[0] * self.count + i - second * self.count) * self.block
        position = start + lax.broadcasted_iota(jnp.int32, (self.block, 1), 0)
        return (position < jnp.where(i < self.count, at[1], at[2])).astype(f32)

    def pick(self, first, second):
        return jnp.where(pl.program_id(0) < self.count, first[...], second[...])

    def specs(self, width, kind):
        return pl.BlockSpec((self.block, width), getattr(self, kind))


def resid_kernel(
    at, x_ref, cot_ref, o_first, o_second, got_first, got_second, w_ref, w_far, shift_out, gain,
    shift, h_ref, gf_ref, resid_ref, sums_ref, *, pair
):
    valid = pair.valid(at)
    attn = (
        dot_nn(pair.pick(o_first, o_second), w_ref[...])
        + dot_nn(pair.pick(got_first, got_second), w_far[...])
        + shift_out[...]
    )
    resid = x_ref[...].astype(f32) + valid * attn
    resid_ref[...] = resid
    unit, _ = normalized(resid)
    h_ref[...] = (valid * (unit * gain[...] + shift[...])).astype(bf16)
    gf = valid * cot_ref[...].astype(f32)
    gf_ref[...] = gf.astype(bf16)

    @pl.when(pl.program_id(0) == 0)
    def _():
        sums_ref[...] = jnp.zeros_like(sums_ref)

    sums_ref[0:1] += jnp.sum(valid * attn * attn, axis=0, keepdims=True)
    sums_ref[1:2] += jnp.sum(gf, axis=0, keepdims=True)


def resid_norm(at, x, cot, o_first, o_second, got_first, got_second, w, w_far, shift_out, gain, shift):
    rows, width = x.shape
    local = o_first.shape[1]
    pair = Pair(rows // 2, min(256, rows // 2))
    return pl.pallas_call(
        functools.partial(resid_kernel, pair=pair),
        grid_spec=pltpu.PrefetchScalarGridSpec(
            num_scalar_prefetch=1,
            grid=(2 * pair.count,),
            in_specs=[
                pair.specs(width, "both"),
                pair.specs(width, "both"),
                pair.specs(local, "first"),
                pair.specs(local, "second"),
                pair.specs(local, "first"),
                pair.specs(local, "second"),
                fixed((local, width)),
                fixed((local, width)),
                fixed((1, width)),
                fixed((1, width)),
                fixed((1, width)),
            ],
            out_specs=[pair.specs(width, "both")] * 3 + [fixed((8, width))],
        ),
        out_shape=[
            jax.ShapeDtypeStruct((rows, width), bf16),
            jax.ShapeDtypeStruct((rows, width), bf16),
            jax.ShapeDtypeStruct((rows, width), f32),
            jax.ShapeDtypeStruct((8, width), f32),
        ],
        compiler_params=params(),
        cost_estimate=cost(8),
        name="resid_norm",
    )(at, x, cot, o_first, o_second, got_first, got_second, w, w_far, shift_out, gain, shift)


class Ring:
    def __init__(self, dp):
        self.chips = dp // 2
        self.far_hops = self.chips // 2
        self.near_hops = self.chips - 1 - self.far_hops
        place = lax.axis_index("dp")
        self.tensor = lax.axis_index("tensor")
        self.base = place // dp * dp
        place = place % dp
        self.core = place % 2
        chip = place // 2
        depth = chip // 2
        self.spot = depth + (chip % 2) * (self.chips - 1 - 2 * depth)
        self.turn = 1 - 2 * self.core

    def device(self, spot, core):
        spot = (spot + self.chips) % self.chips
        side = spot // (self.chips // 2)
        chip = 2 * (spot + side * (self.chips - 1 - 2 * spot)) + side
        return (self.base + chip * 2 + core, self.tensor)

    def ahead(self):
        return self.device(self.spot + self.turn, self.core)

    def behind(self):
        return self.device(self.spot - self.turn, self.core)

    def sibling(self):
        return self.device(self.spot, 1 - self.core)

    def partner(self):
        return (lax.axis_index("dp"), 1 - self.tensor)

    def chunk(self, offset):
        return (self.spot + self.turn * offset + 2 * self.chips) % self.chips


def send(source, target, sems, index, device):
    copy = pltpu.make_async_remote_copy(
        src_ref=source,
        dst_ref=target,
        send_sem=sems.at[0, index],
        recv_sem=sems.at[1, index],
        device_id=device,
        device_id_type=pl.DeviceIdType.MESH,
    )
    return copy


def loop(start, stop, step):
    def run(index, carry):
        step(index)
        return carry

    lax.fori_loop(start, stop, run, 0)


class Group:
    def __init__(self, ring, source, acc, scratch):
        self.ring = ring
        self.source = source
        self.acc = acc
        self.pair, self.slots, self.pair_sems, self.ring_sems, self.load_sem = scratch
        self.rows = source.shape[0] // (2 * ring.chips)

    @staticmethod
    def scratch(rows, width, dp):
        chips = dp // 2
        size = rows // (2 * chips)
        return [
            pltpu.VMEM((chips, size, width), bf16),
            pltpu.VMEM((chips - 1, size, width), bf16),
            pltpu.SemaphoreType.DMA((2, chips)),
            pltpu.SemaphoreType.DMA((2, chips - 1)),
            pltpu.SemaphoreType.DMA((1,)),
        ]

    def place(self, core, chunk):
        start = (core * self.ring.chips + chunk) * self.rows
        return pl.ds(pl.multiple_of(start, 16), self.rows)

    def mine(self, chunk):
        if self.acc is None:
            return self.source.at[self.place(self.ring.core, chunk)]
        return self.acc.at[pl.ds(pl.multiple_of(chunk * self.rows, 16), self.rows)]

    def load(self):
        count = self.rows * self.ring.chips
        start = pl.multiple_of(self.ring.core * count, 16)
        return pltpu.make_async_copy(
            self.source.at[pl.ds(start, count)], self.acc, self.load_sem.at[0]
        )

    def to_sibling(self, chunk):
        source = self.source.at[self.place(1 - self.ring.core, chunk)]
        return send(source, self.pair.at[chunk], self.pair_sems, chunk, self.ring.sibling())

    def hand_over(self):
        ring = self.ring

        def both(step):
            self.to_sibling(ring.chunk(step - ring.far_hops)).start()
            self.to_sibling(ring.chunk(ring.near_hops - step)).start()

        loop(0, ring.near_hops, both)
        self.to_sibling(ring.chunk(-1)).start()
        self.to_sibling(ring.chunk(0)).start()

    def term(self, chunk):
        self.to_sibling(chunk).wait_recv()
        return self.mine(chunk)[...].astype(f32) + self.pair[chunk].astype(f32)

    def far_copy(self, step):
        chunk = self.ring.chunk(self.ring.far_hops - step)
        return send(
            self.mine(chunk), self.slots.at[step], self.ring_sems, step, self.ring.ahead()
        )

    def near_copy(self, step):
        slot = self.ring.far_hops + step
        chunk = self.ring.chunk(step - self.ring.near_hops)
        return send(
            self.mine(chunk), self.slots.at[slot], self.ring_sems, slot, self.ring.behind()
        )

    def far_step(self, step, first=False):
        chunk = self.ring.chunk(self.ring.far_hops - step)
        value = self.term(chunk)
        if not first:
            self.far_copy(step - 1).wait_recv()
            value += self.slots[step - 1].astype(f32)
        self.mine(chunk)[...] = value.astype(bf16)
        self.far_copy(step).start()

    def near_step(self, step, first=False):
        slot = self.ring.far_hops + step
        chunk = self.ring.chunk(step - self.ring.near_hops)
        value = self.term(chunk)
        if not first:
            self.near_copy(step - 1).wait_recv()
            value += self.slots[slot - 1].astype(f32)
        self.mine(chunk)[...] = value.astype(bf16)
        self.near_copy(step).start()

    def both_steps(self, step, first=False):
        self.far_step(step, first)
        self.near_step(step, first)

    def finish(self):
        ring = self.ring
        value = self.term(ring.chunk(0))
        self.far_copy(ring.far_hops - 1).wait_recv()
        self.near_copy(ring.near_hops - 1).wait_recv()
        value += self.slots[ring.far_hops - 1].astype(f32)
        return value + self.slots[ring.chips - 2].astype(f32)

    def sent(self):
        ring = self.ring
        loop(0, ring.chips, lambda chunk: self.to_sibling(chunk).wait_send())
        loop(0, ring.far_hops, lambda step: self.far_copy(step).wait_send())
        loop(0, ring.near_hops, lambda step: self.near_copy(step).wait_send())


class Spread:
    def __init__(self, ring, out, scratch):
        self.ring = ring
        self.out = out
        self.pair_sems, self.ring_sems = scratch
        self.rows = out.shape[0] // (2 * ring.chips)

    @staticmethod
    def scratch(dp):
        chips = dp // 2
        return [pltpu.SemaphoreType.DMA((2, chips)), pltpu.SemaphoreType.DMA((2, chips))]

    def place(self, core, chunk):
        start = (core * self.ring.chips + chunk) * self.rows
        return pl.ds(pl.multiple_of(start, 16), self.rows)

    def pass_on(self, chunk, slot, device):
        where = self.out.at[self.place(self.ring.core, chunk)]
        return send(where, where, self.ring_sems, slot, device)

    def to_sibling(self, chunk):
        where = self.out.at[self.place(self.ring.core, chunk)]
        return send(where, where, self.pair_sems, chunk, self.ring.sibling())

    def from_sibling(self, chunk):
        where = self.out.at[self.place(1 - self.ring.core, chunk)]
        return send(where, where, self.pair_sems, chunk, self.ring.sibling())

    def far_copy(self, step):
        return self.pass_on(self.ring.chunk(-step), step, self.ring.ahead())

    def near_copy(self, step):
        return self.pass_on(self.ring.chunk(step), self.ring.far_hops + step, self.ring.behind())

    def far_landed(self, step):
        return self.pass_on(self.ring.chunk(-step - 1), step, self.ring.ahead())

    def near_landed(self, step):
        return self.pass_on(
            self.ring.chunk(step + 1), self.ring.far_hops + step, self.ring.behind()
        )

    def begin(self):
        self.far_copy(0).start()
        self.near_copy(0).start()
        self.to_sibling(self.ring.chunk(0)).start()

    def far_step(self, step, last=False):
        self.far_landed(step - 1).wait_recv()
        if not last:
            self.far_copy(step).start()
        self.to_sibling(self.ring.chunk(-step)).start()

    def near_step(self, step, last=False):
        self.near_landed(step - 1).wait_recv()
        if not last:
            self.near_copy(step).start()
        self.to_sibling(self.ring.chunk(step)).start()

    def both_steps(self, step):
        self.far_step(step)
        self.near_step(step)

    def close(self):
        self.far_step(self.ring.near_hops)
        self.near_step(self.ring.near_hops, last=True)

    def sent(self):
        ring = self.ring
        loop(0, ring.chips, lambda chunk: self.from_sibling(chunk).wait_recv())
        loop(0, ring.chips, lambda chunk: self.to_sibling(chunk).wait_send())
        loop(0, ring.far_hops, lambda step: self.far_copy(step).wait_send())
        loop(0, ring.near_hops, lambda step: self.near_copy(step).wait_send())


def greet(*devices):
    barrier = pltpu.get_barrier_semaphore()
    for device in devices:
        pl.semaphore_signal(barrier, inc=1, device_id=device, device_id_type=pl.DeviceIdType.MESH)
    pl.semaphore_wait(barrier, len(devices))


def padded(rows, dp):
    unit = 16 * dp
    return -(-rows // unit) * unit


def feed_kernel(
    h_ref, gf_ref, e_far, b_far, s_far, e_own, b_own, s_own,
    f_ref, gh_ref, grad_ref, db_far, db_own, shard_ref,
    act_ref, gu_ref, tiles, crossing, got, y_sems, *rest, chunk, dp
):
    seq_len = h_ref.shape[0]
    tile = e_own.shape[1]
    root = 0.7978845608
    cube = 0.044715
    step = pl.program_id(0)
    far_steps = tiles.shape[0]
    is_far = step < far_steps
    parts = seq_len // chunk
    ring = Ring(dp)
    groups = [
        Group(ring, tiles.at[index], None, rest[5 * index : 5 * index + 5])
        for index in range(far_steps)
    ]

    def cross(index):
        return send(crossing.at[index], got.at[index], y_sems, index, ring.partner())

    def finish(index):
        crossing[index] = groups[index].finish().astype(bf16)
        cross(index).start()

    plan = {}

    def spacing(index):
        left = (parts + 1) * (2 * far_steps - 1 - index) - 2
        return min(parts, left // ring.far_hops)

    for index, group in enumerate(groups):
        slot = (parts + 1) * (index + 1) - 1
        plan.setdefault(slot, []).append(group.hand_over)
        for hop in range(ring.far_hops):
            slot_of_hop = slot + 2 + hop * spacing(index)
            action = functools.partial(group.far_step, hop)
            if hop < ring.near_hops:
                action = functools.partial(group.both_steps, hop, hop == 0)
            plan.setdefault(slot_of_hop, []).append(action)
        slot += 2 + ring.far_hops * spacing(index)
        plan.setdefault(slot, []).append(functools.partial(finish, index))

    def tick(part):
        for slot, actions in plan.items():
            if slot % (parts + 1) == part:

                @pl.when(step == slot // (parts + 1))
                def _():
                    for action in actions:
                        action()

    @pl.when(step == 0)
    def _():
        f_ref[...] = jnp.zeros_like(f_ref)
        gh_ref[...] = jnp.zeros_like(gh_ref)
        greet(ring.ahead(), ring.behind(), ring.sibling(), ring.partner())

    e = jnp.where(is_far, e_far[...], e_own[...])
    s = jnp.where(is_far, s_far[...].reshape(s_own.shape), s_own[...])
    bias = jnp.where(is_far, b_far[...], b_own[...])
    total = jnp.zeros((1, tile), f32)
    for index in range(parts):
        rows = pl.ds(index * chunk, chunk)
        u = dot_nn(h_ref[rows, :], e) + bias
        ga = dot_nt(gf_ref[rows, :], s)
        square = u * u
        bent = jnp.tanh(u * (root + (root * cube) * square))
        half = 0.5 + 0.5 * bent
        act = (u * half).astype(bf16)
        slope = half + (0.5 * u) * (1.0 - bent * bent) * (root + (3.0 * root * cube) * square)
        gu_wide = (slope * ga).astype(bf16)
        act_ref[rows, :] = act
        gu_ref[rows, :] = gu_wide
        total += jnp.sum(gu_wide.astype(f32), axis=0, keepdims=True)
        f_ref[rows, :] += dot_nn(act, s)
        gh_ref[rows, :] += dot_nt(gu_wide, e)
        tick(index)
    grad_e = dot_tn(gu_ref[...], h_ref[...]).astype(bf16)
    grad_s = dot_tn(act_ref[...], gf_ref[...]).astype(bf16)

    @pl.when(is_far)
    def _():
        db_far[...] = total
        tiles[jnp.minimum(step, far_steps - 1), :tile, :] = grad_e
        tiles[jnp.minimum(step, far_steps - 1), tile:, :] = grad_s

    @pl.when(jnp.logical_not(is_far))
    def _():
        db_own[...] = total
        half_chunks, _, rows, width = grad_ref.shape
        grad_ref[: half_chunks // 2, 0] = grad_e.reshape(half_chunks // 2, rows, width)
        grad_ref[half_chunks // 2 :, 0] = grad_s.reshape(half_chunks // 2, rows, width)

    tick(parts)

    @pl.when(step == pl.num_programs(0) - 1)
    def _():
        for index in range(far_steps):
            cross(index).wait_recv()
            shard_ref[index] = got[index]
        for index, group in enumerate(groups):
            cross(index).wait_send()
            group.sent()


def feed(h, gf, e_far, b_far, s_far, e_own, b_own, s_own, dp):
    seq_len, width = h.shape
    hidden = e_own.shape[1]
    tile = min(512, hidden)
    steps = hidden // tile
    size = 2 * tile // dp
    shares = s_far.shape[0]
    whole_rows = whole((seq_len, width))

    def far(i):
        return jnp.minimum(i, steps - 1)

    def own(i):
        return jnp.maximum(i - steps, 0)

    def weights(of):
        return [
            pl.BlockSpec((width, tile), lambda i: (0, of(i))),
            pl.BlockSpec((1, tile), lambda i: (0, of(i))),
            pl.BlockSpec((tile, width), lambda i: (of(i), 0)),
        ]

    scratch = []
    for _ in range(steps):
        scratch += Group.scratch(2 * tile, width, dp)
    return pl.pallas_call(
        functools.partial(feed_kernel, chunk=min(256, seq_len), dp=dp),
        grid=(2 * steps,),
        in_specs=[whole_rows, whole_rows]
        + weights(far)[:2]
        + [pl.BlockSpec((shares, tile // shares, width), lambda i: (0, far(i), 0))]
        + weights(own),
        out_specs=[
            whole_rows,
            whole_rows,
            pl.BlockSpec((dp, 1, size, width), lambda i: (0, own(i), 0, 0)),
            pl.BlockSpec((1, tile), lambda i: (0, far(i))),
            pl.BlockSpec((1, tile), lambda i: (0, own(i))),
            whole((steps, size, width)),
        ],
        out_shape=[
            jax.ShapeDtypeStruct((seq_len, width), f32),
            jax.ShapeDtypeStruct((seq_len, width), f32),
            jax.ShapeDtypeStruct((dp, steps, size, width), bf16),
            jax.ShapeDtypeStruct((1, hidden), f32),
            jax.ShapeDtypeStruct((1, hidden), f32),
            jax.ShapeDtypeStruct((steps, size, width), bf16),
        ],
        scratch_shapes=[
            pltpu.VMEM((seq_len, tile), bf16),
            pltpu.VMEM((seq_len, tile), bf16),
            pltpu.VMEM((steps, 2 * tile, width), bf16),
            pltpu.VMEM((steps, size, width), bf16),
            pltpu.VMEM((steps, size, width), bf16),
            pltpu.SemaphoreType.DMA((2, steps)),
        ]
        + scratch,
        compiler_params=remote_params(1),
        cost_estimate=cost(45),
        name="feed",
    )(h, gf, e_far, b_far, s_far, e_own, b_own, s_own)


def three_parts(values):
    first = values.astype(bf16).astype(f32)
    rest = values - first
    second = rest.astype(bf16).astype(f32)
    return first, second, rest - second


def attend_back(length, qkv, o, lse, go, acc_ref, seq, pair, local, block, between):
    seq_len = qkv.shape[1]
    scale = HD**-0.5

    def columns(part):
        return pl.ds(pl.multiple_of(part * local + pair * PAIR, PAIR), PAIR)

    lane = lane_index(seq_len)
    position = lax.broadcasted_iota(jnp.int32, (seq_len, PAIR), 0)
    inside = position < length
    key_bias = jnp.where(inside, 0.0, masked_fill)
    row, column = causal_block(block)
    keep = row <= column
    q = qkv[seq, :, columns(0)]
    k = qkv[seq, :, columns(1)]
    v = qkv[seq, :, columns(2)]
    grad_o = go[seq, :, columns(0)]
    q_wide = q.astype(f32) * scale
    k_wide = k.astype(f32)
    v_wide = v.astype(f32)
    go_wide = grad_o.astype(f32)
    both = go_wide * o[:, columns(0)].astype(f32)
    lse_parts = three_parts(-lse[:, columns(0)])
    low = lane < HD
    zero = jnp.zeros_like(q)
    acc_ref[...] = jnp.zeros_like(acc_ref)
    count = seq_len // block
    grads_k = [None] * count
    grads_v = [None] * count
    for head in range(2):
        mine = low if head == 0 else jnp.logical_not(low)
        spare = HD if head == 0 else 0
        delta = jnp.sum(jnp.where(mine, both, 0.0), axis=-1, keepdims=True)
        delta_parts = three_parts(-jnp.broadcast_to(delta, (seq_len, PAIR)))

        def extras(parts):
            return jnp.where(
                lane == spare + 1,
                parts[0],
                jnp.where(lane == spare + 2, parts[1], jnp.where(lane == spare + 3, parts[2], 0.0)),
            )

        ones = jnp.where((lane > spare) & (lane < spare + 4), 1.0, 0.0)
        q_aug = jnp.where(mine, q_wide, jnp.where(lane == spare, 1.0, extras(lse_parts))).astype(bf16)
        k_aug = jnp.where(mine, k_wide, jnp.where(lane == spare, key_bias, ones)).astype(bf16)
        v_aug = jnp.where(mine, v_wide, ones).astype(bf16)
        go_aug = jnp.where(mine, go_wide, extras(delta_parts)).astype(bf16)
        q_own = jnp.where(mine, q, zero)
        k_own = jnp.where(mine, k, zero)
        go_own = jnp.where(mine, grad_o, zero)
        for index in range(count):
            start, end = index * block, (index + 1) * block
            scores = dot_nt(k_aug[start:end], q_aug[start:])
            first = jnp.where(keep, scores[:, :block], masked_fill)
            if index + 1 < count:
                scores = jnp.concatenate([first, scores[:, block:]], axis=1)
            else:
                scores = first
            shares = jnp.exp(scores)
            moved = dot_nt(v_aug[start:end], go_aug[start:])
            grad_scores = (shares * moved).astype(bf16)
            grad_v = dot_nn(shares.astype(bf16), go_own[start:])
            grad_k = dot_nn(grad_scores, q_own[start:])
            grads_v[index] = grad_v if head == 0 else grads_v[index] + grad_v
            grads_k[index] = grad_k if head == 0 else grads_k[index] + grad_k
            acc_ref[start:, :] += dot_tn(grad_scores, k_own[start:end])
        between(head)
    qkv[seq, :, columns(0)] = (acc_ref[...] * scale).astype(bf16)
    qkv[seq, :, columns(1)] = (jnp.concatenate(grads_k, axis=0) * scale).astype(bf16)
    qkv[seq, :, columns(2)] = jnp.where(inside, jnp.concatenate(grads_v, axis=0), 0.0).astype(bf16)


def back_kernel(
    len_ref, sums_in, db_own, db_far, shift_mlp, gain_two, w_out, w_far, gain_ref, shift_ref,
    cot, resid, f_sum, gh_sum, tokens, qkv_first, qkv_second, h_first, h_second,
    o_keep, o_sent, lse_keep, lse_sent, o_keep_second, o_sent_second, lse_keep_second, lse_sent_second,
    got_first, got_second, weight, feed_own, feed_far,
    result_out, feed_out, more_out, query_out, last_out, input_out,
    load_sems, y_sems, block_sems, cot_buf, wide_bufs, result_buf, go_send, sums, gain_acc,
    qkv, o, lse, go, ga, mixed, h, w, acc_ref, row_send, row_got,
    feed_far_shard, feed_shard, more_shard, more_got, query_shard, last_shard, tile_send, tile_got,
    feed_acc, far_local, own_local, query_local, last_local, *rest, dp
):
    rest = list(rest)

    def take(count):
        taken = rest[:count]
        del rest[:count]
        return taken

    half, width = got_first.shape[0], tokens.shape[2]
    seq_len = 2 * half
    local = qkv.shape[2] // 3
    pairs = local // PAIR
    block = min(256, half)
    ring = Ring(dp)
    here = ring.tensor
    there = 1 - here
    feed_group = Group(ring, feed_own, feed_acc, take(5))
    far_group = Group(ring, far_local, None, take(5))
    own_group = Group(ring, own_local, None, take(5))
    query_group = Group(ring, query_local, None, take(5))
    last_group = Group(ring, last_local, None, take(5))
    feed_spread = Spread(ring, feed_out, take(2))
    more_spread = Spread(ring, more_out, take(2))
    query_spread = Spread(ring, query_out, take(2))
    last_spread = Spread(ring, last_out, take(2))

    def load(source, target, number):
        return pltpu.make_async_copy(source, target, load_sems.at[number])

    rows_here = pl.ds(pl.multiple_of(here * half, 16), half)
    rows_there = pl.ds(pl.multiple_of(there * half, 16), half)
    front, rear = pl.ds(0, half), pl.ds(half, half)
    mixed_loads = [
        load(o_keep, mixed.at[0, front], 1),
        load(o_keep_second, mixed.at[0, rear], 2),
        load(got_first, mixed.at[1, front], 3),
        load(got_second, mixed.at[1, rear], 4),
    ]
    first_loads = [
        load(qkv_first, qkv.at[0], 5),
        load(o_keep, o.at[rows_here], 6),
        load(o_sent, o.at[rows_there], 7),
        load(lse_keep, lse.at[rows_here], 8),
        load(lse_sent, lse.at[rows_there], 9),
    ]
    row_loads = [load(weight, w, 11)]
    second_loads = [load(qkv_second, qkv.at[1], 12)]
    late_loads = [load(h_first, h.at[0], 14), load(h_second, h.at[1], 15)]
    token_loads = [load(tokens.at[0], ga.at[front], 16), load(tokens.at[1], ga.at[rear], 17)]
    shard_load = load(feed_far, feed_far_shard, 18)
    reloads = [
        load(o_keep_second, o.at[rows_here], 19),
        load(o_sent_second, o.at[rows_there], 20),
        load(lse_keep_second, lse.at[rows_here], 21),
        load(lse_sent_second, lse.at[rows_there], 22),
    ]

    def cross(source, target, number):
        return send(source, target, y_sems, number, ring.partner())

    go_cross = [
        cross(go_send.at[front], go.at[0, rows_here], 0),
        cross(go_send.at[rear], go.at[1, rows_here], 1),
    ]
    go_landed = [
        cross(go_send.at[front], go.at[0, rows_there], 0),
        cross(go_send.at[rear], go.at[1, rows_there], 1),
    ]
    row_cross = [
        cross(row_send.at[0], row_got.at[0], 2),
        cross(row_send.at[1], row_got.at[1], 3),
    ]
    more_cross = cross(more_shard, more_got, 5)
    tile_cross = cross(tile_send, tile_got, 6)

    part = cot_buf.shape[1]
    parts = seq_len // part

    def fetch(index):
        slot = index % 2
        rows = pl.ds(pl.multiple_of(index * part, 16), part)
        copies = [pltpu.make_async_copy(cot.at[rows], cot_buf.at[slot], block_sems.at[slot, 0])]
        for number, source in enumerate((resid, f_sum, gh_sum)):
            copies.append(
                pltpu.make_async_copy(
                    source.at[rows], wide_bufs.at[slot, number], block_sems.at[slot, 1 + number]
                )
            )
        return copies

    def put(index):
        slot = index % 2
        rows = pl.ds(pl.multiple_of(index * part, 16), part)
        return pltpu.make_async_copy(result_buf.at[slot], result_out.at[rows], block_sems.at[slot, 6])

    def add(row, values):
        sums[row : row + 1] += jnp.sum(values, axis=0, keepdims=True)

    def turn(index):
        slot = index % 2
        for copy in fetch(index):
            copy.wait()

        @pl.when(index + 1 < parts)
        def _():
            for copy in fetch(index + 1):
                copy.start()

        @pl.when(index >= 2)
        def _():
            put(index - 2).wait()

        seq = index * part // half
        offset = index * part - seq * half
        rows = pl.ds(pl.multiple_of(offset, 16), part)
        flat = pl.ds(pl.multiple_of(index * part, 16), part)
        placed = pl.ds(pl.multiple_of(here * half + offset, 16), part)
        position = here * half + offset + lax.broadcasted_iota(jnp.int32, (part, 1), 0)
        valid = (position < len_ref[seq]).astype(f32)
        first = wide_bufs[slot, 0]
        mlp = wide_bufs[slot, 1] + shift_mlp[...]
        result = first + valid * mlp
        result_buf[slot] = result
        put(index).start()
        unit, inverse = normalized(first)
        grad_norm = valid * wide_bufs[slot, 2]
        grad = cot_buf[slot].astype(f32) + norm_back(unit, inverse, gain_two[...], grad_norm)
        input_out[seq, rows, :] = grad
        grad_attn = valid * grad
        low = grad_attn.astype(bf16)
        ga[flat, :] = low
        go_send[flat, :] = dot_nt(low, w_far[...]).astype(bf16)
        go[seq, placed, :] = dot_nt(low, w_out[...]).astype(bf16)
        add(0, grad_attn)
        add(1, grad_norm * unit)
        add(2, grad_norm)
        add(4, valid * result * result)
        add(6, valid * mlp * mlp)

        @pl.when(index == parts // 2 - 1)
        def _():
            go_cross[0].start()
            feed_group.load().wait()
            feed_group.both_steps(0, first=True)

    for copy in fetch(0):
        copy.start()
    feed_group.load().start()
    greet(ring.ahead(), ring.behind(), ring.sibling(), ring.partner())
    feed_group.hand_over()
    for copy in mixed_loads + first_loads + row_loads + second_loads + [shard_load] + late_loads:
        copy.start()
    sums[...] = jnp.zeros_like(sums)
    gain_acc[...] = jnp.zeros_like(gain_acc)
    loop(0, parts, turn)
    go_cross[1].start()
    feed_group.both_steps(1)
    put(parts - 2).wait()
    put(parts - 1).wait()

    lane = lax.broadcasted_iota(jnp.int32, (1, width), 1)
    count = jnp.zeros((1, width), f32)
    for start in range(0, half, width):
        position = here * half + lane + start
        for seq in range(2):
            count += ((lane + start < half) & (position < len_ref[seq])).astype(f32)
    sums[3:4] = sums_in[1:2]
    sums[5:6] = sums_in[0:1]
    sums[7:8] = count
    for copy in mixed_loads:
        copy.wait()
    tail = far_local.shape[0] - local - 16
    for target, index, small in ((far_local, 1, db_far), (own_local, 0, db_own)):
        target[pl.ds(0, local), :] = dot_tn(mixed[index], ga[...]).astype(bf16)
        pieces = [small[:, start : start + width] for start in range(0, small.shape[1], width)]
        pieces.append(jnp.zeros((8 - len(pieces), width), f32))
        target[pl.ds(local, 16), :] = jnp.concatenate([sums[0:8], *pieces], axis=0).astype(bf16)
        target[pl.ds(local + 16, tail), :] = jnp.zeros((tail, width), bf16)
    for copy in token_loads:
        copy.start()
    far_group.hand_over()
    own_group.hand_over()
    for copy in first_loads:
        copy.wait()
    go_landed[0].wait_recv()

    def store(spread, shard, number):
        copy = load(shard, spread.out.at[spread.place(ring.core, ring.spot)], number)
        copy.start()
        copy.wait()
        spread.begin()

    def feed_begin():
        shard_load.wait()
        value = feed_group.finish() + feed_far_shard[...].astype(f32)
        feed_shard[...] = value.astype(bf16)
        store(feed_spread, feed_shard, 0)

    def more_shard_cross():
        more_shard[...] = far_group.finish().astype(bf16)
        more_cross.start()

    def more_begin():
        value = own_group.finish()
        more_cross.wait_recv()
        more_cross.wait_send()
        more_shard[...] = (value + more_got[...].astype(f32)).astype(bf16)
        store(more_spread, more_shard, 10)

    def hop(group, step):
        if step == ring.far_hops - 1:
            group.far_step(step)
        else:
            group.both_steps(step, first=step == 0)

    def spread_step(spread, step):
        if step == ring.far_hops:
            spread.far_step(step, last=True)
        elif step == ring.near_hops:
            spread.close()
        else:
            spread.both_steps(step)

    def query_begin():
        query_shard[...] = query_group.finish().astype(bf16)
        store(query_spread, query_shard, 13)

    tile_row = lax.broadcasted_iota(jnp.int32, (16, width), 0)

    def last_hand_over():
        tile_cross.wait_recv()
        added = jnp.where(tile_row < 2, tile_got[...], 0.0)
        last_local[pl.ds(3 * PAIR, 16), :] = (tile_send[...] + added).astype(bf16)
        last_group.hand_over()

    def last_begin():
        last_shard[...] = last_group.finish().astype(bf16)
        store(last_spread, last_shard, 13)

    def through(rows):
        total = dot_nt(rows[:, :local], w[0])
        for index in range(1, 3):
            total += dot_nt(rows[:, index * local : (index + 1) * local], w[index])
        return total

    def send_rows(seq):
        def one(index):
            rows = pl.ds(pl.multiple_of(index * block, 16), block)
            from_rows = pl.ds(pl.multiple_of(there * half + index * block, 16), block)
            row_send[seq, rows, :] = through(qkv[seq, from_rows, :]).astype(bf16)

        loop(0, half // block, one)
        row_cross[seq].start()

    def keep_rows(seq):
        row_cross[seq].wait_recv()

        def one(index):
            rows = pl.ds(pl.multiple_of(index * block, 16), block)
            from_rows = pl.ds(pl.multiple_of(here * half + index * block, 16), block)
            position = here * half + index * block
            position += lax.broadcasted_iota(jnp.int32, (block, 1), 0)
            grad = through(qkv[seq, from_rows, :]) + row_got[seq, rows, :].astype(f32)
            grad = jnp.where(position < len_ref[seq], grad, 0.0)
            x_rows = pl.ds(pl.multiple_of(seq * half + index * block, 16), block)
            unit, inverse = normalized(ga[x_rows, :].astype(f32))
            input_out[seq, rows, :] += norm_back(unit, inverse, gain_ref[...], grad)

        loop(0, half // block, one)

    def query_rows(pair):
        if pair == 0:
            for copy in late_loads + token_loads:
                copy.wait()
        for index in range(3):
            columns = pl.ds(index * local + pair * PAIR, PAIR)
            value = dot_tn(qkv[0, :, columns], h[0]) + dot_tn(qkv[1, :, columns], h[1])
            target = last_local if pair == pairs - 1 else query_local
            start = 0 if pair == pairs - 1 else 3 * pair * PAIR
            target[pl.ds(start + index * PAIR, PAIR), :] = value.astype(bf16)
            weighted = value * w[index, :, pl.ds(pair * PAIR, PAIR)].astype(f32).T
            gain_acc[0:1] += jnp.sum(weighted, axis=0, keepdims=True)
        if pair == pairs - 2:
            used = 3 * (pairs - 1) * PAIR
            if query_local.shape[0] > used:
                rows = query_local.shape[0] - used
                query_local[pl.ds(used, rows), :] = jnp.zeros((rows, width), bf16)
            query_group.hand_over()
        if pair == pairs - 1:
            rows = last_local.shape[0] - 3 * PAIR
            last_local[pl.ds(3 * PAIR, rows), :] = jnp.zeros((rows, width), bf16)
            ones = jnp.ones((16, seq_len), bf16)
            totals = dot_nn(ones, qkv[0]) + dot_nn(ones, qkv[1])
            high = totals.astype(bf16)
            low = (totals - high.astype(f32)).astype(bf16)
            shift_grad = (through(high) + through(low))[0:1]
            gain_grad = (gain_acc[0:1] - shift_ref[...] * shift_grad) / gain_ref[...]
            biases = jnp.concatenate([totals[0:1, :local], totals[0:1, 2 * local :]], axis=1)
            last = jnp.where(tile_row == 2, biases, 0.0)
            last = jnp.where(tile_row == 1, shift_grad, last)
            last = jnp.where(tile_row == 0, gain_grad, last)
            tile_send[...] = last
            tile_cross.start()

    plan = {}

    def chain(tick, *actions):
        for number, action in enumerate(actions):
            if action is not None:
                plan.setdefault(tick + number, []).append(action)

    def hops(first, *groups):
        def one(step):
            for group in groups:
                hop(group, step)

        return [functools.partial(one, step) for step in range(first, ring.far_hops)]

    def spreads(spread):
        steps = range(1, ring.far_hops + 1)
        return [functools.partial(spread_step, spread, step) for step in steps]

    ticks = [1, 4, 7, 9, 11]
    free = len(ticks)
    chain(0, *hops(2, feed_group), feed_begin, *spreads(feed_spread))
    chain(0, *hops(0, far_group, own_group), more_shard_cross, more_begin, *spreads(more_spread))
    chain(free - 1, *hops(0, query_group), query_begin, *spreads(query_spread))
    chain(free, functools.partial(send_rows, 1))
    plan[free].insert(0, plan[free].pop())
    plan[free].insert(1, last_hand_over)
    chain(free, *hops(0, last_group), last_begin, *spreads(last_spread))
    chain(free + 1, functools.partial(keep_rows, 0))
    chain(free + ring.far_hops - 1, functools.partial(keep_rows, 1))

    def attention(index):
        seq = index // pairs
        pair = index % pairs

        @pl.when(index == pairs)
        def _():
            for copy in reloads:
                copy.start()
            for copy in row_loads:
                copy.wait()
            send_rows(0)
            for copy in second_loads + reloads:
                copy.wait()
            go_landed[1].wait_recv()

        def between(head):
            for tick, slot in enumerate(ticks):
                if slot % 2 == head:

                    @pl.when(index == slot // 2)
                    def _():
                        for action in plan[tick]:
                            action()

        attend_back(len_ref[seq], qkv, o, lse, go, acc_ref, seq, pair, local, block, between)
        for number in range(pairs):
            pl.when(index == pairs + number)(functools.partial(query_rows, number))

    loop(0, 2 * pairs, attention)
    for number in sorted(plan):
        if number >= free:
            for action in plan[number]:
                action()
    for group in (feed_group, far_group, own_group, query_group, last_group):
        group.sent()
    for copy in go_cross + row_cross + [tile_cross]:
        copy.wait_send()
    for spread in (feed_spread, more_spread, query_spread, last_spread):
        spread.sent()


def back(
    lens, sums, db_own, db_far, shift_mlp, gain_two, w_out, w_far, gain, shift, rows, tokens, qkvs, hs,
    attended, gots, weight, feed_own, feed_far, dp
):
    _, half, width = tokens.shape
    seq_len = 2 * half
    local = weight.shape[2]
    columns = 3 * local
    pairs = local // PAIR
    feed_rows = feed_own.shape[0]
    more_rows = padded(local + 32, dp)
    query_rows = padded(3 * (pairs - 1) * PAIR, dp)
    last_rows = padded(3 * PAIR + 32, dp)
    anywhere = pl.BlockSpec(memory_space=pl.ANY)
    inside = pl.BlockSpec(memory_space=pltpu.VMEM)
    feed_size, more_size, query_size = feed_rows // dp, more_rows // dp, query_rows // dp
    last_size = last_rows // dp
    both_rows = pltpu.VMEM((2, half, width), bf16)
    part = min(128, half)
    return pl.pallas_call(
        functools.partial(back_kernel, dp=dp),
        in_specs=[pl.BlockSpec(memory_space=pltpu.SMEM)] + [inside] * 9 + [anywhere] * 22,
        out_specs=[anywhere] * 5 + [inside],
        out_shape=[
            jax.ShapeDtypeStruct((seq_len, width), f32),
            jax.ShapeDtypeStruct((feed_rows, width), bf16),
            jax.ShapeDtypeStruct((more_rows, width), bf16),
            jax.ShapeDtypeStruct((query_rows, width), bf16),
            jax.ShapeDtypeStruct((last_rows, width), bf16),
            jax.ShapeDtypeStruct((2, half, width), f32),
        ],
        scratch_shapes=[
            pltpu.SemaphoreType.DMA((23,)),
            pltpu.SemaphoreType.DMA((2, 7)),
            pltpu.SemaphoreType.DMA((2, 7)),
            pltpu.VMEM((2, part, width), bf16),
            pltpu.VMEM((2, 3, part, width), f32),
            pltpu.VMEM((2, part, width), f32),
            pltpu.VMEM((seq_len, local), bf16),
            pltpu.VMEM((8, width), f32),
            pltpu.VMEM((8, width), f32),
            pltpu.VMEM((2, seq_len, columns), bf16),
            pltpu.VMEM((seq_len, local), bf16),
            pltpu.VMEM((seq_len, local), f32),
            pltpu.VMEM((2, seq_len, local), bf16),
            pltpu.VMEM((seq_len, width), bf16),
            pltpu.VMEM((2, seq_len, local), bf16),
            pltpu.VMEM((2, seq_len, width), bf16),
            pltpu.VMEM(weight.shape, bf16),
            pltpu.VMEM((seq_len, PAIR), f32),
            both_rows,
            both_rows,
            pltpu.VMEM((feed_size, width), bf16),
            pltpu.VMEM((feed_size, width), bf16),
            pltpu.VMEM((more_size, width), bf16),
            pltpu.VMEM((more_size, width), bf16),
            pltpu.VMEM((query_size, width), bf16),
            pltpu.VMEM((last_size, width), bf16),
            pltpu.VMEM((16, width), f32),
            pltpu.VMEM((16, width), f32),
            pltpu.VMEM((feed_rows // 2, width), bf16),
            pltpu.VMEM((more_rows, width), bf16),
            pltpu.VMEM((more_rows, width), bf16),
            pltpu.VMEM((query_rows, width), bf16),
            pltpu.VMEM((last_rows, width), bf16),
        ]
        + Group.scratch(feed_rows, width, dp)
        + Group.scratch(more_rows, width, dp)
        + Group.scratch(more_rows, width, dp)
        + Group.scratch(query_rows, width, dp)
        + Group.scratch(last_rows, width, dp)
        + Spread.scratch(dp) * 4,
        compiler_params=remote_params(2),
        cost_estimate=cost(90),
        name="back",
    )(
        lens, sums, db_own, db_far, shift_mlp, gain_two, w_out, w_far, gain, shift, *rows, tokens, *qkvs,
        *hs, *attended, *gots, weight, feed_own, feed_far,
    )


def lay_out_kernel(
    e_ref, s_ref, out_ref, q_ref, last_ref, result_ref, input_ref, small_ref, tail_ref,
    e_out, s_out, o_out, a_out, r_out, i_out, *vectors, local
):
    flat = s_out.shape
    e_out[...] = e_ref[...].reshape(flat).T.astype(f32)
    s_out[...] = s_ref[...].reshape(flat).astype(f32)
    o_out[...] = out_ref[...].astype(f32)
    r_out[...] = result_ref[...]
    i_out[...] = input_ref[...]
    step = pl.program_id(0)

    @pl.when(step == 0)
    def _():
        small = small_ref[...].astype(f32)
        tail = tail_ref[...].astype(f32)
        for index in range(4):
            vectors[index][...] = small[index]
        vectors[4][...] = tail[0]
        vectors[5][...] = tail[1]
        vectors[6][...] = tail[2, :local]
        vectors[7][...] = tail[2, local:]
        width = small.shape[1]
        for index in range(vectors[8].shape[0] // width):
            vectors[8][index * width : (index + 1) * width] = small[8 + index]
        vectors[9][...] = small[4:8]

    pairs = local // PAIR
    each = pl.num_programs(0) // 3
    for part in range(3):
        for pair in range(pairs):

            @pl.when(step == part * each + min(pair, each - 1))
            def _():
                source = last_ref if pair == pairs - 1 else q_ref
                start = (0 if pair == pairs - 1 else 3 * pair * PAIR) + part * PAIR
                value = source[start : start + PAIR, :].T
                a_out[0, :, pair * PAIR : (pair + 1) * PAIR] = value.astype(f32)


def lay_out(feed_sum, more_sum, query_sum, last_sum, result, grad, hidden, local):
    chunks, tiles, feed_size, width = feed_sum.shape
    unit = 2 * PAIR
    steps = hidden // unit
    turns = steps // tiles
    group = unit // feed_size
    rows = result.shape[0]
    size = rows * 3 // (2 * steps)
    blocks = rows // size
    proj = local // steps
    vectors = [(width,)] * 6 + [(local,)] * 2 + [(hidden,), (4, width)]

    def some(i):
        return jnp.minimum(i, blocks - 1), 0

    return pl.pallas_call(
        functools.partial(lay_out_kernel, local=local),
        grid=(steps,),
        in_specs=[
            pl.BlockSpec((group, 1, feed_size, width), lambda i: (i % turns, i // turns, 0, 0)),
            pl.BlockSpec(
                (group, 1, feed_size, width), lambda i: (i % turns + turns, i // turns, 0, 0)
            ),
            pl.BlockSpec((proj, width), lambda i: (i, 0)),
            whole(query_sum.shape),
            whole(last_sum.shape),
            pl.BlockSpec((size, width), some),
            pl.BlockSpec((size, width), some),
            pl.BlockSpec((16, width), lambda i: (local // 16, 0)),
            pl.BlockSpec((16, width), lambda i: (3 * PAIR // 16, 0)),
        ],
        out_specs=[
            pl.BlockSpec((width, unit), lambda i: (0, i)),
            pl.BlockSpec((unit, width), lambda i: (i, 0)),
            pl.BlockSpec((proj, width), lambda i: (i, 0)),
            pl.BlockSpec((1, width, local), lambda i: (i // (steps // 3), 0, 0)),
            pl.BlockSpec((size, width), some),
            pl.BlockSpec((size, width), some),
        ]
        + [whole(shape) for shape in vectors],
        out_shape=[
            jax.ShapeDtypeStruct((width, hidden), f32),
            jax.ShapeDtypeStruct((hidden, width), f32),
            jax.ShapeDtypeStruct((local, width), f32),
            jax.ShapeDtypeStruct((3, width, local), f32),
            jax.ShapeDtypeStruct((rows, width), f32),
            jax.ShapeDtypeStruct((rows, width), f32),
        ]
        + [jax.ShapeDtypeStruct(shape, f32) for shape in vectors],
        compiler_params=params(),
        cost_estimate=cost(10),
        name="lay_out",
    )(feed_sum, feed_sum, more_sum, query_sum, last_sum, result, grad, more_sum, last_sum)


def body(
    tokens,
    lengths,
    layer_index,
    norm_one_gain,
    norm_one_bias,
    attend_weight,
    query_bias,
    value_bias,
    output_weight,
    output_bias,
    norm_two_gain,
    norm_two_bias,
    expand_weight,
    expand_bias,
    shrink_weight,
    shrink_bias,
    cotangent,
):
    seq_dev, half, width = tokens.shape
    dp = lax.axis_size("dp")
    here = lax.axis_index("tensor")
    there = 1 - here
    place = lax.axis_index("dp")

    def exchange(values):
        return lax.ppermute(values, "tensor", [(0, 1), (1, 0)])

    def layer(stack):
        return select_layer(stack, layer_index)

    def wide(stack):
        return layer(stack).astype(f32)[None]

    def after(values, earlier):
        return lax.optimization_barrier((values, earlier))[0]

    def share(stack):
        rows = stack.shape[1] // dp
        piece = lax.dynamic_slice(
            stack, (layer_index[0], place * rows, 0), (1, rows, stack.shape[2])
        )
        return piece[0]

    def tiled_share(stack):
        tiles = max(1, stack.shape[1] // 512)
        each = stack.shape[1] // tiles // dp
        return jnp.concatenate(
            [
                lax.dynamic_slice(
                    stack,
                    (layer_index[0], index * each * dp + place * each, 0),
                    (1, each, stack.shape[2]),
                )[0]
                for index in range(tiles)
            ],
            axis=0,
        )

    def gather(piece):
        return lax.all_gather(piece, "dp", axis=0, tiled=False)

    hidden = expand_weight.shape[2]
    shrink_rows = hidden // dp
    pieces = [
        tokens[0],
        jnp.concatenate([tiled_share(shrink_weight), share(output_weight)], axis=0),
        share(expand_weight),
    ]
    pieces[1:] = lax.optimization_barrier(pieces[1:])
    token_got = [exchange(pieces[0])]
    first_got = exchange(pieces[1])
    expand_got = exchange(pieces[2])
    token_got.append(exchange(after(tokens[1], token_got[0])))
    first_all = gather(first_got)
    out_far = first_all[:, shrink_rows:].reshape(output_weight.shape[1:])
    expand_far = gather(expand_got).reshape(width, hidden)
    expand_shift_far = exchange(after(layer(expand_bias), token_got[0]))[None].astype(f32)

    sides = jnp.stack([here, there]).astype(jnp.int32)

    def at(side, seq):
        return jnp.stack([sides[side], lengths[seq]])

    at_rows = jnp.concatenate([sides[:1], lengths])
    gain_one, shift_one = wide(norm_one_gain), wide(norm_one_bias)
    gain_two, shift_two = wide(norm_two_gain), wide(norm_two_bias)
    attend_own = layer(attend_weight.transpose(0, 2, 1, 3))
    out_mat, expand_own, shrink_own = layer(output_weight), layer(expand_weight), layer(shrink_weight)
    local = attend_own.shape[2]
    qkv_bias = jnp.concatenate(
        [wide(query_bias), jnp.zeros((1, local), f32), wide(value_bias)], axis=1
    )

    hs, qkvs, attended, kept, gots = [], [], [], [], []
    for seq in range(seq_dev):
        h, qkv = project(
            at(0, seq), tokens[seq], token_got[seq], gain_one, shift_one, attend_own, qkv_bias
        )
        o_sent, lse_sent = attend(at(1, seq), qkv, 7)
        gots.append(exchange(o_sent))
        o_keep, lse_keep = attend(at(0, seq), qkv, 7)
        hs.append(h)
        qkvs.append(qkv)
        kept.append(o_keep)
        attended += [o_keep, o_sent, lse_keep, lse_sent]

    x_rows = tokens.reshape(-1, width)
    cot = cotangent.reshape(-1, width)
    shrink_all = first_all
    if shrink_rows * dp // max(1, hidden // 512) // dp % 16:
        tiles = max(1, hidden // 512)
        shrink_all = first_all[:, :shrink_rows].reshape(dp, tiles, -1, width)
        shrink_all = shrink_all.transpose(1, 0, 2, 3).reshape(1, hidden, width)
    h_two, gf, resid, sums = resid_norm(
        at_rows, x_rows, cot, *kept, *gots, out_mat, out_far, wide(output_bias), gain_two, shift_two
    )
    span = min(dp, 16)
    f_sum, gh_sum, grads_own, db_far, db_own, feed_far = feed(
        h_two, gf, expand_far, expand_shift_far, shrink_all, expand_own, wide(expand_bias), shrink_own,
        span,
    )

    result, feed_sum, more_sum, query_sum, last_sum, input_grad = back(
        lengths, sums, db_own, db_far, wide(shrink_bias), gain_two, out_mat,
        out_far, gain_one, shift_one, (cot, resid, f_sum, gh_sum), tokens, qkvs, hs,
        attended, gots, attend_own, grads_own.reshape(-1, width), feed_far.reshape(-1, width), span,
    )
    if dp > span:
        spans = [[base + index for base in range(0, dp, span)] for index in range(span)]
        feed_sum, more_sum, query_sum, last_sum = (
            lax.psum(part.astype(f32), "dp", axis_index_groups=spans)
            for part in (feed_sum, more_sum, query_sum, last_sum)
        )

    expand_grad, shrink_grad, out_grad, attend_grad, result, input_grad, *small = lay_out(
        feed_sum.reshape(grads_own.shape), more_sum, query_sum, last_sum, result,
        input_grad.reshape(-1, width), hidden, local,
    )
    squares = jnp.sum(small[9], axis=1)
    rms_values = jnp.sqrt(squares[:3] / (squares[3] * width))
    return (
        result.reshape(tokens.shape),
        input_grad.reshape(tokens.shape),
        small[4],
        small[5],
        attend_grad.transpose(1, 0, 2),
        small[6],
        small[7],
        out_grad,
        small[0],
        small[1],
        small[2],
        expand_grad,
        small[8],
        shrink_grad,
        small[3],
        rms_values,
    )


def solution(mesh):
    in_specs = (
        P("dp", "tensor", None),
        P("dp"),
        P(),
        P(),
        P(),
        P(None, None, None, "tensor"),
        P(None, "tensor"),
        P(None, "tensor"),
        P(None, "tensor", None),
        P(),
        P(),
        P(),
        P(None, None, "tensor"),
        P(None, "tensor"),
        P(None, "tensor", None),
        P(),
        P("dp", "tensor", None),
    )
    out_specs = (
        P("dp", "tensor", None),
        P("dp", "tensor", None),
        P(),
        P(),
        P(None, None, "tensor"),
        P("tensor"),
        P("tensor"),
        P("tensor", None),
        P(),
        P(),
        P(),
        P(None, "tensor"),
        P("tensor"),
        P("tensor", None),
        P(),
        P(),
    )
    return jax.shard_map(body, mesh=mesh, in_specs=in_specs, out_specs=out_specs, check_vma=False)
```
